32 devices in a mesh: section: 2 (over x), mp: 16 (over z, y, core).
Axes of the slice: x: 2, y: 2, z: 4, core: 2. Of those that a mesh axis runs over, the one named last changes fastest.
Arguments:
- hidden: bfloat16 [2, 32, 8192], P('section', 'mp'), may hold values from -6 to 6
- attn_gain: float32 [2, 8192], P('section'), may hold values from 0.1 to 1.9
- w_query: bfloat16 [2, 8192, 8192], P('section', None, 'mp'), may hold values from -0.0625 to 0.0625
- w_key: bfloat16 [2, 8192, 1024], P('section', None, 'mp'), may hold values from -0.0625 to 0.0625
- w_value: bfloat16 [2, 8192, 1024], P('section', None, 'mp'), may hold values from -0.0625 to 0.0625
- w_out: bfloat16 [2, 8192, 8192], P('section', 'mp'), may hold values from -0.0625 to 0.0625
- mlp_gain: float32 [2, 8192], P('section'), may hold values from 0.1 to 1.9
- w_gate_up: bfloat16 [2, 8192, 2, 16384], P('section', None, None, 'mp'), may hold values from -0.0625 to 0.0625
- w_down: bfloat16 [2, 16384, 8192], P('section', 'mp'), may hold values from -0.046875 to 0.046875
- key_cache: bfloat16 [2, 2, 32, 512, 1024], P('section', None, 'mp'), may hold values from -620 to 620
- value_cache: bfloat16 [2, 2, 32, 512, 1024], P('section', None, 'mp'), may hold values from -6 to 6
- lengths: int32 [2, 32], P(None, 'mp'), may hold values from 1 to 512, 8192 in all within a row
Outputs:
- out: bfloat16 [2, 32, 8192], P('section', 'mp')
The draws below stay inside these ranges and needn't reach their ends.
Inputs may be any that keep to these rules, and one draw needn't show every extreme that they name: In each micro-batch the lengths of the 32 batch rows sum to 8192, and one batch row has exactly 512.
All inputs are finite; a program needn't handle non-finite values. No bound on the sum of `lengths` on one device may be relied on, other than what follows from the above.
Results may differ from the reference program's by a relative error of at most 0.039.
Values may be sent and summed in bfloat16 or wider, within the bound.
No kernel may reach another device: no remote copies, remote signals or barrier semaphores. Data moves between devices by JAX's collectives and lax.ppermute only.
A program may use at most 192 MiB of HBM per device.

```python
import math
import jax
import jax.numpy as jnp
import numpy as np
from jax import lax

D = 8192
QUERY_HEADS = 64
KEY_VALUE_HEADS = 8
HEAD_SIZE = 128
FF = 16384
L = 512
QW = 8192
KW = 1024
R_MB = 32


def draw_key_cache(key, part):
    key = jax.random.fold_in(key, 11)
    base_key = jax.random.fold_in(key, 0)
    values = jnp.clip(jax.random.normal(base_key, (2, 2, R_MB, L, KW), jnp.float32), -6.0, 6.0)
    return values.astype(jnp.bfloat16)


def level_of(rng, extent, cuts, least, largest):
    def one(dim, shards_of):
        heights = jax.random.uniform(jax.random.fold_in(jax.random.fold_in(rng, 6), dim), (shards_of,), jnp.float32, least / len(cuts), largest / len(cuts))
        return jnp.repeat(jnp.exp(heights), extent[dim] // shards_of).reshape((-1,) + (1,) * (len(extent) - dim - 1))

    gain = one(*cuts[0])
    for cut in cuts[1:]:
        gain = gain * one(*cut)
    return gain


def split_up(amount, total, limit, lean):
    weights = [(1 << 20) // math.isqrt(rank ** lean) + 1 for rank in range(2, amount + 1)]
    surplus, counts = total - limit - (amount - 1), [1] * (amount - 1)
    while surplus > 0:
        movable = [i for i in range(amount - 1) if counts[i] < limit]
        pool, budget = sum([weights[i] for i in movable]), surplus
        for i in movable:
            extra = min(limit - counts[i], max(1, budget * weights[i] // pool), surplus)
            counts[i] = counts[i] + extra
            surplus = surplus - extra
    return np.array([limit] + counts)


def uneven(rng, amount, total, reach, slope):
    if amount == 2:
        one = jax.random.randint(rng, (), max(1, total - reach), min(reach, total - 1) + 1)
        return jnp.stack([one, total - one])
    sizes = jnp.asarray(split_up(amount, total, reach, slope), jnp.int32)
    twos = (amount - 1) // 2
    source_of, taker = sizes[1:1 + 2 * twos:2], sizes[2:2 + 2 * twos:2]
    margin = jnp.minimum(source_of - 1, reach - taker)
    shifted = jax.random.randint(jax.random.fold_in(rng, 1), (twos,), 0, 1 << 20) % (margin + 1)
    sizes = sizes.at[1:1 + 2 * twos:2].set(source_of - shifted).at[2:2 + 2 * twos:2].set(taker + shifted)
    return sizes[jax.random.permutation(jax.random.fold_in(rng, 2), amount)]


def noise(own_key, shape, spread, most, pieces=(), kind=jnp.bfloat16):
    drawn = jax.random.normal(own_key, shape, jnp.float32) * spread
    if len(pieces) > 0:
        drawn = level_of(own_key, shape, pieces, -0.22, 0.18) * drawn
    return jnp.clip(drawn, min=-most, max=most).astype(kind)


def setup_inputs(seed: int = 0) -> dict:
    key_list = jax.random.split(jax.random.key(seed), 13)
    return {
        "hidden": noise(key_list[0], (2, R_MB, D), 1.0, 6.0, ((0, 2), (1, 16))),
        "attn_gain": jnp.clip(1.0 + 0.18 * jax.random.normal(key_list[1], (2, D), jnp.float32), 0.1, 1.9),
        "w_query": noise(key_list[2], (2, D, QW), D ** -0.5, 0.0625, ((0, 2), (2, 16))),
        "w_key": noise(key_list[3], (2, D, KW), D ** -0.5, 0.0625, ((0, 2), (2, 16))),
        "w_value": noise(key_list[4], (2, D, KW), D ** -0.5, 0.0625, ((0, 2), (2, 16))),
        "w_out": noise(key_list[5], (2, QW, D), QW ** -0.5, 0.0625, ((0, 2), (1, 16))),
        "mlp_gain": jnp.clip(1.0 + 0.18 * jax.random.normal(key_list[6], (2, D), jnp.float32), 0.1, 1.9),
        "w_gate_up": noise(key_list[7], (2, D, 2, FF), D ** -0.5, 0.0625, ((0, 2), (3, 16))),
        "w_down": noise(key_list[8], (2, FF, D), FF ** -0.5, 0.046875, ((0, 2), (1, 16))),
        "key_cache": draw_key_cache(jax.random.fold_in(key_list[12], 71), 0),
        "value_cache": noise(key_list[10], (2, 2, R_MB, L, KW), 1.0, 6.0, ((0, 2), (2, 16))),
        "lengths": jax.vmap(lambda own: uneven(own, R_MB, R_MB * L // 2, L, 1))(jax.random.split(key_list[11], 2)).reshape((2, R_MB)).astype(jnp.int32),
    }


epsilon = 1e-05

def norm_rows(values, norm_gain):
    wide = values.astype(jnp.float32)
    square_mean = lax.optimization_barrier(jnp.mean(wide * wide, axis=-1, keepdims=True))
    return (wide * lax.rsqrt(square_mean + epsilon) * norm_gain).astype(jnp.bfloat16)

def rotate(features, positions):
    half_dim = HEAD_SIZE // 2
    frequency = 500000.0 ** (-2.0 * jnp.arange(half_dim, dtype=jnp.float32) / HEAD_SIZE)
    angles = positions.astype(jnp.float32)[:, None] * frequency[None, :]
    cosine = jnp.cos(angles)[:, None, :]
    sine_part = jnp.sin(angles)[:, None, :]
    wide = features.astype(jnp.float32).reshape(features.shape[0], -1, HEAD_SIZE)
    first_half = wide[..., :half_dim]
    second_half = wide[..., half_dim:]
    turned = jnp.concatenate([first_half * cosine - second_half * sine_part, second_half * cosine + first_half * sine_part], axis=-1)
    return turned.reshape(features.shape).astype(jnp.bfloat16)

def attend(query_rows, fresh_key, fresh_value, cached_key_rows, cached_value_rows, current):
    cached_row_count = query_rows.shape[0]
    heads_per_group = QUERY_HEADS // KEY_VALUE_HEADS
    score_scale = HEAD_SIZE ** (-0.5)
    query_head_rows = query_rows.astype(jnp.float32).reshape(cached_row_count, KEY_VALUE_HEADS, heads_per_group, HEAD_SIZE)
    key_head_rows = cached_key_rows.astype(jnp.float32).reshape(cached_row_count, -1, KEY_VALUE_HEADS, HEAD_SIZE)
    value_head_rows = cached_value_rows.astype(jnp.float32).reshape(cached_row_count, -1, KEY_VALUE_HEADS, HEAD_SIZE)
    scores = jnp.einsum('rgjd,rlgd->rgjl', query_head_rows, key_head_rows) * score_scale
    self_score = jnp.einsum('zneh,znh->zne', query_head_rows, fresh_key.astype(jnp.float32).reshape(cached_row_count, KEY_VALUE_HEADS, HEAD_SIZE)) * score_scale
    places = jnp.arange(key_head_rows.shape[1], dtype=jnp.int32)
    live = (places[None, :] < current[:, None])[:, None, None, :]
    scores = jnp.where(live, scores, -1e+30)
    highest = jnp.maximum(lax.optimization_barrier(jnp.max(scores, axis=-1)), self_score)
    raised = jnp.exp(scores - highest[..., None])
    own_raised = jnp.exp(self_score - highest)
    denominator = lax.optimization_barrier(jnp.sum(raised, axis=-1)) + own_raised
    weights = (raised / denominator[..., None]).astype(jnp.bfloat16)
    self_weight = (own_raised / denominator).astype(jnp.bfloat16)
    mixed_output = jnp.einsum('rgjl,rlgd->rgjd', weights.astype(jnp.float32), value_head_rows)
    mixed_output = mixed_output + self_weight.astype(jnp.float32)[..., None] * fresh_value.astype(jnp.float32).reshape(cached_row_count, KEY_VALUE_HEADS, 1, HEAD_SIZE)
    return mixed_output.reshape(cached_row_count, QUERY_HEADS * HEAD_SIZE).astype(jnp.bfloat16)

def reference(hidden, attn_gain, w_query, w_key, w_value, w_out, mlp_gain, w_gate_up, w_down, key_cache, value_cache, lengths):

    def layer(stream, layer_index, micro_batch):
        normed = norm_rows(stream, attn_gain[layer_index])
        query_rows = jnp.dot(normed, w_query[layer_index], preferred_element_type=jnp.float32).astype(jnp.bfloat16)
        fresh_key = jnp.dot(normed, w_key[layer_index], preferred_element_type=jnp.float32).astype(jnp.bfloat16)
        fresh_value = jnp.dot(normed, w_value[layer_index], preferred_element_type=jnp.float32).astype(jnp.bfloat16)
        current = lengths[micro_batch]
        heads_out = attend(rotate(query_rows, current), rotate(fresh_key, current), fresh_value, key_cache[layer_index, micro_batch], value_cache[layer_index, micro_batch], current)
        attn_part = jnp.dot(heads_out, w_out[layer_index], preferred_element_type=jnp.float32)
        middle = (stream.astype(jnp.float32) + attn_part).astype(jnp.bfloat16)
        normed_mlp = norm_rows(middle, mlp_gain[layer_index])
        gate_part = jnp.dot(normed_mlp, w_gate_up[layer_index, :, 0, :], preferred_element_type=jnp.float32)
        up_part = jnp.dot(normed_mlp, w_gate_up[layer_index, :, 1, :], preferred_element_type=jnp.float32)
        acts = (jax.nn.silu(gate_part) * up_part).astype(jnp.bfloat16)
        mlp_part = jnp.dot(acts, w_down[layer_index], preferred_element_type=jnp.float32)
        return (middle.astype(jnp.float32) + mlp_part).astype(jnp.bfloat16)
    first_batch = layer(layer(hidden[0], 0, 0), 1, 0)
    second_batch = layer(layer(hidden[1], 1, 1), 0, 1)
    return jnp.stack([second_batch, first_batch])
```

```python
import jax
import jax.numpy as jnp
import numpy as np
from jax import lax
from jax.sharding import PartitionSpec as P

QUERY_HEADS = 64
KEY_VALUE_HEADS = 8
HEAD_SIZE = 128


epsilon = 1e-05


def swap(value, mask, axis="mp"):
    count = lax.axis_size(axis)
    return lax.ppermute(value, axis, [(source, source ^ mask) for source in range(count)])


def bit_count():
    return (lax.axis_size("mp") - 1).bit_length()


def halving_masks():
    bits = bit_count()
    return [1, 2] + [1 << b for b in range(bits - 1, 1, -1)]


def relative_ids(masks):
    ids = np.zeros((1,), np.int32)
    for mask in reversed(masks):
        ids = np.concatenate([ids, ids ^ mask])
    return ids


def direct_ids():
    count = lax.axis_size("mp")
    far = np.arange(count // 2, dtype=np.int32) * 2
    return np.concatenate([far, far + 1])


def to_relative(chunks, ids):
    me = lax.axis_index("mp")
    return jnp.take(chunks, jnp.asarray(ids) ^ me, axis=0)


def to_absolute(chunks, ids):
    me = lax.axis_index("mp")
    place = np.argsort(ids).astype(np.int32)
    count = ids.shape[0]
    return jnp.take(chunks, jnp.asarray(place)[jnp.arange(count) ^ me], axis=0)


def scatter_halving(partial):
    masks = halving_masks()
    held = to_relative(partial, relative_ids(masks))
    for mask in masks:
        half = held.shape[0] // 2
        got = swap(held[half:].astype(jnp.bfloat16), mask)
        held = held[:half] + got.astype(jnp.float32)
    return held[0]


def gather_doubling(chunk):
    masks = halving_masks()
    held = chunk[None]
    for mask in reversed(masks):
        held = jnp.concatenate([held, swap(held, mask)], axis=0)
    return to_absolute(held, relative_ids(masks))


def scatter_direct(partial):
    held = to_relative(partial, direct_ids())
    half = held.shape[0] // 2
    held = held[:half] + swap(held[half:].astype(jnp.bfloat16), 1).astype(jnp.float32)
    low = held.astype(jnp.bfloat16)
    total = held[0]
    for far in range(1, half):
        total = total + swap(low[far], 2 * far).astype(jnp.float32)
    return total


def gather_direct(chunk):
    half = lax.axis_size("mp") // 2
    held = jnp.stack([chunk] + [swap(chunk, 2 * far) for far in range(1, half)])
    held = jnp.concatenate([held, swap(held, 1)], axis=0)
    return to_absolute(held, direct_ids())


def columns_to_chunks(values):
    count = lax.axis_size("mp")
    rows, width = values.shape
    return values.reshape(rows, count, width // count).transpose(1, 0, 2)


def chunks_to_columns(chunks):
    count, rows, width = chunks.shape
    return chunks.transpose(1, 0, 2).reshape(rows, count * width)


def norm_rows(values, norm_gain):
    wide = values.astype(jnp.float32)
    square_mean = jnp.mean(wide * wide, axis=-1, keepdims=True)
    return (wide * lax.rsqrt(square_mean + epsilon) * norm_gain).astype(jnp.bfloat16)


def rotate(features, positions):
    half_dim = HEAD_SIZE // 2
    frequency = 500000.0 ** (-2.0 * jnp.arange(half_dim, dtype=jnp.float32) / HEAD_SIZE)
    angles = positions.astype(jnp.float32)[:, None] * frequency[None, :]
    cosine = jnp.cos(angles)[:, None, :]
    sine_part = jnp.sin(angles)[:, None, :]
    wide = features.astype(jnp.float32).reshape(features.shape[0], -1, HEAD_SIZE)
    first_half = wide[..., :half_dim]
    second_half = wide[..., half_dim:]
    turned = jnp.concatenate(
        [
            first_half * cosine - second_half * sine_part,
            second_half * cosine + first_half * sine_part,
        ],
        axis=-1,
    )
    return turned.reshape(features.shape).astype(jnp.bfloat16)


def attend(query_rows, fresh_key, fresh_value, cached_key_rows, cached_value_rows, current):
    cached_row_count = query_rows.shape[0]
    heads_per_group = QUERY_HEADS // KEY_VALUE_HEADS
    score_scale = HEAD_SIZE ** (-0.5)
    query_head_rows = query_rows.reshape(
        cached_row_count, KEY_VALUE_HEADS, heads_per_group, HEAD_SIZE
    )
    key_head_rows = cached_key_rows.reshape(cached_row_count, -1, KEY_VALUE_HEADS, HEAD_SIZE)
    value_head_rows = cached_value_rows.reshape(cached_row_count, -1, KEY_VALUE_HEADS, HEAD_SIZE)
    scores = (
        jnp.einsum(
            "rgjd,rlgd->rgjl", query_head_rows, key_head_rows, preferred_element_type=jnp.float32
        )
        * score_scale
    )
    self_score = (
        jnp.einsum(
            "zneh,znh->zne",
            query_head_rows,
            fresh_key.reshape(cached_row_count, KEY_VALUE_HEADS, HEAD_SIZE),
            preferred_element_type=jnp.float32,
        )
        * score_scale
    )
    places = jnp.arange(key_head_rows.shape[1], dtype=jnp.int32)
    live = (places[None, :] < current[:, None])[:, None, None, :]
    scores = jnp.where(live, scores, -1e30)
    highest = jnp.maximum(jnp.max(scores, axis=-1), self_score)
    raised = jnp.exp(scores - highest[..., None])
    own_raised = jnp.exp(self_score - highest)
    denominator = jnp.sum(raised, axis=-1) + own_raised
    weights = (raised / denominator[..., None]).astype(jnp.bfloat16)
    self_weight = (own_raised / denominator).astype(jnp.bfloat16)
    mixed_output = jnp.einsum(
        "rgjl,rlgd->rgjd", weights, value_head_rows, preferred_element_type=jnp.float32
    )
    mixed_output = mixed_output + self_weight.astype(jnp.float32)[..., None] * fresh_value.astype(
        jnp.float32
    ).reshape(cached_row_count, KEY_VALUE_HEADS, 1, HEAD_SIZE)
    return mixed_output.reshape(cached_row_count, QUERY_HEADS * HEAD_SIZE).astype(jnp.bfloat16)


def body(
    hidden,
    attn_gain,
    w_query,
    w_key,
    w_value,
    w_out,
    mlp_gain,
    w_gate_up,
    w_down,
    key_cache,
    value_cache,
    lengths,
):
    rows_dev = hidden.shape[1]
    count = lax.axis_size("mp")
    section_index = lax.axis_index("section")
    model_index = lax.axis_index("mp")
    query_proj = w_query[0]
    key_proj = w_key[0]
    value_proj = w_value[0]
    out_proj = w_out[0]
    gate_up = w_gate_up[0]
    down_proj = w_down[0]
    first_gain = attn_gain[0]
    second_gain = mlp_gain[0]
    key_store = key_cache[0]
    value_store = value_cache[0]
    query_cols = query_proj.shape[1]
    key_cols = key_proj.shape[1]
    whole = gather_direct(hidden[0]).reshape(rows_dev * count, -1)
    width = whole.shape[1]
    mine = lax.dynamic_slice_in_dim(whole, model_index * (width // count), width // count, 1)
    for turn_index in range(2):
        project_normed = norm_rows(whole, first_gain)
        joined = jnp.concatenate(
            [
                jnp.dot(project_normed, query_proj, preferred_element_type=jnp.float32),
                jnp.dot(project_normed, key_proj, preferred_element_type=jnp.float32),
                jnp.dot(project_normed, value_proj, preferred_element_type=jnp.float32),
            ],
            axis=1,
        ).astype(jnp.bfloat16)
        micro_batch = jnp.remainder(section_index + turn_index, 2)
        spread = lax.all_to_all(
            joined.reshape(count, rows_dev, -1), "mp", split_axis=0, concat_axis=0
        ).transpose(1, 0, 2)
        query_rows = spread[..., :query_cols].reshape(rows_dev, -1)
        fresh_key = spread[..., query_cols : query_cols + key_cols].reshape(rows_dev, -1)
        fresh_value = spread[..., query_cols + key_cols :].reshape(rows_dev, -1)
        current = lax.dynamic_index_in_dim(lengths, micro_batch, 0, keepdims=False)
        cached_key_rows = lax.dynamic_index_in_dim(key_store, micro_batch, 0, keepdims=False)
        cached_value_rows = lax.dynamic_index_in_dim(value_store, micro_batch, 0, keepdims=False)
        mixed_output = attend(
            rotate(query_rows, current),
            rotate(fresh_key, current),
            fresh_value,
            cached_key_rows,
            cached_value_rows,
            current,
        )
        heads_out = lax.all_to_all(mixed_output, "mp", split_axis=1, concat_axis=0, tiled=True)
        partial = jnp.dot(heads_out, out_proj, preferred_element_type=jnp.float32)
        attn_part = scatter_halving(columns_to_chunks(partial))
        middle = (mine.astype(jnp.float32) + attn_part).astype(jnp.bfloat16)
        middle_whole = chunks_to_columns(gather_doubling(middle))
        gate_and_up = jnp.einsum(
            "rd,dcf->rcf",
            norm_rows(middle_whole, second_gain),
            gate_up,
            preferred_element_type=jnp.float32,
        )
        acts = (jax.nn.silu(gate_and_up[:, 0]) * gate_and_up[:, 1]).astype(jnp.bfloat16)
        partial = jnp.dot(acts, down_proj, preferred_element_type=jnp.float32)
        if turn_index == 0:
            mlp_part = scatter_direct(columns_to_chunks(partial))
            leaving = (middle.astype(jnp.float32) + mlp_part).astype(jnp.bfloat16)
            mine = swap(leaving, 1, "section")
            whole = chunks_to_columns(gather_direct(mine))
    mlp_part = scatter_direct(partial.reshape(count, rows_dev, width))
    middle_rows = lax.dynamic_slice_in_dim(middle_whole, model_index * rows_dev, rows_dev, 0)
    stream = (middle_rows.astype(jnp.float32) + mlp_part).astype(jnp.bfloat16)
    return stream[None]


def solution(mesh):
    placed = (
        P("section", "mp", None),
        P("section", None),
        P("section", None, "mp"),
        P("section", None, "mp"),
        P("section", None, "mp"),
        P("section", "mp", None),
        P("section", None),
        P("section", None, None, "mp"),
        P("section", "mp", None),
        P("section", None, "mp", None, None),
        P("section", None, "mp", None, None),
        P(None, "mp"),
    )
    return jax.shard_map(
        body, mesh=mesh, in_specs=placed, out_specs=P("section", "mp", None), check_vma=False
    )
```

```python
import functools

import jax
import jax.numpy as jnp
import numpy as np
from jax import lax
from jax.experimental import pallas as pl
from jax.experimental.pallas import tpu as pltpu
from jax.sharding import PartitionSpec as P

QUERY_HEADS = 64
KEY_VALUE_HEADS = 8
HEAD_SIZE = 128

epsilon = 1e-05

VMEM_LIMIT = 58 << 20


def swap(value, mask, axis="mp"):
    count = lax.axis_size(axis)
    return lax.ppermute(value, axis, [(source, source ^ mask) for source in range(count)])


def halving_masks():
    bits = (lax.axis_size("mp") - 1).bit_length()
    return [1, 2] + [1 << b for b in range(bits - 1, 1, -1)]


def relative_ids():
    ids = np.zeros((1,), np.int32)
    for mask in reversed(halving_masks()):
        ids = np.concatenate([ids, ids ^ mask])
    return ids


def finish_halving(held, masks):
    for mask in masks:
        half = held.shape[0] // 2
        got = swap(held[half:].astype(jnp.bfloat16), mask)
        held = held[:half] + got.astype(jnp.float32)
    return held[0]


def scatter_halving(send, keep):
    masks = halving_masks()
    held = keep.astype(jnp.float32) + swap(send, masks[0]).astype(jnp.float32)
    return finish_halving(held, masks[1:])


def scatter_exchange(send, keep):
    count = lax.axis_size("mp")
    half = count // 2
    held = keep.astype(jnp.float32) + swap(send, 1).astype(jnp.float32)
    place = np.argsort(relative_ids()[:half]).astype(np.int32)
    me = lax.axis_index("mp") // 2
    ordered = jnp.take(
        held.astype(jnp.bfloat16), jnp.asarray(place)[jnp.arange(half) ^ me], axis=0
    )
    groups = [list(range(core, count, 2)) for core in range(2)]
    got = lax.all_to_all(
        ordered, "mp", split_axis=0, concat_axis=0, axis_index_groups=groups, tiled=True
    )
    return jnp.sum(got.astype(jnp.float32), axis=0)


def gather_doubling(chunk):
    held = chunk[None]
    for mask in reversed(halving_masks()):
        held = jnp.concatenate([held, swap(held, mask)], axis=0)
    return held


def to_absolute(chunks):
    me = lax.axis_index("mp")
    place = np.argsort(relative_ids()).astype(np.int32)
    return jnp.take(chunks, jnp.asarray(place)[jnp.arange(place.shape[0]) ^ me], axis=0)


def columns_to_chunks(values, count):
    rows, width = values.shape
    return values.reshape(rows, count, width // count).transpose(1, 0, 2)


def vmem():
    return pl.BlockSpec(memory_space=pltpu.VMEM)


def smem():
    return pl.BlockSpec(memory_space=pltpu.SMEM)


def hbm():
    return pl.BlockSpec(memory_space=pl.ANY)


def inverse_rms(x_ref, count, rows):
    width = x_ref.shape[0] * x_ref.shape[2]

    def add(k, total):
        wide = x_ref[k].astype(jnp.float32)
        return total + jnp.sum(wide * wide, axis=-1, keepdims=True)

    total = lax.fori_loop(0, count, add, jnp.zeros((rows, 1), jnp.float32))
    return lax.rsqrt(total / width + epsilon)


def normed_chunk(x_ref, gain_ref, scale, k, place):
    wide = x_ref[k].astype(jnp.float32)
    return (wide * scale * gain_ref[pl.ds(place, 1), :]).astype(jnp.bfloat16)


def project_kernel(ids_ref, x_ref, gain_ref, wq_ref, wk_ref, wv_ref, out_ref,
                   q_buf, kv_buf, q_sum, kv_sum, sems):
    count, rows, chunk = x_ref.shape
    keys = wk_ref.shape[0]
    queries = wq_ref.shape[1]

    def copies(k):
        at = pl.multiple_of(ids_ref[k] * chunk, chunk)
        span = pl.ds(at, chunk)
        return (
            pltpu.make_async_copy(wq_ref.at[span, :], q_buf.at[k], sems.at[0, k]),
            pltpu.make_async_copy(wk_ref.at[:, span], kv_buf.at[k, pl.ds(0, keys)], sems.at[1, k]),
            pltpu.make_async_copy(
                wv_ref.at[:, span], kv_buf.at[k, pl.ds(keys, keys)], sems.at[2, k]
            ),
        )

    @pl.loop(0, count)
    def _(k):
        for copy in copies(k):
            copy.start()

    scale = inverse_rms(x_ref, count, rows)
    q_sum[...] = jnp.zeros_like(q_sum)
    kv_sum[...] = jnp.zeros_like(kv_sum)

    @pl.loop(0, count)
    def _(k):
        normed = normed_chunk(x_ref, gain_ref, scale, k, ids_ref[k])
        for copy in copies(k):
            copy.wait()
        q_sum[...] += jnp.dot(normed, q_buf[k], preferred_element_type=jnp.float32)
        kv_sum[...] += lax.dot_general(
            normed, kv_buf[k], (((1,), (1,)), ((), ())), preferred_element_type=jnp.float32
        )

    out_ref[:, :queries] = q_sum[...].astype(jnp.bfloat16)
    out_ref[:, queries:] = kv_sum[...].astype(jnp.bfloat16)


def project(ids, chunks, gain, wq, wk, wv):
    count, rows, chunk = chunks.shape
    queries, keys = wq.shape[1], wk.shape[0]
    return pl.pallas_call(
        project_kernel,
        out_shape=jax.ShapeDtypeStruct((rows, queries + 2 * keys), jnp.bfloat16),
        in_specs=[smem(), vmem(), vmem(), hbm(), hbm(), hbm()],
        out_specs=vmem(),
        scratch_shapes=[
            pltpu.VMEM((count, chunk, queries), jnp.bfloat16),
            pltpu.VMEM((count, 2 * keys, chunk), jnp.bfloat16),
            pltpu.VMEM((rows, queries), jnp.float32),
            pltpu.VMEM((rows, 2 * keys), jnp.float32),
            pltpu.SemaphoreType.DMA((3, count)),
        ],
        compiler_params=pltpu.CompilerParams(vmem_limit_bytes=VMEM_LIMIT),
    )(ids, chunks, gain.reshape(count, chunk), wq, wk, wv)


def attend_kernel(where_ref, length_ref, q_ref, k_ref, v_ref, cos_ref, sin_ref, keys_ref,
                  values_ref, out_ref, key_buf, value_buf, wide_q, sems):
    rows, heads, size = q_ref.shape
    groups = k_ref.shape[1]
    share = heads // groups
    places = key_buf.shape[1]
    batch = where_ref[0]

    def copies(row):
        return (
            pltpu.make_async_copy(keys_ref.at[batch, row], key_buf.at[row], sems.at[0, row]),
            pltpu.make_async_copy(values_ref.at[batch, row], value_buf.at[row], sems.at[1, row]),
        )

    for row in range(rows):
        for copy in copies(row):
            copy.start()
    wide_q[...] = jnp.zeros_like(wide_q)
    for row in range(rows):
        cosine = cos_ref[pl.ds(row, 1), :]
        sine = sin_ref[pl.ds(row, 1), :]

        def turned(features):
            wide = features.astype(jnp.float32)
            other = jnp.concatenate([wide[:, size // 2 :], wide[:, : size // 2]], axis=1)
            return (wide * cosine + other * sine).astype(jnp.bfloat16)

        query = turned(q_ref[row])
        own_key = turned(k_ref[row]).astype(jnp.float32)
        own_value = v_ref[row].astype(jnp.float32)
        own_parts = []
        for group in range(groups):
            part = query[group * share : (group + 1) * share]
            wide_q[group * share : (group + 1) * share, group * size : (group + 1) * size] = part
            own_parts.append(
                jnp.sum(part.astype(jnp.float32) * own_key[group : group + 1], axis=1, keepdims=True)
            )
        own_score = jnp.concatenate(own_parts, axis=0) * (size ** -0.5)
        key_copy, value_copy = copies(row)
        key_copy.wait()
        scores = lax.dot_general(
            wide_q[...], key_buf[row], (((1,), (1,)), ((), ())), preferred_element_type=jnp.float32
        ) * (size ** -0.5)
        spot = lax.broadcasted_iota(jnp.int32, (heads, places), 1)
        scores = jnp.where(spot < length_ref[batch, row], scores, -1e30)
        highest = jnp.maximum(jnp.max(scores, axis=1, keepdims=True), own_score)
        raised = jnp.exp(scores - highest)
        own_raised = jnp.exp(own_score - highest)
        denominator = jnp.sum(raised, axis=1, keepdims=True) + own_raised
        weights = (raised / denominator).astype(jnp.bfloat16)
        own_weight = (own_raised / denominator).astype(jnp.bfloat16).astype(jnp.float32)
        value_copy.wait()
        mixed = jnp.dot(weights, value_buf[row], preferred_element_type=jnp.float32)
        for group in range(groups):
            span = slice(group * share, (group + 1) * share)
            out_ref[row, span, :] = (
                mixed[span, group * size : (group + 1) * size]
                + own_weight[span] * own_value[group : group + 1]
            ).astype(jnp.bfloat16)


def attend(where, lengths, query, key, value, cosine, sine, key_store, value_store):
    rows, heads, size = query.shape
    places, width = key_store.shape[2:]
    return pl.pallas_call(
        attend_kernel,
        out_shape=jax.ShapeDtypeStruct(query.shape, jnp.bfloat16),
        in_specs=[smem(), smem()] + [vmem()] * 5 + [hbm(), hbm()],
        out_specs=vmem(),
        scratch_shapes=[
            pltpu.VMEM((rows, places, width), jnp.bfloat16),
            pltpu.VMEM((rows, places, width), jnp.bfloat16),
            pltpu.VMEM((heads, width), jnp.bfloat16),
            pltpu.SemaphoreType.DMA((2, rows)),
        ],
        compiler_params=pltpu.CompilerParams(vmem_limit_bytes=VMEM_LIMIT),
    )(where, lengths, query, key, value, cosine, sine, key_store, value_store)


def spread_kernel(ids_ref, x_ref, w_ref, send_ref, keep_ref, w_buf, sems):
    count, _, chunk = w_buf.shape
    half = count // 2

    def copy(k):
        at = pl.multiple_of(ids_ref[k] * chunk, chunk)
        return pltpu.make_async_copy(w_ref.at[:, pl.ds(at, chunk)], w_buf.at[k], sems.at[k])

    @pl.loop(0, count)
    def _(k):
        copy((k + half) % count).start()

    values = x_ref[...]
    for start, target in ((half, send_ref), (0, keep_ref)):

        @pl.loop(0, half)
        def _(k):
            copy(start + k).wait()
            target[k] = jnp.dot(
                values, w_buf[start + k], preferred_element_type=jnp.float32
            ).astype(jnp.bfloat16)


def spread_project(ids, values, weights):
    rows, depth = values.shape
    count = ids.shape[0]
    chunk = weights.shape[1] // count
    shape = jax.ShapeDtypeStruct((count // 2, rows, chunk), jnp.bfloat16)
    return pl.pallas_call(
        spread_kernel,
        out_shape=(shape, shape),
        in_specs=[smem(), vmem(), hbm()],
        out_specs=(vmem(), vmem()),
        scratch_shapes=[
            pltpu.VMEM((count, depth, chunk), jnp.bfloat16),
            pltpu.SemaphoreType.DMA((count,)),
        ],
        compiler_params=pltpu.CompilerParams(vmem_limit_bytes=VMEM_LIMIT),
    )(ids, values, weights)


def mlp_kernel(ids_ref, x_ref, gain_ref, gu_ref, down_ref, send_ref, keep_ref,
               gu_buf, down_buf, wide_x, total, act, gu_sems, down_sems):
    count, rows, chunk = x_ref.shape
    blocks = gu_buf.shape[1]
    half = count // 2

    def gu_copies(k):
        at = pl.multiple_of(ids_ref[k] * chunk, chunk)
        return [
            pltpu.make_async_copy(
                gu_ref.at[pl.ds(at, chunk), :, pl.ds(j * 128, 128)],
                gu_buf.at[k, j],
                gu_sems.at[k, j],
            )
            for j in range(blocks)
        ]

    def down_copy(k):
        at = pl.multiple_of(ids_ref[k] * chunk, chunk)
        return pltpu.make_async_copy(
            down_ref.at[:, pl.ds(at, chunk)], down_buf.at[k], down_sems.at[k]
        )

    @pl.loop(0, count)
    def _(k):
        for copy in gu_copies(k):
            copy.start()

    @pl.loop(0, count)
    def _(k):
        down_copy((k + half) % count).start()

    scale = inverse_rms(x_ref, count, rows)
    total[...] = jnp.zeros_like(total)
    line = lax.broadcasted_iota(jnp.int32, (128, 512), 0)
    column = lax.broadcasted_iota(jnp.int32, (128, 512), 1)
    aim = jnp.where(column < 256, 2 * line, 2 * line + 257)
    widen = jnp.where(column == aim, 1.0, 0.0).astype(jnp.bfloat16)

    @pl.loop(0, count)
    def _(k):
        normed = normed_chunk(x_ref, gain_ref, scale, k, ids_ref[k])
        for b in range(chunk // 128):
            wide = jnp.dot(
                normed[:, b * 128 : (b + 1) * 128], widen, preferred_element_type=jnp.float32
            ).astype(jnp.bfloat16)
            wide_x[:rows, b * 256 : (b + 1) * 256] = wide[:, :256]
            wide_x[rows:, b * 256 : (b + 1) * 256] = wide[:, 256:]
        for copy in gu_copies(k):
            copy.wait()
        for j in range(0, blocks, 2):
            pair = jnp.concatenate(
                [gu_buf.at[k, j + i].reshape(2 * chunk, 128)[...] for i in range(2)], axis=1
            )
            total[:, j * 128 : (j + 2) * 128] += jnp.dot(
                wide_x[...], pair, preferred_element_type=jnp.float32
            )

    gate = total[:rows, :]
    act[...] = (gate / (1.0 + jnp.exp(-gate)) * total[rows:, :]).astype(jnp.bfloat16)

    for start, target in ((half, send_ref), (0, keep_ref)):

        @pl.loop(0, half)
        def _(k):
            down_copy(start + k).wait()
            target[k] = jnp.dot(
                act[...], down_buf[start + k], preferred_element_type=jnp.float32
            ).astype(jnp.bfloat16)


def mlp(ids, chunks, gain, gate_up, down):
    count, rows, chunk = chunks.shape
    units = down.shape[0]
    shape = jax.ShapeDtypeStruct((count // 2, rows, chunk), jnp.bfloat16)
    return pl.pallas_call(
        mlp_kernel,
        out_shape=(shape, shape),
        in_specs=[smem(), vmem(), vmem(), hbm(), hbm()],
        out_specs=(vmem(), vmem()),
        scratch_shapes=[
            pltpu.VMEM((count, units // 128, chunk, 2, 128), jnp.bfloat16),
            pltpu.VMEM((count, units, chunk), jnp.bfloat16),
            pltpu.VMEM((2 * rows, 2 * chunk), jnp.bfloat16),
            pltpu.VMEM((2 * rows, units), jnp.float32),
            pltpu.VMEM((rows, units), jnp.bfloat16),
            pltpu.SemaphoreType.DMA((count, units // 128)),
            pltpu.SemaphoreType.DMA((count,)),
        ],
        compiler_params=pltpu.CompilerParams(vmem_limit_bytes=VMEM_LIMIT),
    )(ids, chunks, gain.reshape(count, chunk), gate_up, down)


def turning(positions):
    half_dim = HEAD_SIZE // 2
    frequency = 500000.0 ** (-2.0 * jnp.arange(half_dim, dtype=jnp.float32) / HEAD_SIZE)
    angles = positions.astype(jnp.float32)[:, None] * frequency[None, :]
    cosine = jnp.cos(angles)
    sine = jnp.sin(angles)
    return jnp.concatenate([cosine, cosine], axis=1), jnp.concatenate([-sine, sine], axis=1)


def body(
    hidden,
    attn_gain,
    w_query,
    w_key,
    w_value,
    w_out,
    mlp_gain,
    w_gate_up,
    w_down,
    key_cache,
    value_cache,
    lengths,
):
    rows_dev = hidden.shape[1]
    count = lax.axis_size("mp")
    rows = rows_dev * count
    section_index = lax.axis_index("section")
    model_index = lax.axis_index("mp")
    query_cols = w_query.shape[2]
    key_cols = w_key.shape[2]
    width = hidden.shape[2]
    ids = jnp.asarray(relative_ids()) ^ model_index
    straight = jnp.arange(count, dtype=jnp.int32)
    wk = w_key[0].T
    wv = w_value[0].T
    start = to_absolute(gather_doubling(hidden[0])).reshape(rows, width)
    chunks = columns_to_chunks(start, count)
    mine = lax.dynamic_index_in_dim(chunks, model_index, 0, keepdims=False)
    order = straight
    for turn_index in range(2):
        batch = jnp.remainder(section_index + turn_index, 2).astype(jnp.int32)
        cosine, sine = turning(lax.dynamic_index_in_dim(lengths, batch, 0, keepdims=False))
        joined = project(order, chunks, attn_gain[0], w_query[0], wk, wv)
        spread = lax.all_to_all(
            joined.reshape(count, rows_dev, -1), "mp", split_axis=0, concat_axis=0
        ).transpose(1, 0, 2)
        query = spread[..., :query_cols].reshape(rows_dev, QUERY_HEADS, HEAD_SIZE)
        key = spread[..., query_cols : query_cols + key_cols].reshape(
            rows_dev, KEY_VALUE_HEADS, HEAD_SIZE
        )
        value = spread[..., query_cols + key_cols :].reshape(rows_dev, KEY_VALUE_HEADS, HEAD_SIZE)
        mixed = attend(
            batch.reshape(1), lengths, query, key, value, cosine, sine, key_cache[0], value_cache[0]
        )
        heads_out = lax.all_to_all(
            mixed.reshape(rows_dev, QUERY_HEADS * HEAD_SIZE),
            "mp",
            split_axis=1,
            concat_axis=0,
            tiled=True,
        )
        attn_part = scatter_halving(*spread_project(ids, heads_out, w_out[0]))
        middle = (mine.astype(jnp.float32) + attn_part).astype(jnp.bfloat16)
        send, keep = mlp(ids, gather_doubling(middle), mlp_gain[0], w_gate_up[0], w_down[0])
        mlp_part = scatter_exchange(send, keep)
        mine = (middle.astype(jnp.float32) + mlp_part).astype(jnp.bfloat16)
        if turn_index == 0:
            mine = swap(mine, 1, "section")
            chunks = gather_doubling(mine)
            order = ids
    parts = lax.all_to_all(
        mine.reshape(count, rows_dev, width // count), "mp", split_axis=0, concat_axis=0
    )
    return parts.transpose(1, 0, 2).reshape(1, rows_dev, width)


def solution(mesh):
    placed = (
        P("section", "mp", None),
        P("section", None),
        P("section", None, "mp"),
        P("section", None, "mp"),
        P("section", None, "mp"),
        P("section", "mp", None),
        P("section", None),
        P("section", None, None, "mp"),
        P("section", "mp", None),
        P("section", None, "mp", None, None),
        P("section", None, "mp", None, None),
        P(None, "mp"),
    )
    return jax.shard_map(
        body, mesh=mesh, in_specs=placed, out_specs=P("section", "mp", None), check_vma=False
    )
```

```python
import functools

import jax
import jax.numpy as jnp
from jax import lax
from jax.experimental import pallas as pl
from jax.experimental.pallas import tpu as pltpu
from jax.sharding import PartitionSpec as P

QUERY_HEADS = 64
KEY_VALUE_HEADS = 8
HEAD_SIZE = 128

epsilon = 1e-05


def swap(value, mask, axis="mp"):
    count = lax.axis_size(axis)
    return lax.ppermute(value, axis, [(source, source ^ mask) for source in range(count)])


def exchange(parts):
    count = lax.axis_size("mp")
    groups = [list(range(core, count, 2)) for core in range(2)]
    return lax.all_to_all(
        parts, "mp", split_axis=0, concat_axis=0, axis_index_groups=groups, tiled=True
    )


def scatter(send, keep):
    held = keep.astype(jnp.float32) + swap(send, 1).astype(jnp.float32)
    return jnp.sum(exchange(held.astype(jnp.bfloat16)).astype(jnp.float32), axis=0)


def gather(part):
    own = exchange(jnp.broadcast_to(part[None], (lax.axis_size("mp") // 2,) + part.shape))
    return own, swap(own, 1)


def columns_to_chunks(values, count):
    rows, width = values.shape
    return values.reshape(rows, count, width // count).transpose(1, 0, 2)


def vmem():
    return pl.BlockSpec(memory_space=pltpu.VMEM)


def smem():
    return pl.BlockSpec(memory_space=pltpu.SMEM)


def resident(weights):
    return pltpu.with_memory_space_constraint(weights, pltpu.VMEM)


def hbm():
    return pl.BlockSpec(memory_space=pl.ANY)


def inverse_rms(x_refs):
    half, rows, chunk = x_refs[0].shape
    total = jnp.zeros((rows, 1), jnp.float32)
    for x_ref in x_refs:

        def add(k, total):
            wide = x_ref[k].astype(jnp.float32)
            return total + jnp.sum(wide * wide, axis=-1, keepdims=True)

        total = lax.fori_loop(0, half, add, total)
    return lax.rsqrt(total / (2 * half * chunk) + epsilon)


def span_of(ids_ref, k, chunk):
    return pl.ds(pl.multiple_of(ids_ref[k] * chunk, chunk), chunk)


def normed_chunk(x_ref, gain_ref, scale, k, span):
    wide = x_ref[k].astype(jnp.float32)
    return (wide * scale * gain_ref[:, span]).astype(jnp.bfloat16)


def project_kernel(ids_ref, own_ref, other_ref, gain_ref, wq_ref, wk_ref, wv_ref, out_ref,
                   q_sum, kv_sum):
    half, rows, chunk = own_ref.shape
    queries = wq_ref.shape[1]
    keys = wk_ref.shape[0]
    count, rows_dev, _ = out_ref.shape
    scale = inverse_rms((own_ref, other_ref))
    q_sum[...] = jnp.zeros_like(q_sum)
    kv_sum[...] = jnp.zeros_like(kv_sum)
    for first, x_ref in ((0, own_ref), (half, other_ref)):

        @pl.loop(0, half)
        def _(k):
            span = span_of(ids_ref, first + k, chunk)
            normed = normed_chunk(x_ref, gain_ref, scale, k, span)
            q_sum[...] += jnp.dot(normed, wq_ref[span, :], preferred_element_type=jnp.float32)
            for at, w_ref in ((0, wk_ref), (keys, wv_ref)):
                kv_sum[:, at : at + keys] += lax.dot_general(
                    normed,
                    w_ref[:, span],
                    (((1,), (1,)), ((), ())),
                    preferred_element_type=jnp.float32,
                )

    for owner in range(count):
        lines = slice(owner * rows_dev, (owner + 1) * rows_dev)
        out_ref[owner, :, :queries] = q_sum[lines, :].astype(jnp.bfloat16)
        out_ref[owner, :, queries:] = kv_sum[lines, :].astype(jnp.bfloat16)


def project(ids, own, other, gain, wq, wk, wv):
    half, rows, _ = own.shape
    queries, keys = wq.shape[1], wk.shape[0]
    size = queries + 2 * keys
    return pl.pallas_call(
        project_kernel,
        out_shape=pltpu.VMEM((2 * half, rows // (2 * half), size), jnp.bfloat16),
        in_specs=[smem()] + [vmem()] * 6,
        out_specs=vmem(),
        scratch_shapes=[
            pltpu.VMEM((rows, queries), jnp.float32),
            pltpu.VMEM((rows, 2 * keys), jnp.float32),
        ],
        compiler_params=pltpu.CompilerParams(vmem_limit_bytes=4 << 20),
        cost_estimate=pl.CostEstimate(
            flops=2 * rows * wq.shape[0] * size,
            bytes_accessed=2 * wq.shape[0] * size,
            transcendentals=0,
        ),
    )(ids, own, other, gain, resident(wq), resident(wk), resident(wv))


def attend_kernel(where_ref, length_ref, q_ref, kv_ref, cos_ref, sin_ref, keys_ref,
                  values_ref, out_ref, key_buf, value_buf, wide_q, sems):
    rows, devices, queries = q_ref.shape
    _, _, groups, size = kv_ref.shape
    slots = queries // size
    heads = devices * slots
    places = key_buf.shape[1]
    batch = where_ref[0]

    def copies(row):
        return (
            pltpu.make_async_copy(keys_ref.at[batch, row], key_buf.at[row], sems.at[0, row]),
            pltpu.make_async_copy(values_ref.at[batch, row], value_buf.at[row], sems.at[1, row]),
        )

    for row in range(rows):
        for which, copy in enumerate(copies(row)):
            copy.start(priority=which)
    line = lax.broadcasted_iota(jnp.int32, (devices, 1), 0)
    group_of = line * groups // devices
    for row in range(rows):
        cosine = cos_ref[pl.ds(row, 1), :]
        sine = sin_ref[pl.ds(row, 1), :]

        def turned(features):
            wide = features.astype(jnp.float32)
            other = jnp.concatenate([wide[:, size // 2 :], wide[:, : size // 2]], axis=1)
            return (wide * cosine + other * sine).astype(jnp.bfloat16).astype(jnp.float32)

        own_key = turned(kv_ref[row, 0])
        own_value = kv_ref[row, 1].astype(jnp.float32)
        key_lines = jnp.zeros((devices, size), jnp.float32)
        value_lines = jnp.zeros((devices, size), jnp.float32)
        for group in range(groups):
            here = group_of == group
            key_lines = jnp.where(here, own_key[group : group + 1], key_lines)
            value_lines = jnp.where(here, own_value[group : group + 1], value_lines)
        own_parts = []
        for slot in range(slots):
            part = turned(q_ref[row, :, slot * size : (slot + 1) * size])
            own_parts.append(jnp.sum(part * key_lines, axis=1, keepdims=True))
            for group in range(groups):
                wide_q[
                    slot * devices : (slot + 1) * devices, group * size : (group + 1) * size
                ] = jnp.where(group_of == group, part, 0.0).astype(jnp.bfloat16)
        own_score = jnp.concatenate(own_parts, axis=0) * (size ** -0.5)
        key_copy, value_copy = copies(row)
        key_copy.wait()
        scores = lax.dot_general(
            wide_q[...], key_buf[row], (((1,), (1,)), ((), ())), preferred_element_type=jnp.float32
        ) * (size ** -0.5)
        spot = lax.broadcasted_iota(jnp.int32, (heads, places), 1)
        scores = jnp.where(spot < length_ref[batch, row], scores, -1e30)
        highest = jnp.maximum(jnp.max(scores, axis=1, keepdims=True), own_score)
        raised = jnp.exp(scores - highest)
        own_raised = jnp.exp(own_score - highest)
        denominator = jnp.sum(raised, axis=1, keepdims=True) + own_raised
        weights = (raised / denominator).astype(jnp.bfloat16)
        own_weight = (own_raised / denominator).astype(jnp.bfloat16).astype(jnp.float32)
        value_copy.wait()
        mixed = jnp.dot(weights, value_buf[row], preferred_element_type=jnp.float32)
        for slot in range(slots):
            lines = slice(slot * devices, (slot + 1) * devices)
            picked = own_weight[lines] * value_lines
            for group in range(groups):
                picked = picked + jnp.where(
                    group_of == group, mixed[lines, group * size : (group + 1) * size], 0.0
                )
            out_ref[row, :, slot * size : (slot + 1) * size] = picked.astype(jnp.bfloat16)


def attend(where, lengths, query, fresh, cosine, sine, key_store, value_store):
    rows, devices, queries = query.shape
    places, width = key_store.shape[2:]
    heads = devices * queries // HEAD_SIZE
    return pl.pallas_call(
        attend_kernel,
        out_shape=pltpu.VMEM(query.shape, jnp.bfloat16),
        in_specs=[smem(), smem()] + [vmem()] * 4 + [hbm(), hbm()],
        out_specs=vmem(),
        scratch_shapes=[
            pltpu.VMEM((rows, places, width), jnp.bfloat16),
            pltpu.VMEM((rows, places, width), jnp.bfloat16),
            pltpu.VMEM((heads, width), jnp.bfloat16),
            pltpu.SemaphoreType.DMA((2, rows)),
        ],
        compiler_params=pltpu.CompilerParams(vmem_limit_bytes=8 << 20),
        cost_estimate=pl.CostEstimate(
            flops=4 * rows * heads * places * width,
            bytes_accessed=4 * rows * places * width,
            transcendentals=rows * heads * places,
        ),
    )(where, lengths, query, fresh, cosine, sine, key_store, value_store)


def spread_kernel(ids_ref, x_ref, w_ref, keep_ref, send_ref, values):
    half, rows, chunk = keep_ref.shape
    count, rows_dev, _ = x_ref.shape
    for owner in range(count):
        values[owner * rows_dev : (owner + 1) * rows_dev, :] = x_ref[owner].astype(jnp.float32)
    ready = values[...].astype(jnp.bfloat16)
    for first, target in ((0, keep_ref), (half, send_ref)):

        @pl.loop(0, half)
        def _(k):
            span = span_of(ids_ref, first + k, chunk)
            target[k] = jnp.dot(
                ready, w_ref[:, span], preferred_element_type=jnp.float32
            ).astype(jnp.bfloat16)


def spread_project(ids, values, weights):
    count, rows_dev, depth = values.shape
    rows = count * rows_dev
    width = weights.shape[1]
    shape = pltpu.VMEM((count // 2, rows, width // count), jnp.bfloat16)
    return pl.pallas_call(
        spread_kernel,
        out_shape=(shape, shape),
        in_specs=[smem(), vmem(), vmem()],
        out_specs=(vmem(), vmem()),
        scratch_shapes=[pltpu.VMEM((rows, depth), jnp.float32)],
        compiler_params=pltpu.CompilerParams(vmem_limit_bytes=4 << 20),
        cost_estimate=pl.CostEstimate(
            flops=2 * rows * depth * width, bytes_accessed=2 * depth * width, transcendentals=0
        ),
    )(ids, values, resident(weights))


def mlp_kernel(by_rows, ids_ref, own_ref, other_ref, gain_ref, gu_ref, down_ref, keep_ref,
               send_ref, gu_buf, wide_x, total, act, gu_sems):
    half, rows, chunk = own_ref.shape
    blocks = gu_buf.shape[1]

    def gu_copies(k):
        span = span_of(ids_ref, k, chunk)
        return [
            pltpu.make_async_copy(
                gu_ref.at[span, :, pl.ds(j * 128, 128)], gu_buf.at[k, j], gu_sems.at[k, j]
            )
            for j in range(blocks)
        ]

    @pl.loop(0, 2 * half)
    def _(k):
        for j, copy in enumerate(gu_copies(k)):
            copy.start(priority=j % 2)

    scale = inverse_rms((own_ref, other_ref))
    total[...] = jnp.zeros_like(total)
    line = lax.broadcasted_iota(jnp.int32, (128, 512), 0)
    column = lax.broadcasted_iota(jnp.int32, (128, 512), 1)
    aim = jnp.where(column < 256, 2 * line, 2 * line + 257)
    widen = jnp.where(column == aim, 1.0, 0.0).astype(jnp.bfloat16)

    for first, x_ref in ((0, own_ref), (half, other_ref)):

        @pl.loop(0, half)
        def _(place):
            k = first + place
            span = span_of(ids_ref, k, chunk)
            normed = normed_chunk(x_ref, gain_ref, scale, place, span)
            for b in range(chunk // 128):
                wide = jnp.dot(
                    normed[:, b * 128 : (b + 1) * 128], widen, preferred_element_type=jnp.float32
                ).astype(jnp.bfloat16)
                wide_x[:rows, b * 256 : (b + 1) * 256] = wide[:, :256]
                wide_x[rows:, b * 256 : (b + 1) * 256] = wide[:, 256:]
            for copy in gu_copies(k):
                copy.wait()
            for j in range(0, blocks, 2):
                pair = jnp.concatenate(
                    [gu_buf.at[k, j + i].reshape(2 * chunk, 128)[...] for i in range(2)], axis=1
                )
                total[:, j * 128 : (j + 2) * 128] += jnp.dot(
                    wide_x[...], pair, preferred_element_type=jnp.float32
                )

    gate = total[:rows, :]
    act[...] = (gate / (1.0 + jnp.exp(-gate)) * total[rows:, :]).astype(jnp.bfloat16)

    def down(span):
        return jnp.dot(act[...], down_ref[:, span], preferred_element_type=jnp.float32)

    if by_rows:
        rows_dev = keep_ref.shape[1]
        first_core = ids_ref[0] == 0

        @pl.loop(0, 2 * half)
        def _(k):
            span = span_of(ids_ref, k, chunk)
            part = down(span)
            for chip in range(half):
                at = 2 * chip * rows_dev
                low = part[at : at + rows_dev]
                high = part[at + rows_dev : at + 2 * rows_dev]
                keep_ref[chip, :, span] = jnp.where(first_core, low, high).astype(jnp.bfloat16)
                send_ref[chip, :, span] = jnp.where(first_core, high, low).astype(jnp.bfloat16)

    else:
        for first, target in ((0, keep_ref), (half, send_ref)):

            @pl.loop(0, half)
            def _(k):
                target[k] = down(span_of(ids_ref, first + k, chunk)).astype(jnp.bfloat16)


def mlp(ids, own, other, gain, gate_up, down, by_rows):
    half, rows, chunk = own.shape
    units, width = down.shape
    part = (half, rows // (2 * half), width) if by_rows else own.shape
    shape = pltpu.VMEM(part, jnp.bfloat16)
    return pl.pallas_call(
        functools.partial(mlp_kernel, by_rows),
        out_shape=(shape, shape),
        in_specs=[smem(), vmem(), vmem(), vmem(), hbm(), vmem()],
        out_specs=(vmem(), vmem()),
        scratch_shapes=[
            pltpu.VMEM((2 * half, units // 128, chunk, 2, 128), jnp.bfloat16),
            pltpu.VMEM((2 * rows, 2 * chunk), jnp.bfloat16),
            pltpu.VMEM((2 * rows, units), jnp.float32),
            pltpu.VMEM((rows, units), jnp.bfloat16),
            pltpu.SemaphoreType.DMA((2 * half, units // 128)),
        ],
        compiler_params=pltpu.CompilerParams(vmem_limit_bytes=37 << 20),
        cost_estimate=pl.CostEstimate(
            flops=6 * rows * units * width, bytes_accessed=6 * units * width, transcendentals=0
        ),
    )(ids, own, other, gain, gate_up, resident(down))


def turning(positions):
    half_dim = HEAD_SIZE // 2
    frequency = 500000.0 ** (-2.0 * jnp.arange(half_dim, dtype=jnp.float32) / HEAD_SIZE)
    angles = positions.astype(jnp.float32)[:, None] * frequency[None, :]
    cosine = jnp.cos(angles)
    sine = jnp.sin(angles)
    return jnp.concatenate([cosine, cosine], axis=1), jnp.concatenate([-sine, sine], axis=1)


def body(
    hidden,
    attn_gain,
    w_query,
    w_key,
    w_value,
    w_out,
    mlp_gain,
    w_gate_up,
    w_down,
    key_cache,
    value_cache,
    lengths,
):
    rows_dev = hidden.shape[1]
    count = lax.axis_size("mp")
    half = count // 2
    rows = rows_dev * count
    section_index = lax.axis_index("section")
    model_index = lax.axis_index("mp")
    core = model_index % 2
    query_cols = w_query.shape[2]
    key_cols = w_key.shape[2]
    width = hidden.shape[2]
    chips = 2 * jnp.arange(half, dtype=jnp.int32)
    ids = jnp.concatenate([chips + core, chips + 1 - core])
    wk = w_key[0].T
    wv = w_value[0].T

    def by_core(own, other):
        pair = jnp.where(core == 0, jnp.stack([own, other], 1), jnp.stack([other, own], 1))
        return pair.reshape((count,) + own.shape[1:])

    start = by_core(*gather(hidden[0])).reshape(rows, width)
    chunks = columns_to_chunks(start, count)
    mine = lax.dynamic_index_in_dim(chunks, model_index, 0, keepdims=False)
    own, other = chunks[:half], chunks[half:]
    order = jnp.arange(count, dtype=jnp.int32)
    for turn_index in range(2):
        batch = jnp.remainder(section_index + turn_index, 2).astype(jnp.int32)
        cosine, sine = turning(lax.dynamic_index_in_dim(lengths, batch, 0, keepdims=False))
        joined = project(order, own, other, attn_gain, w_query[0], wk, wv)
        spread = lax.all_to_all(joined, "mp", split_axis=0, concat_axis=0)
        query = spread[..., :query_cols].transpose(1, 0, 2)
        fresh = (
            spread[..., query_cols:]
            .reshape(count, rows_dev, 2, key_cols)
            .transpose(1, 2, 0, 3)
            .reshape(rows_dev, 2, KEY_VALUE_HEADS, HEAD_SIZE)
        )
        mixed = attend(
            batch.reshape(1), lengths, query, fresh, cosine, sine, key_cache[0], value_cache[0]
        )
        heads_out = lax.all_to_all(mixed.transpose(1, 0, 2), "mp", split_axis=0, concat_axis=0)
        keep, send = spread_project(ids, heads_out, w_out[0])
        middle = (mine.astype(jnp.float32) + scatter(send, keep)).astype(jnp.bfloat16)
        own, other = gather(middle)
        last = turn_index == 1
        keep, send = mlp(ids, own, other, mlp_gain, w_gate_up[0], w_down[0], last)
        mlp_part = scatter(send, keep)
        if last:
            at = model_index * rows_dev
            mine = by_core(
                lax.dynamic_slice_in_dim(own, at, rows_dev, 1),
                lax.dynamic_slice_in_dim(other, at, rows_dev, 1),
            )
            middle = mine.transpose(1, 0, 2).reshape(rows_dev, width)
        mine = (middle.astype(jnp.float32) + mlp_part).astype(jnp.bfloat16)
        if not last:
            mine = swap(mine, 1, "section")
            own, other = gather(mine)
            order = ids
    return mine[None]


def solution(mesh):
    placed = (
        P("section", "mp", None),
        P("section", None),
        P("section", None, "mp"),
        P("section", None, "mp"),
        P("section", None, "mp"),
        P("section", "mp", None),
        P("section", None),
        P("section", None, None, "mp"),
        P("section", "mp", None),
        P("section", None, "mp", None, None),
        P("section", None, "mp", None, None),
        P(None, "mp"),
    )
    return jax.shard_map(
        body, mesh=mesh, in_specs=placed, out_specs=P("section", "mp", None), check_vma=False
    )
```

```python
import functools

import jax
import jax.numpy as jnp
from jax import lax
from jax.experimental import pallas as pl
from jax.experimental.pallas import tpu as pltpu
from jax.sharding import PartitionSpec as P

QUERY_HEADS = 64
KEY_VALUE_HEADS = 8
HEAD_SIZE = 128

epsilon = 1e-05

UNROLL = 4


def swap(value, mask, axis="mp"):
    count = lax.axis_size(axis)
    return lax.ppermute(value, axis, [(source, source ^ mask) for source in range(count)])


def exchange(parts):
    count = lax.axis_size("mp")
    groups = [list(range(core, count, 2)) for core in range(2)]
    return lax.all_to_all(
        parts, "mp", split_axis=0, concat_axis=0, axis_index_groups=groups, tiled=True
    )


def merge(send, keep):
    held = keep.astype(jnp.float32) + swap(send, 1).astype(jnp.float32)
    return held.astype(jnp.bfloat16)


def scatter(held):
    return jnp.sum(exchange(held).astype(jnp.float32), axis=0)


def gather(part):
    own = exchange(jnp.broadcast_to(part[None], (lax.axis_size("mp") // 2,) + part.shape))
    return own, swap(own, 1)


def columns_to_chunks(values, count):
    rows, width = values.shape
    return values.reshape(rows, count, width // count).transpose(1, 0, 2)


def vmem():
    return pl.BlockSpec(memory_space=pltpu.VMEM)


def smem():
    return pl.BlockSpec(memory_space=pltpu.SMEM)


def placed_in(values, space):
    return pltpu.with_memory_space_constraint(values, space)


def hbm():
    return pl.BlockSpec(memory_space=pl.ANY)


def run_copies(copies):
    for at, copy in enumerate(copies):
        copy.start(priority=at % 2)
    for copy in copies:
        copy.wait()


def fetch_kernel(pieces, token_ref, *refs):
    arrays = len(pieces)
    sems = refs[-1]
    copies = []
    for array, (count, source, target) in enumerate(zip(pieces, refs, refs[arrays:])):
        size = source.shape[0] // count
        for piece in range(count):
            span = pl.ds(piece * size, size)
            copies.append(
                pltpu.make_async_copy(source.at[span], target.at[span], sems.at[array, piece])
            )
    run_copies(copies)


def fetch(token, *arrays):
    pieces = [8 if array.shape[0] % 128 == 0 else 1 for array in arrays]
    return pl.pallas_call(
        functools.partial(fetch_kernel, pieces),
        out_shape=[pltpu.VMEM(array.shape, array.dtype) for array in arrays],
        in_specs=[hbm()] * (1 + len(arrays)),
        out_specs=[vmem()] * len(arrays),
        scratch_shapes=[pltpu.SemaphoreType.DMA((len(arrays), 8))],
        compiler_params=pltpu.CompilerParams(vmem_limit_bytes=1 << 20),
        cost_estimate=pl.CostEstimate(
            flops=0, bytes_accessed=sum(2 * array.size for array in arrays), transcendentals=0
        ),
    )(token, *[placed_in(array, pltpu.HBM) for array in arrays])


def fetch_caches_kernel(token_ref, where_ref, keys_ref, values_ref, key_ref, value_ref, sems):
    rows, places, _ = key_ref.shape
    batch = where_ref[0]
    copies = []
    for array, (source, target) in enumerate(((keys_ref, key_ref), (values_ref, value_ref))):
        for row in range(rows):
            for piece in range(2):
                span = pl.ds(piece * (places // 2), places // 2)
                copies.append(
                    pltpu.make_async_copy(
                        source.at[batch, row, span],
                        target.at[row, span],
                        sems.at[array, row, piece],
                    )
                )
    run_copies(copies)


def fetch_caches(token, where, keys, values):
    shape = pltpu.VMEM(keys.shape[1:], keys.dtype)
    return pl.pallas_call(
        fetch_caches_kernel,
        out_shape=[shape, shape],
        in_specs=[hbm(), smem(), hbm(), hbm()],
        out_specs=[vmem(), vmem()],
        scratch_shapes=[pltpu.SemaphoreType.DMA((2, keys.shape[1], 2))],
        compiler_params=pltpu.CompilerParams(vmem_limit_bytes=1 << 20),
        cost_estimate=pl.CostEstimate(
            flops=0, bytes_accessed=2 * keys.size, transcendentals=0
        ),
    )(token, where, placed_in(keys, pltpu.HBM), placed_in(values, pltpu.HBM))


def fetch_pairs_kernel(first, token_ref, source, target, sems):
    blocks, depth = target.shape[:2]
    size = depth // 4
    copies = []
    for block in range(blocks):
        for piece in range(4):
            span = pl.ds(piece * size, size)
            copies.append(
                pltpu.make_async_copy(
                    source.at[span, :, pl.ds((first + block) * 128, 128)],
                    target.at[block, span],
                    sems.at[block, piece],
                )
            )
    run_copies(copies)


def fetch_pairs(token, weights, first, blocks):
    depth = weights.shape[0]
    out = pl.pallas_call(
        functools.partial(fetch_pairs_kernel, first),
        out_shape=pltpu.VMEM((blocks, depth, 2, 128), weights.dtype),
        in_specs=[hbm(), hbm()],
        out_specs=vmem(),
        scratch_shapes=[pltpu.SemaphoreType.DMA((blocks, 4))],
        compiler_params=pltpu.CompilerParams(vmem_limit_bytes=1 << 20),
        cost_estimate=pl.CostEstimate(
            flops=0, bytes_accessed=4 * blocks * depth * 128, transcendentals=0
        ),
    )(token, placed_in(weights, pltpu.HBM))
    return out.reshape(blocks, 2 * depth, 128)


def inverse_rms(x_refs):
    half, rows, chunk = x_refs[0].shape
    total = jnp.zeros((rows, 1), jnp.float32)
    for x_ref in x_refs:

        def add(k, total):
            wide = x_ref[k].astype(jnp.float32)
            return total + jnp.sum(wide * wide, axis=-1, keepdims=True)

        total = lax.fori_loop(0, half, add, total)
    return lax.rsqrt(total / (2 * half * chunk) + epsilon)


def span_of(ids_ref, k, chunk):
    return pl.ds(pl.multiple_of(ids_ref[k] * chunk, chunk), chunk)


def normed_chunk(x_ref, gain_ref, scale, k, span):
    wide = x_ref[k].astype(jnp.float32)
    return (wide * scale * gain_ref[:, span]).astype(jnp.bfloat16)


def project_kernel(ids_ref, own_ref, other_ref, gain_ref, wq_ref, wk_ref, wv_ref, out_ref,
                   q_sum, kv_sum):
    half, rows, chunk = own_ref.shape
    queries = wq_ref.shape[1]
    keys = wk_ref.shape[0]
    count, rows_dev, _ = out_ref.shape
    scale = inverse_rms((own_ref, other_ref))
    q_sum[...] = jnp.zeros_like(q_sum)
    kv_sum[...] = jnp.zeros_like(kv_sum)
    for first, x_ref in ((0, own_ref), (half, other_ref)):

        @pl.loop(0, half // UNROLL)
        def _(group):
            q_part = 0.0
            parts = [0.0, 0.0]
            for step in range(UNROLL):
                k = group * UNROLL + step
                span = span_of(ids_ref, first + k, chunk)
                normed = normed_chunk(x_ref, gain_ref, scale, k, span)
                q_part += jnp.dot(normed, wq_ref[span, :], preferred_element_type=jnp.float32)
                for which, w_ref in enumerate((wk_ref, wv_ref)):
                    parts[which] += lax.dot_general(
                        normed,
                        w_ref[:, span],
                        (((1,), (1,)), ((), ())),
                        preferred_element_type=jnp.float32,
                    )
            q_sum[...] += q_part
            kv_sum[...] += jnp.concatenate(parts, axis=1)

    for owner in range(count):
        lines = slice(owner * rows_dev, (owner + 1) * rows_dev)
        out_ref[owner, :, :queries] = q_sum[lines, :].astype(jnp.bfloat16)
        out_ref[owner, :, queries:] = kv_sum[lines, :].astype(jnp.bfloat16)


def project(ids, own, other, gain, wq, wk, wv):
    half, rows, _ = own.shape
    queries, keys = wq.shape[1], wk.shape[0]
    size = queries + 2 * keys
    return pl.pallas_call(
        project_kernel,
        out_shape=pltpu.VMEM((2 * half, rows // (2 * half), size), jnp.bfloat16),
        in_specs=[smem()] + [vmem()] * 6,
        out_specs=vmem(),
        scratch_shapes=[
            pltpu.VMEM((rows, queries), jnp.float32),
            pltpu.VMEM((rows, 2 * keys), jnp.float32),
        ],
        compiler_params=pltpu.CompilerParams(vmem_limit_bytes=4 << 20),
        cost_estimate=pl.CostEstimate(
            flops=2 * rows * wq.shape[0] * size,
            bytes_accessed=2 * wq.shape[0] * size,
            transcendentals=0,
        ),
    )(ids, own, other, gain, *[placed_in(w, pltpu.VMEM) for w in (wq, wk, wv)])


def attend_kernel(where_ref, length_ref, q_ref, kv_ref, cos_ref, sin_ref, key_buf,
                  value_buf, out_ref, wide_q):
    rows, devices, queries = q_ref.shape
    _, _, groups, size = kv_ref.shape
    slots = queries // size
    heads = devices * slots
    places = key_buf.shape[1]
    batch = where_ref[0]

    line = lax.broadcasted_iota(jnp.int32, (devices, 1), 0)
    group_of = line * groups // devices
    for row in range(rows):
        cosine = cos_ref[pl.ds(row, 1), :]
        sine = sin_ref[pl.ds(row, 1), :]

        def turned(features):
            wide = features.astype(jnp.float32)
            other = jnp.concatenate([wide[:, size // 2 :], wide[:, : size // 2]], axis=1)
            return (wide * cosine + other * sine).astype(jnp.bfloat16).astype(jnp.float32)

        own_key = turned(kv_ref[row, 0])
        own_value = kv_ref[row, 1].astype(jnp.float32)
        key_lines = jnp.zeros((devices, size), jnp.float32)
        value_lines = jnp.zeros((devices, size), jnp.float32)
        for group in range(groups):
            here = group_of == group
            key_lines = jnp.where(here, own_key[group : group + 1], key_lines)
            value_lines = jnp.where(here, own_value[group : group + 1], value_lines)
        own_parts = []
        for slot in range(slots):
            part = turned(q_ref[row, :, slot * size : (slot + 1) * size])
            own_parts.append(jnp.sum(part * key_lines, axis=1, keepdims=True))
            for group in range(groups):
                wide_q[
                    slot * devices : (slot + 1) * devices, group * size : (group + 1) * size
                ] = jnp.where(group_of == group, part, 0.0).astype(jnp.bfloat16)
        own_score = jnp.concatenate(own_parts, axis=0) * (size ** -0.5)
        scores = lax.dot_general(
            wide_q[...], key_buf[row], (((1,), (1,)), ((), ())), preferred_element_type=jnp.float32
        ) * (size ** -0.5)
        spot = lax.broadcasted_iota(jnp.int32, (heads, places), 1)
        scores = jnp.where(spot < length_ref[batch, row], scores, -1e30)
        highest = jnp.maximum(jnp.max(scores, axis=1, keepdims=True), own_score)
        raised = jnp.exp(scores - highest)
        own_raised = jnp.exp(own_score - highest)
        denominator = jnp.sum(raised, axis=1, keepdims=True) + own_raised
        weights = (raised / denominator).astype(jnp.bfloat16)
        own_weight = (own_raised / denominator).astype(jnp.bfloat16).astype(jnp.float32)
        mixed = jnp.dot(weights, value_buf[row], preferred_element_type=jnp.float32)
        for slot in range(slots):
            lines = slice(slot * devices, (slot + 1) * devices)
            picked = own_weight[lines] * value_lines
            for group in range(groups):
                picked = picked + jnp.where(
                    group_of == group, mixed[lines, group * size : (group + 1) * size], 0.0
                )
            out_ref[row, :, slot * size : (slot + 1) * size] = picked.astype(jnp.bfloat16)


def attend(where, lengths, query, fresh, cosine, sine, keys, values):
    rows, devices, queries = query.shape
    places, width = keys.shape[1:]
    heads = devices * queries // HEAD_SIZE
    return pl.pallas_call(
        attend_kernel,
        out_shape=pltpu.VMEM(query.shape, jnp.bfloat16),
        in_specs=[smem(), smem()] + [vmem()] * 6,
        out_specs=vmem(),
        scratch_shapes=[pltpu.VMEM((heads, width), jnp.bfloat16)],
        compiler_params=pltpu.CompilerParams(vmem_limit_bytes=4 << 20),
        cost_estimate=pl.CostEstimate(
            flops=4 * rows * heads * places * width,
            bytes_accessed=4 * rows * places * width,
            transcendentals=rows * heads * places,
        ),
    )(
        where,
        lengths,
        query,
        fresh,
        cosine,
        sine,
        placed_in(keys, pltpu.VMEM),
        placed_in(values, pltpu.VMEM),
    )


def spread_kernel(ids_ref, x_ref, w_ref, keep_ref, send_ref, values):
    half, rows, chunk = keep_ref.shape
    count, rows_dev, _ = x_ref.shape
    for owner in range(count):
        values[owner * rows_dev : (owner + 1) * rows_dev, :] = x_ref[owner].astype(jnp.float32)
    ready = values[...].astype(jnp.bfloat16)
    for first, target in ((0, keep_ref), (half, send_ref)):

        @pl.loop(0, half // UNROLL)
        def _(group):
            for step in range(UNROLL):
                k = group * UNROLL + step
                span = span_of(ids_ref, first + k, chunk)
                target[k] = jnp.dot(
                    ready, w_ref[:, span], preferred_element_type=jnp.float32
                ).astype(jnp.bfloat16)


def spread_project(ids, values, weights):
    count, rows_dev, depth = values.shape
    rows = count * rows_dev
    width = weights.shape[1]
    shape = pltpu.VMEM((count // 2, rows, width // count), jnp.bfloat16)
    return pl.pallas_call(
        spread_kernel,
        out_shape=(shape, shape),
        in_specs=[smem(), vmem(), vmem()],
        out_specs=(vmem(), vmem()),
        scratch_shapes=[pltpu.VMEM((rows, depth), jnp.float32)],
        compiler_params=pltpu.CompilerParams(vmem_limit_bytes=4 << 20),
        cost_estimate=pl.CostEstimate(
            flops=2 * rows * depth * width, bytes_accessed=2 * depth * width, transcendentals=0
        ),
    )(ids, values, placed_in(weights, pltpu.VMEM))


def mlp_kernel(by_rows, ids_ref, own_ref, other_ref, gain_ref, low_ref, high_ref, down_ref,
               keep_ref, send_ref, stacked, wide_x, total, act):
    half, rows, chunk = own_ref.shape
    blocks = [ref.at[j] for ref in (low_ref, high_ref) for j in range(ref.shape[0])]
    per_chunk = chunk // 128

    scale = inverse_rms((own_ref, other_ref))
    for first, x_ref in ((0, own_ref), (half, other_ref)):

        @pl.loop(0, half)
        def _(place):
            k = first + place
            normed = normed_chunk(x_ref, gain_ref, scale, place, span_of(ids_ref, k, chunk))
            for b in range(per_chunk):
                stacked[k * per_chunk + b] = normed[:, b * 128 : (b + 1) * 128]

    line = lax.broadcasted_iota(jnp.int32, (128, 512), 0)
    column = lax.broadcasted_iota(jnp.int32, (128, 512), 1)
    aim = jnp.where(column < 256, 2 * line, 2 * line + 257)
    widen = jnp.where(column == aim, 1.0, 0.0).astype(jnp.bfloat16)

    @pl.loop(0, 2 * half * per_chunk // 8)
    def _(group):
        span = pl.ds(group * 8, 8)
        wide = jnp.dot(
            stacked[span].reshape(8 * rows, 128), widen, preferred_element_type=jnp.float32
        ).astype(jnp.bfloat16)
        for b in range(8):
            lines = slice(b * rows, (b + 1) * rows)
            wide_x[group, :rows, b * 256 : (b + 1) * 256] = wide[lines, :256]
            wide_x[group, rows:, b * 256 : (b + 1) * 256] = wide[lines, 256:]

    total[...] = jnp.zeros_like(total)
    per_group = 8 // per_chunk

    @pl.loop(0, wide_x.shape[0])
    def _(group):
        for j in range(0, len(blocks), 2):
            part = 0.0
            for step in range(per_group):
                at = ids_ref[group * per_group + step] * (2 * chunk)
                span = pl.ds(pl.multiple_of(at, 2 * chunk), 2 * chunk)
                pair = jnp.concatenate([blocks[j][span, :], blocks[j + 1][span, :]], axis=1)
                part += jnp.dot(
                    wide_x[group, :, step * 2 * chunk : (step + 1) * 2 * chunk],
                    pair,
                    preferred_element_type=jnp.float32,
                )
            total[:, j * 128 : (j + 2) * 128] += part

    gate = total[:rows, :]
    act[...] = (gate / (1.0 + jnp.exp(-gate)) * total[rows:, :]).astype(jnp.bfloat16)

    def down(span):
        return jnp.dot(act[...], down_ref[:, span], preferred_element_type=jnp.float32)

    if by_rows:
        rows_dev = keep_ref.shape[1]
        first_core = ids_ref[0] == 0

        @pl.loop(0, 2 * half // 2)
        def _(group):
            for step in range(2):
                span = span_of(ids_ref, group * 2 + step, chunk)
                part = down(span)
                for chip in range(half):
                    at = 2 * chip * rows_dev
                    low = part[at : at + rows_dev]
                    high = part[at + rows_dev : at + 2 * rows_dev]
                    keep_ref[chip, :, span] = jnp.where(first_core, low, high).astype(jnp.bfloat16)
                    send_ref[chip, :, span] = jnp.where(first_core, high, low).astype(jnp.bfloat16)

    else:
        for first, target in ((0, keep_ref), (half, send_ref)):

            @pl.loop(0, half // UNROLL)
            def _(group):
                for step in range(UNROLL):
                    k = group * UNROLL + step
                    target[k] = down(span_of(ids_ref, first + k, chunk)).astype(jnp.bfloat16)


def mlp(ids, own, other, gain, low, high, down, by_rows):
    half, rows, chunk = own.shape
    units, width = down.shape
    part = (half, rows // (2 * half), width) if by_rows else own.shape
    shape = pltpu.VMEM(part, jnp.bfloat16)
    return pl.pallas_call(
        functools.partial(mlp_kernel, by_rows),
        out_shape=(shape, shape),
        in_specs=[smem()] + [vmem()] * 6,
        out_specs=(vmem(), vmem()),
        scratch_shapes=[
            pltpu.VMEM((width // 128, rows, 128), jnp.bfloat16),
            pltpu.VMEM((width // 1024, 2 * rows, 2048), jnp.bfloat16),
            pltpu.VMEM((2 * rows, units), jnp.float32),
            pltpu.VMEM((rows, units), jnp.bfloat16),
        ],
        compiler_params=pltpu.CompilerParams(vmem_limit_bytes=(3 << 20) + 10 * rows * width),
        cost_estimate=pl.CostEstimate(
            flops=6 * rows * units * width, bytes_accessed=6 * units * width, transcendentals=0
        ),
    )(ids, own, other, gain, *[placed_in(w, pltpu.VMEM) for w in (low, high, down)])


def turning(positions):
    half_dim = HEAD_SIZE // 2
    frequency = 500000.0 ** (-2.0 * jnp.arange(half_dim, dtype=jnp.float32) / HEAD_SIZE)
    angles = positions.astype(jnp.float32)[:, None] * frequency[None, :]
    cosine = jnp.cos(angles)
    sine = jnp.sin(angles)
    return jnp.concatenate([cosine, cosine], axis=1), jnp.concatenate([-sine, sine], axis=1)


def body(
    hidden,
    attn_gain,
    w_query,
    w_key,
    w_value,
    w_out,
    mlp_gain,
    w_gate_up,
    w_down,
    key_cache,
    value_cache,
    lengths,
):
    rows_dev = hidden.shape[1]
    count = lax.axis_size("mp")
    half = count // 2
    rows = rows_dev * count
    section_index = lax.axis_index("section")
    model_index = lax.axis_index("mp")
    core = model_index % 2
    query_cols = w_query.shape[2]
    key_cols = w_key.shape[2]
    width = hidden.shape[2]
    chips = 2 * jnp.arange(half, dtype=jnp.int32)
    ids = jnp.concatenate([chips + core, chips + 1 - core])
    wk = w_key[0].T
    wv = w_value[0].T

    def by_core(own, other):
        pair = jnp.where(core == 0, jnp.stack([own, other], 1), jnp.stack([other, own], 1))
        return pair.reshape((count,) + own.shape[1:])

    blocks = w_gate_up.shape[3] // 128
    qkv = fetch(hidden, w_query[0], wk, wv)
    start = by_core(*gather(hidden[0])).reshape(rows, width)
    chunks = columns_to_chunks(start, count)
    mine = lax.dynamic_index_in_dim(chunks, model_index, 0, keepdims=False)
    own, other = chunks[:half], chunks[half:]
    order = jnp.arange(count, dtype=jnp.int32)
    for turn_index in range(2):
        batch = jnp.remainder(section_index + turn_index, 2).astype(jnp.int32).reshape(1)
        cosine, sine = turning(lax.dynamic_index_in_dim(lengths, batch[0], 0, keepdims=False))
        joined = project(order, own, other, attn_gain, *qkv)
        keys, values = fetch_caches(joined, batch, key_cache[0], value_cache[0])
        spread = lax.all_to_all(joined, "mp", split_axis=0, concat_axis=0)
        query = spread[..., :query_cols].transpose(1, 0, 2)
        fresh = (
            spread[..., query_cols:]
            .reshape(count, rows_dev, 2, key_cols)
            .transpose(1, 2, 0, 3)
            .reshape(rows_dev, 2, KEY_VALUE_HEADS, HEAD_SIZE)
        )
        mixed = attend(batch, lengths, query, fresh, cosine, sine, keys, values)
        (out_proj,) = fetch(mixed, w_out[0])
        heads_out = lax.all_to_all(mixed.transpose(1, 0, 2), "mp", split_axis=0, concat_axis=0)
        keep, send = spread_project(ids, heads_out, out_proj)
        held = merge(send, keep)
        low = fetch_pairs(held, w_gate_up[0], 0, blocks // 2)
        middle = (mine.astype(jnp.float32) + scatter(held)).astype(jnp.bfloat16)
        high = fetch_pairs(middle, w_gate_up[0], blocks // 2, blocks // 2)
        (down,) = fetch(middle, w_down[0])
        own, other = gather(middle)
        last = turn_index == 1
        keep, send = mlp(ids, own, other, mlp_gain, low, high, down, last)
        mlp_part = scatter(merge(send, keep))
        if last:
            at = model_index * rows_dev
            mine = by_core(
                lax.dynamic_slice_in_dim(own, at, rows_dev, 1),
                lax.dynamic_slice_in_dim(other, at, rows_dev, 1),
            )
            middle = mine.transpose(1, 0, 2).reshape(rows_dev, width)
        mine = (middle.astype(jnp.float32) + mlp_part).astype(jnp.bfloat16)
        if not last:
            mine = swap(mine, 1, "section")
            qkv = fetch(mine, w_query[0], wk, wv)
            own, other = gather(mine)
            order = ids
    return mine[None]


def solution(mesh):
    placed = (
        P("section", "mp", None),
        P("section", None),
        P("section", None, "mp"),
        P("section", None, "mp"),
        P("section", None, "mp"),
        P("section", "mp", None),
        P("section", None),
        P("section", None, None, "mp"),
        P("section", "mp", None),
        P("section", None, "mp", None, None),
        P("section", None, "mp", None, None),
        P(None, "mp"),
    )
    return jax.shard_map(
        body, mesh=mesh, in_specs=placed, out_specs=P("section", "mp", None), check_vma=False
    )
```

```python
import functools

import jax
import jax.numpy as jnp
import numpy as np
from jax import lax
from jax.experimental import pallas as pl
from jax.experimental.pallas import tpu as pltpu
from jax.sharding import PartitionSpec as P

QUERY_HEADS = 64
KEY_VALUE_HEADS = 8
HEAD_SIZE = 128

epsilon = 1e-05

UNROLL = 4


def swap(value, mask, axis="mp"):
    count = lax.axis_size(axis)
    return lax.ppermute(value, axis, [(source, source ^ mask) for source in range(count)])


def exchange(parts):
    count = lax.axis_size("mp")
    groups = [list(range(core, count, 2)) for core in range(2)]
    return lax.all_to_all(
        parts, "mp", split_axis=0, concat_axis=0, axis_index_groups=groups, tiled=True
    )


def chip_masks():
    return [1 << bit for bit in range(1, (lax.axis_size("mp") - 1).bit_length())]


def relative_ids():
    ids = np.zeros((1,), np.int32)
    for mask in reversed(chip_masks()):
        ids = np.concatenate([ids, ids ^ mask])
    return ids


def vmem():
    return pl.BlockSpec(memory_space=pltpu.VMEM)


def smem():
    return pl.BlockSpec(memory_space=pltpu.SMEM)


def placed_in(values, space):
    return pltpu.with_memory_space_constraint(values, space)


def hbm():
    return pl.BlockSpec(memory_space=pl.ANY)


def run_copies(copies):
    for at, copy in enumerate(copies):
        copy.start(priority=at % 2)
    for copy in copies:
        copy.wait()


def fetch_kernel(pieces, token_ref, *refs):
    arrays = len(pieces)
    sems = refs[-1]
    copies = []
    for array, (count, source, target) in enumerate(zip(pieces, refs, refs[arrays:])):
        size = source.shape[0] // count
        for piece in range(count):
            span = pl.ds(piece * size, size)
            copies.append(
                pltpu.make_async_copy(source.at[span], target.at[span], sems.at[array, piece])
            )
    run_copies(copies)


def fetch(token, *arrays):
    pieces = [8 if array.shape[0] % 128 == 0 else 1 for array in arrays]
    return pl.pallas_call(
        functools.partial(fetch_kernel, pieces),
        out_shape=[pltpu.VMEM(array.shape, array.dtype) for array in arrays],
        in_specs=[hbm()] * (1 + len(arrays)),
        out_specs=[vmem()] * len(arrays),
        scratch_shapes=[pltpu.SemaphoreType.DMA((len(arrays), 8))],
        compiler_params=pltpu.CompilerParams(vmem_limit_bytes=1 << 20),
        cost_estimate=pl.CostEstimate(
            flops=0, bytes_accessed=sum(2 * array.size for array in arrays), transcendentals=0
        ),
    )(token, *[placed_in(array, pltpu.HBM) for array in arrays])


def fetch_caches_kernel(token_ref, where_ref, keys_ref, values_ref, key_ref, value_ref, sems):
    rows, places, _ = key_ref.shape
    batch = where_ref[0]
    copies = []
    for array, (source, target) in enumerate(((keys_ref, key_ref), (values_ref, value_ref))):
        for row in range(rows):
            for piece in range(2):
                span = pl.ds(piece * (places // 2), places // 2)
                copies.append(
                    pltpu.make_async_copy(
                        source.at[batch, row, span],
                        target.at[row, span],
                        sems.at[array, row, piece],
                    )
                )
    run_copies(copies)


def fetch_caches(token, where, keys, values):
    shape = pltpu.VMEM(keys.shape[1:], keys.dtype)
    return pl.pallas_call(
        fetch_caches_kernel,
        out_shape=[shape, shape],
        in_specs=[hbm(), smem(), hbm(), hbm()],
        out_specs=[vmem(), vmem()],
        scratch_shapes=[pltpu.SemaphoreType.DMA((2, keys.shape[1], 2))],
        compiler_params=pltpu.CompilerParams(vmem_limit_bytes=1 << 20),
        cost_estimate=pl.CostEstimate(
            flops=0, bytes_accessed=2 * keys.size, transcendentals=0
        ),
    )(token, where, placed_in(keys, pltpu.HBM), placed_in(values, pltpu.HBM))


def fetch_pairs_kernel(first, token_ref, source, *refs):
    targets, sems = refs[:-1], refs[-1]
    size = source.shape[0] // 4
    copies = []
    for block, target in enumerate(targets):
        for piece in range(4):
            span = pl.ds(piece * size, size)
            copies.append(
                pltpu.make_async_copy(
                    source.at[span, :, pl.ds((first + block) * 128, 128)],
                    target.at[span],
                    sems.at[block, piece],
                )
            )
    run_copies(copies)


def fetch_pairs(token, weights, first, blocks):
    depth = weights.shape[0]
    return pl.pallas_call(
        functools.partial(fetch_pairs_kernel, first),
        out_shape=[pltpu.VMEM((depth, 2, 128), weights.dtype)] * blocks,
        in_specs=[hbm(), hbm()],
        out_specs=[vmem()] * blocks,
        scratch_shapes=[pltpu.SemaphoreType.DMA((blocks, 4))],
        compiler_params=pltpu.CompilerParams(vmem_limit_bytes=1 << 20),
        cost_estimate=pl.CostEstimate(
            flops=0, bytes_accessed=4 * blocks * depth * 128, transcendentals=0
        ),
    )(token, placed_in(weights, pltpu.HBM))


def step_call(kernel, shapes, operands, held_back):
    return pl.pallas_call(
        kernel,
        out_shape=[pltpu.VMEM(shape, jnp.bfloat16) for shape in shapes],
        in_specs=[vmem()] * len(operands) + [hbm()] * len(held_back),
        out_specs=[vmem()] * len(shapes),
        compiler_params=pltpu.CompilerParams(vmem_limit_bytes=4 << 20),
        cost_estimate=pl.CostEstimate(
            flops=2 * operands[0].size, bytes_accessed=6 * operands[0].size, transcendentals=0
        ),
    )(*operands, *[placed_in(array, pltpu.VMEM) for array in held_back])


def add_kernel(outs, operands, *refs):
    targets = refs[-outs:]
    share = targets[0].shape[0]
    for which, target in enumerate(targets):
        for place in range(share):
            total = 0.0
            for ref in refs[:operands]:
                total += ref[which * share + place].astype(jnp.float32)
            target[place] = total.astype(jnp.bfloat16)


def add_parts(operands, outs, held_back=()):
    lead = operands[0].shape[0]
    shape = (lead // outs,) + operands[0].shape[1:]
    return step_call(
        functools.partial(add_kernel, outs, len(operands)), [shape] * outs, operands, held_back
    )


def finish_kernel(own_ref, keep_ref, got_ref, *refs):
    total = keep_ref[0].astype(jnp.float32) + got_ref[0].astype(jnp.float32)
    if len(own_ref.shape) == 2:
        total += own_ref[...].astype(jnp.float32)
    else:
        parts = [own_ref[owner].astype(jnp.float32) for owner in range(own_ref.shape[0])]
        total += jnp.concatenate(parts, axis=0)
    refs[-1][...] = total.astype(jnp.bfloat16)


def join_kernel(low_ref, high_ref, *refs):
    half = low_ref.shape[0]
    out_ref = refs[-1]
    for place in range(half):
        out_ref[place] = low_ref[place]
        out_ref[half + place] = high_ref[place]


def join(low, high, held_back=()):
    shape = (2 * low.shape[0],) + low.shape[1:]
    return step_call(join_kernel, [shape], (low, high), held_back)[0]


def run_job(jobs, token):
    return jobs.pop(0)(token) if jobs else ()


def scatter(send, keep):
    (held,) = add_parts((keep, swap(send, 1)), 1)
    return jnp.sum(exchange(held).astype(jnp.float32), axis=0)


def scatter_halving(send, keep, own, jobs):
    got = swap(send, 1)
    held_back = ()
    for mask in chip_masks():
        keep, send = add_parts((keep, got), 2, held_back)
        got = swap(send, mask)
        held_back = run_job(jobs, send)
    return step_call(finish_kernel, [keep.shape[1:]], (own, keep, got), held_back)[0]


def gather_doubling(part, jobs):
    held = part[None]
    for mask in reversed(chip_masks()):
        got = swap(held, mask)
        held = join(held, got, run_job(jobs, held))
    return held, swap(held, 1)


def inverse_rms(x_refs):
    half, rows, chunk = x_refs[0].shape
    total = jnp.zeros((rows, chunk), jnp.float32)
    for x_ref in x_refs:

        def add(group, total):
            for step in range(UNROLL):
                wide = x_ref[group * UNROLL + step].astype(jnp.float32)
                total = total + wide * wide
            return total

        total = lax.fori_loop(0, half // UNROLL, add, total)
    return lax.rsqrt(jnp.sum(total, axis=-1, keepdims=True) / (2 * half * chunk) + epsilon)


def span_of(ids_ref, k, chunk):
    return pl.ds(pl.multiple_of(ids_ref[k] * chunk, chunk), chunk)


def normed_chunk(x_ref, gain_ref, scale, k, span):
    wide = x_ref[k].astype(jnp.float32)
    return (wide * scale * gain_ref[:, span]).astype(jnp.bfloat16)


def project_kernel(ids_ref, own_ref, other_ref, gain_ref, wq_ref, wk_ref, wv_ref, out_ref,
                   mine_ref, q_sum, kv_sum, wide):
    queries = wq_ref.shape[1]
    count, rows_dev, _ = out_ref.shape
    half = count // 2
    by_rows = own_ref.shape[1] == rows_dev
    chunk = wq_ref.shape[0] // count
    if by_rows:
        for first, x_ref in ((0, own_ref), (half, other_ref)):
            for place in range(half):
                at = (first + place) * rows_dev
                wide[at : at + rows_dev, :] = x_ref[place].astype(jnp.float32)
        total = 0.0
        for k in range(count):
            part = wide[:, k * chunk : (k + 1) * chunk]
            total += part * part
        mean = jnp.sum(total, axis=-1, keepdims=True) / (count * chunk)
        scale = lax.rsqrt(mean + epsilon)
    else:
        scale = inverse_rms((own_ref, other_ref))
    q_sum[...] = jnp.zeros_like(q_sum)
    kv_sum[...] = jnp.zeros_like(kv_sum)
    for first, x_ref in ((0, own_ref), (half, other_ref)):

        @pl.loop(0, half // UNROLL)
        def _(group):
            q_part = 0.0
            kv_part = 0.0
            for step in range(UNROLL):
                k = group * UNROLL + step
                if by_rows:
                    span = pl.ds(pl.multiple_of((first + k) * chunk, chunk), chunk)
                    normed = (wide[:, span] * scale * gain_ref[:, span]).astype(jnp.bfloat16)
                else:
                    span = span_of(ids_ref, first + k, chunk)
                    normed = normed_chunk(x_ref, gain_ref, scale, k, span)
                q_part += jnp.dot(normed, wq_ref[span, :], preferred_element_type=jnp.float32)
                kv_part += lax.dot_general(
                    normed,
                    jnp.concatenate([wk_ref[:, span], wv_ref[:, span]], axis=0),
                    (((1,), (1,)), ((), ())),
                    preferred_element_type=jnp.float32,
                )
            q_sum[...] += q_part
            kv_sum[...] += kv_part

    for place in range(count):
        owner = ids_ref[place] if by_rows else place
        lines = slice(place * rows_dev, (place + 1) * rows_dev)
        out_ref[owner, :, :queries] = q_sum[lines, :].astype(jnp.bfloat16)
        out_ref[owner, :, queries:] = kv_sum[lines, :].astype(jnp.bfloat16)
        if by_rows:
            span = span_of(ids_ref, 0, chunk)
            mine_ref[owner] = wide[lines, span].astype(jnp.bfloat16)


def project(ids, own, other, gain, wq, wk, wv):
    count = ids.shape[0]
    width, queries = wq.shape
    keys = wk.shape[0]
    size = queries + 2 * keys
    rows_dev = 2 * own.size // (count * width)
    rows = count * rows_dev
    by_rows = own.shape[1] == rows_dev
    return pl.pallas_call(
        project_kernel,
        out_shape=[
            pltpu.VMEM((count, rows_dev, size), jnp.bfloat16),
            pltpu.VMEM((count, rows_dev, width // count), jnp.bfloat16),
        ],
        in_specs=[smem()] + [vmem()] * 6,
        out_specs=[vmem(), vmem()],
        scratch_shapes=[
            pltpu.VMEM((rows, queries), jnp.float32),
            pltpu.VMEM((rows, 2 * keys), jnp.float32),
            pltpu.VMEM((rows, width if by_rows else 128), jnp.float32),
        ],
        compiler_params=pltpu.CompilerParams(vmem_limit_bytes=(3 << 20) + 4 * rows * width),
        cost_estimate=pl.CostEstimate(
            flops=2 * rows * width * size, bytes_accessed=2 * width * size, transcendentals=0
        ),
    )(ids, own, other, gain, *[placed_in(w, pltpu.VMEM) for w in (wq, wk, wv)])


def attend_kernel(where_ref, length_ref, in_ref, cos_ref, sin_ref, key_buf, value_buf, out_ref,
                  lined, wide_q):
    rows, devices, queries = out_ref.shape
    width = key_buf.shape[2]
    keys = (in_ref.shape[2] - queries) // 2
    size = cos_ref.shape[1]
    groups = width // size
    pieces = size // keys
    slots = queries // size
    heads = devices * slots
    places = key_buf.shape[1]
    batch = where_ref[0]

    for device in range(devices):
        wide = in_ref[device].astype(jnp.float32)
        for row in range(rows):
            lined[row, device : device + 1, :] = wide[row : row + 1]
    line = lax.broadcasted_iota(jnp.int32, (devices, 1), 0)
    group_of = line * groups // devices
    for row in range(rows):
        cosine = cos_ref[pl.ds(row, 1), :]
        sine = sin_ref[pl.ds(row, 1), :]

        def turned(wide):
            other = jnp.concatenate([wide[:, size // 2 :], wide[:, : size // 2]], axis=1)
            return (wide * cosine + other * sine).astype(jnp.bfloat16).astype(jnp.float32)

        key_lines = jnp.zeros((devices, size), jnp.float32)
        value_lines = jnp.zeros((devices, size), jnp.float32)
        for group in range(groups):
            own_key, own_value = (
                jnp.concatenate(
                    [
                        lined[row, device : device + 1, at : at + keys]
                        for device in range(group * pieces, (group + 1) * pieces)
                    ],
                    axis=1,
                )
                for at in (queries, queries + keys)
            )
            here = group_of == group
            key_lines = jnp.where(here, turned(own_key), key_lines)
            value_lines = jnp.where(here, own_value, value_lines)
        own_parts = []
        for slot in range(slots):
            part = turned(lined[row, :, slot * size : (slot + 1) * size])
            own_parts.append(jnp.sum(part * key_lines, axis=1, keepdims=True))
            for group in range(groups):
                wide_q[
                    slot * devices : (slot + 1) * devices, group * size : (group + 1) * size
                ] = jnp.where(group_of == group, part, 0.0).astype(jnp.bfloat16)
        own_score = jnp.concatenate(own_parts, axis=0) * (size ** -0.5)
        scores = lax.dot_general(
            wide_q[...], key_buf[row], (((1,), (1,)), ((), ())), preferred_element_type=jnp.float32
        ) * (size ** -0.5)
        spot = lax.broadcasted_iota(jnp.int32, (heads, places), 1)
        scores = jnp.where(spot < length_ref[batch, row], scores, -1e30)
        highest = jnp.maximum(jnp.max(scores, axis=1, keepdims=True), own_score)
        raised = jnp.exp(scores - highest)
        own_raised = jnp.exp(own_score - highest)
        denominator = jnp.sum(raised, axis=1, keepdims=True) + own_raised
        weights = (raised / denominator).astype(jnp.bfloat16)
        own_weight = (own_raised / denominator).astype(jnp.bfloat16).astype(jnp.float32)
        mixed = jnp.dot(weights, value_buf[row], preferred_element_type=jnp.float32)
        for slot in range(slots):
            lines = slice(slot * devices, (slot + 1) * devices)
            picked = own_weight[lines] * value_lines
            for group in range(groups):
                picked = picked + jnp.where(
                    group_of == group, mixed[lines, group * size : (group + 1) * size], 0.0
                )
            out_ref[row, :, slot * size : (slot + 1) * size] = picked.astype(jnp.bfloat16)


def attend(where, lengths, spread, cosine, sine, keys, values, queries):
    devices, rows, length = spread.shape
    places, width = keys.shape[1:]
    heads = devices * queries // HEAD_SIZE
    return pl.pallas_call(
        attend_kernel,
        out_shape=pltpu.VMEM((rows, devices, queries), jnp.bfloat16),
        in_specs=[smem(), smem()] + [vmem()] * 5,
        out_specs=vmem(),
        scratch_shapes=[
            pltpu.VMEM((rows, devices, length), jnp.float32),
            pltpu.VMEM((heads, width), jnp.bfloat16),
        ],
        compiler_params=pltpu.CompilerParams(vmem_limit_bytes=4 << 20),
        cost_estimate=pl.CostEstimate(
            flops=4 * rows * heads * places * width,
            bytes_accessed=4 * rows * places * width,
            transcendentals=rows * heads * places,
        ),
    )(
        where,
        lengths,
        spread,
        cosine,
        sine,
        placed_in(keys, pltpu.VMEM),
        placed_in(values, pltpu.VMEM),
    )


def spread_kernel(ids_ref, x_ref, w_ref, keep_ref, send_ref, values):
    half, rows, chunk = keep_ref.shape
    count, rows_dev, _ = x_ref.shape
    for owner in range(count):
        values[owner * rows_dev : (owner + 1) * rows_dev, :] = x_ref[owner].astype(jnp.float32)
    ready = values[...].astype(jnp.bfloat16)
    for first, target in ((0, keep_ref), (half, send_ref)):

        @pl.loop(0, half // UNROLL)
        def _(group):
            for step in range(UNROLL):
                k = group * UNROLL + step
                span = span_of(ids_ref, first + k, chunk)
                target[k] = jnp.dot(
                    ready, w_ref[:, span], preferred_element_type=jnp.float32
                ).astype(jnp.bfloat16)


def spread_project(ids, values, weights):
    count, rows_dev, depth = values.shape
    rows = count * rows_dev
    width = weights.shape[1]
    shape = pltpu.VMEM((count // 2, rows, width // count), jnp.bfloat16)
    return pl.pallas_call(
        spread_kernel,
        out_shape=(shape, shape),
        in_specs=[smem(), vmem(), vmem()],
        out_specs=(vmem(), vmem()),
        scratch_shapes=[pltpu.VMEM((rows, depth), jnp.float32)],
        compiler_params=pltpu.CompilerParams(vmem_limit_bytes=4 << 20),
        cost_estimate=pl.CostEstimate(
            flops=2 * rows * depth * width, bytes_accessed=2 * depth * width, transcendentals=0
        ),
    )(ids, values, placed_in(weights, pltpu.VMEM))


def mlp_kernel(by_rows, ids_ref, out_ids_ref, own_ref, other_ref, gain_ref, down_hbm, *refs):
    pairs, (keep_ref, send_ref, middle_ref), (stacked, wide_x, total, act, down_ref, sems) = (
        refs[:-9],
        refs[-9:-6],
        refs[-6:],
    )
    half, rows, chunk = own_ref.shape
    blocks = pairs
    per_chunk = chunk // 128

    def down_copy(k):
        return pltpu.make_async_copy(
            down_hbm.at[:, span_of(out_ids_ref, k, chunk)], down_ref.at[lax.rem(k, half)], sems.at[k]
        )

    @pl.loop(0, half)
    def _(k):
        down_copy(k).start()

    scale = inverse_rms((own_ref, other_ref))
    for first, x_ref in ((0, own_ref), (half, other_ref)):

        @pl.loop(0, half)
        def _(place):
            k = first + place
            normed = normed_chunk(x_ref, gain_ref, scale, place, span_of(ids_ref, k, chunk))
            for b in range(per_chunk):
                stacked[k * per_chunk + b] = normed[:, b * 128 : (b + 1) * 128]

    if by_rows:
        rows_dev = middle_ref.shape[0]
        line = lax.broadcasted_iota(jnp.int32, (rows, 1), 0)
        for first, x_ref in ((0, own_ref), (half, other_ref)):

            @pl.loop(0, half)
            def _(place):
                wide = x_ref[place].astype(jnp.float32)
                span = span_of(ids_ref, first + place, chunk)
                for row in range(rows_dev):
                    here = line == ids_ref[0] * rows_dev + row
                    middle_ref[row : row + 1, span] = jnp.sum(
                        jnp.where(here, wide, 0.0), axis=0, keepdims=True
                    )

    line = lax.broadcasted_iota(jnp.int32, (128, 512), 0)
    column = lax.broadcasted_iota(jnp.int32, (128, 512), 1)
    aim = jnp.where(column < 256, 2 * line, 2 * line + 257)
    widen = jnp.where(column == aim, 1.0, 0.0).astype(jnp.bfloat16)

    @pl.loop(0, 2 * half * per_chunk // 8)
    def _(group):
        span = pl.ds(group * 8, 8)
        wide = jnp.dot(
            stacked[span].reshape(8 * rows, 128), widen, preferred_element_type=jnp.float32
        ).astype(jnp.bfloat16)
        for b in range(8):
            lines = slice(b * rows, (b + 1) * rows)
            wide_x[group, :rows, b * 256 : (b + 1) * 256] = wide[lines, :256]
            wide_x[group, rows:, b * 256 : (b + 1) * 256] = wide[lines, 256:]

    total[...] = jnp.zeros_like(total)
    per_group = 8 // per_chunk

    @pl.loop(0, wide_x.shape[0])
    def _(group):
        for j in range(0, len(blocks), 2):
            part = 0.0
            for step in range(per_group):
                at = ids_ref[group * per_group + step] * (2 * chunk)
                span = pl.ds(pl.multiple_of(at, 2 * chunk), 2 * chunk)
                pair = jnp.concatenate([blocks[j][span, :], blocks[j + 1][span, :]], axis=1)
                part += jnp.dot(
                    wide_x[group, :, step * 2 * chunk : (step + 1) * 2 * chunk],
                    pair,
                    preferred_element_type=jnp.float32,
                )
            total[:, j * 128 : (j + 2) * 128] += part

    gate = total[:rows, :]
    act[...] = (gate / (1.0 + jnp.exp(-gate)) * total[rows:, :]).astype(jnp.bfloat16)

    def down(first, k):
        down_copy(first + k).wait()
        return jnp.dot(act[...], down_ref[k], preferred_element_type=jnp.float32)

    for first, target in ((0, keep_ref), (half, send_ref)):

        @pl.loop(0, half // UNROLL)
        def _(group):
            for step in range(UNROLL):
                k = group * UNROLL + step
                part = down(first, k)
                if not by_rows:
                    target[k] = part.astype(jnp.bfloat16)
                    continue
                span = span_of(out_ids_ref, first + k, chunk)
                first_core = out_ids_ref[0] == 0
                for chip in range(half):
                    at = 2 * chip * rows_dev
                    low = part[at : at + rows_dev]
                    high = part[at + rows_dev : at + 2 * rows_dev]
                    keep_ref[chip, :, span] = jnp.where(first_core, low, high).astype(jnp.bfloat16)
                    send_ref[chip, :, span] = jnp.where(first_core, high, low).astype(jnp.bfloat16)
            if first == 0:
                for step in range(UNROLL):
                    down_copy(half + group * UNROLL + step).start()


def mlp(ids, out_ids, own, other, gain, pairs, down, by_rows):
    half, rows, chunk = own.shape
    units, width = down.shape
    part = (half, rows // (2 * half), width) if by_rows else own.shape
    shape = pltpu.VMEM(part, jnp.bfloat16)
    return pl.pallas_call(
        functools.partial(mlp_kernel, by_rows),
        out_shape=(shape, shape, pltpu.VMEM((rows // (2 * half), width), jnp.float32)),
        in_specs=[smem(), smem()] + [vmem()] * 3 + [hbm()] + [vmem()] * len(pairs),
        out_specs=(vmem(), vmem(), vmem()),
        scratch_shapes=[
            pltpu.VMEM((width // 128, rows, 128), jnp.bfloat16),
            pltpu.VMEM((width // 1024, 2 * rows, 2048), jnp.bfloat16),
            pltpu.VMEM((2 * rows, units), jnp.float32),
            pltpu.VMEM((rows, units), jnp.bfloat16),
            pltpu.VMEM((half, units, chunk), jnp.bfloat16),
            pltpu.SemaphoreType.DMA((2 * half,)),
        ],
        compiler_params=pltpu.CompilerParams(
            vmem_limit_bytes=(3 << 19) + 10 * rows * width + (10 * rows + width) * units
        ),
        cost_estimate=pl.CostEstimate(
            flops=6 * rows * units * width, bytes_accessed=6 * units * width, transcendentals=0
        ),
    )(
        ids,
        out_ids,
        own,
        other,
        gain,
        placed_in(down, pltpu.HBM),
        *[placed_in(pair.reshape(2 * width, 128), pltpu.VMEM) for pair in pairs],
    )


def turning(positions):
    half_dim = HEAD_SIZE // 2
    frequency = 500000.0 ** (-2.0 * jnp.arange(half_dim, dtype=jnp.float32) / HEAD_SIZE)
    angles = positions.astype(jnp.float32)[:, None] * frequency[None, :]
    cosine = jnp.cos(angles)
    sine = jnp.sin(angles)
    return jnp.concatenate([cosine, cosine], axis=1), jnp.concatenate([-sine, sine], axis=1)


def body(
    hidden,
    attn_gain,
    w_query,
    w_key,
    w_value,
    w_out,
    mlp_gain,
    w_gate_up,
    w_down,
    key_cache,
    value_cache,
    lengths,
):
    rows_dev = hidden.shape[1]
    count = lax.axis_size("mp")
    half = count // 2
    section_index = lax.axis_index("section")
    model_index = lax.axis_index("mp")
    core = model_index % 2
    width = hidden.shape[2]
    chips = 2 * jnp.arange(half, dtype=jnp.int32)
    ids = jnp.concatenate([chips + core, chips + 1 - core])
    near = jnp.asarray(relative_ids())
    places = jnp.concatenate([near ^ model_index, near ^ model_index ^ 1])
    wk = w_key[0].T
    wv = w_value[0].T
    blocks = w_gate_up.shape[3] // 128
    share = max(blocks // 4, 1)
    batches = [
        jnp.remainder(section_index + turn_index, 2).astype(jnp.int32).reshape(1)
        for turn_index in range(2)
    ]

    def attention_jobs(turn_index):
        got = {}

        def projections(token):
            got["qkv"] = fetch(token, w_query[0], wk, wv)
            return got["qkv"]

        def out_projection(token):
            got["out"] = fetch(token, w_out[0])
            return got["out"]

        def caches(token):
            got["caches"] = fetch_caches(token, batches[turn_index], key_cache[0], value_cache[0])
            return got["caches"]

        return got, [projections, out_projection, caches]

    got, jobs = attention_jobs(0)
    own, other = gather_doubling(hidden[0], jobs)
    mine = None
    for turn_index in range(2):
        last = turn_index == 1
        batch = batches[turn_index]
        cosine, sine = turning(lax.dynamic_index_in_dim(lengths, batch[0], 0, keepdims=False))
        joined, by_owner = project(places, own, other, attn_gain, *got["qkv"])
        spread = lax.all_to_all(joined, "mp", split_axis=0, concat_axis=0)
        mixed = attend(
            batch, lengths, spread, cosine, sine, *got["caches"], w_query.shape[2]
        )
        heads_out = lax.all_to_all(mixed.transpose(1, 0, 2), "mp", split_axis=0, concat_axis=0)
        keep, send = spread_project(places, heads_out, *got["out"])
        pairs = []

        def pair_job(first):
            def job(token):
                pairs.extend(fetch_pairs(token, w_gate_up[0], first, share))
                return pairs[-share:]

            return job

        jobs = [pair_job(first) for first in range(0, blocks, share)]
        middle = scatter_halving(send, keep, by_owner if mine is None else mine, jobs)
        own, other = gather_doubling(middle, jobs)
        keep, send, own_rows = mlp(places, ids, own, other, mlp_gain, pairs, w_down[0], last)
        mlp_part = scatter(send, keep)
        if last:
            middle = own_rows
        mine = (middle.astype(jnp.float32) + mlp_part).astype(jnp.bfloat16)
        if not last:
            got, jobs = attention_jobs(1)
            mine = swap(mine, 1, "section")
            own, other = gather_doubling(mine, jobs)
    return mine[None]


def solution(mesh):
    placed = (
        P("section", "mp", None),
        P("section", None),
        P("section", None, "mp"),
        P("section", None, "mp"),
        P("section", None, "mp"),
        P("section", "mp", None),
        P("section", None),
        P("section", None, None, "mp"),
        P("section", "mp", None),
        P("section", None, "mp", None, None),
        P("section", None, "mp", None, None),
        P(None, "mp"),
    )
    return jax.shard_map(
        body, mesh=mesh, in_specs=placed, out_specs=P("section", "mp", None), check_vma=False
    )
```

```python
import functools

import jax
import jax.numpy as jnp
import numpy as np
from jax import lax
from jax.experimental import pallas as pl
from jax.experimental.pallas import tpu as pltpu
from jax.sharding import PartitionSpec as P

QUERY_HEADS = 64
KEY_VALUE_HEADS = 8
HEAD_SIZE = 128

epsilon = 1e-05

UNROLL = 4


def swap(value, mask, axis="mp"):
    count = lax.axis_size(axis)
    return lax.ppermute(value, axis, [(source, source ^ mask) for source in range(count)])


def exchange(parts):
    count = lax.axis_size("mp")
    groups = [list(range(core, count, 2)) for core in range(2)]
    return lax.all_to_all(
        parts, "mp", split_axis=0, concat_axis=0, axis_index_groups=groups, tiled=True
    )


def chip_masks():
    return [1 << bit for bit in range(1, (lax.axis_size("mp") - 1).bit_length())]


def relative_ids():
    ids = np.zeros((1,), np.int32)
    for mask in reversed(chip_masks()):
        ids = np.concatenate([ids, ids ^ mask])
    return ids


def vmem():
    return pl.BlockSpec(memory_space=pltpu.VMEM)


def smem():
    return pl.BlockSpec(memory_space=pltpu.SMEM)


def placed_in(values, space):
    return pltpu.with_memory_space_constraint(values, space)


def hbm():
    return pl.BlockSpec(memory_space=pl.ANY)


def run_copies(copies):
    for at, copy in enumerate(copies):
        copy.start(priority=at % 2)
    for copy in copies:
        copy.wait()


def fetch_kernel(pieces, tokens, *refs):
    arrays = len(pieces)
    refs, sems = refs[tokens:-1], refs[-1]
    copies = []
    for array, (count, source, target) in enumerate(zip(pieces, refs, refs[arrays:])):
        size = source.shape[0] // count
        for piece in range(count):
            span = pl.ds(piece * size, size)
            copies.append(
                pltpu.make_async_copy(source.at[span], target.at[span], sems.at[array, piece])
            )
    run_copies(copies)


def fetch(tokens, *arrays):
    pieces = [8 if array.shape[0] % 128 == 0 else 1 for array in arrays]
    return pl.pallas_call(
        functools.partial(fetch_kernel, pieces, len(tokens)),
        out_shape=[pltpu.VMEM(array.shape, array.dtype) for array in arrays],
        in_specs=[hbm()] * (len(tokens) + len(arrays)),
        out_specs=[vmem()] * len(arrays),
        scratch_shapes=[pltpu.SemaphoreType.DMA((len(arrays), 8))],
        compiler_params=pltpu.CompilerParams(vmem_limit_bytes=1 << 20),
        cost_estimate=pl.CostEstimate(
            flops=0, bytes_accessed=sum(2 * array.size for array in arrays), transcendentals=0
        ),
    )(*tokens, *[placed_in(array, pltpu.HBM) for array in arrays])


def fetch_caches_kernel(token_ref, where_ref, keys_ref, values_ref, key_ref, value_ref, sems):
    rows, places, _ = key_ref.shape
    batch = where_ref[0]
    copies = []
    for array, (source, target) in enumerate(((keys_ref, key_ref), (values_ref, value_ref))):
        for row in range(rows):
            for piece in range(2):
                span = pl.ds(piece * (places // 2), places // 2)
                copies.append(
                    pltpu.make_async_copy(
                        source.at[batch, row, span],
                        target.at[row, span],
                        sems.at[array, row, piece],
                    )
                )
    run_copies(copies)


def fetch_caches(token, where, keys, values):
    shape = pltpu.VMEM(keys.shape[1:], keys.dtype)
    return pl.pallas_call(
        fetch_caches_kernel,
        out_shape=[shape, shape],
        in_specs=[hbm(), smem(), hbm(), hbm()],
        out_specs=[vmem(), vmem()],
        scratch_shapes=[pltpu.SemaphoreType.DMA((2, keys.shape[1], 2))],
        compiler_params=pltpu.CompilerParams(vmem_limit_bytes=1 << 20),
        cost_estimate=pl.CostEstimate(
            flops=0, bytes_accessed=2 * keys.size, transcendentals=0
        ),
    )(token, where, placed_in(keys, pltpu.HBM), placed_in(values, pltpu.HBM))


def fetch_pairs_kernel(first, token_ref, source, *refs):
    targets, sems = refs[:-1], refs[-1]
    size = source.shape[0] // 4
    copies = []
    for block, target in enumerate(targets):
        for piece in range(4):
            span = pl.ds(piece * size, size)
            copies.append(
                pltpu.make_async_copy(
                    source.at[span, :, pl.ds((first + block) * 128, 128)],
                    target.at[span],
                    sems.at[block, piece],
                )
            )
    run_copies(copies)


def fetch_pairs(token, weights, first, blocks):
    depth = weights.shape[0]
    return pl.pallas_call(
        functools.partial(fetch_pairs_kernel, first),
        out_shape=[pltpu.VMEM((depth, 2, 128), weights.dtype)] * blocks,
        in_specs=[hbm(), hbm()],
        out_specs=[vmem()] * blocks,
        scratch_shapes=[pltpu.SemaphoreType.DMA((blocks, 4))],
        compiler_params=pltpu.CompilerParams(vmem_limit_bytes=1 << 20),
        cost_estimate=pl.CostEstimate(
            flops=0, bytes_accessed=4 * blocks * depth * 128, transcendentals=0
        ),
    )(token, placed_in(weights, pltpu.HBM))


def step_call(kernel, shapes, operands, held_back):
    return pl.pallas_call(
        kernel,
        out_shape=[pltpu.VMEM(shape, jnp.bfloat16) for shape in shapes],
        in_specs=[vmem()] * len(operands) + [hbm()] * len(held_back),
        out_specs=[vmem()] * len(shapes),
        compiler_params=pltpu.CompilerParams(vmem_limit_bytes=4 << 20),
        cost_estimate=pl.CostEstimate(
            flops=2 * operands[0].size, bytes_accessed=6 * operands[0].size, transcendentals=0
        ),
    )(*operands, *[placed_in(array, pltpu.VMEM) for array in held_back])


def add_kernel(outs, operands, *refs):
    targets = refs[-outs:]
    share = targets[0].shape[0]
    for which, target in enumerate(targets):
        for place in range(share):
            total = 0.0
            for ref in refs[:operands]:
                total += ref[which * share + place].astype(jnp.float32)
            target[place] = total.astype(jnp.bfloat16)


def add_parts(operands, outs, held_back=()):
    lead = operands[0].shape[0]
    shape = (lead // outs,) + operands[0].shape[1:]
    return step_call(
        functools.partial(add_kernel, outs, len(operands)), [shape] * outs, operands, held_back
    )


def finish_kernel(own_ref, keep_ref, got_ref, *refs):
    total = keep_ref[0].astype(jnp.float32) + got_ref[0].astype(jnp.float32)
    if len(own_ref.shape) == 2:
        total += own_ref[...].astype(jnp.float32)
    else:
        parts = [own_ref[owner].astype(jnp.float32) for owner in range(own_ref.shape[0])]
        total += jnp.concatenate(parts, axis=0)
    refs[-1][...] = total.astype(jnp.bfloat16)


def join_kernel(low_ref, high_ref, *refs):
    half = low_ref.shape[0]
    out_ref = refs[-1]
    for place in range(half):
        out_ref[place] = low_ref[place]
        out_ref[half + place] = high_ref[place]


def join(low, high, held_back=()):
    shape = (2 * low.shape[0],) + low.shape[1:]
    return step_call(join_kernel, [shape], (low, high), held_back)[0]


def run_job(jobs, token):
    return jobs.pop(0)(token) if jobs else ()


def scatter(send, keep):
    (held,) = add_parts((keep, swap(send, 1)), 1)
    return jnp.sum(exchange(held).astype(jnp.float32), axis=0)


def scatter_halving(keep, got, own, jobs):
    held_back = ()
    for mask in chip_masks():
        keep, send = add_parts((keep, got), 2, held_back)
        got = swap(send, mask)
        held_back = run_job(jobs, send)
    return step_call(finish_kernel, [keep.shape[1:]], (own, keep, got), held_back)[0]


def gather(part):
    own = exchange(jnp.broadcast_to(part[None], (lax.axis_size("mp") // 2,) + part.shape))
    return own, swap(own, 1)


def hop(part, mask):
    count = lax.axis_size("mp")
    pairs = [(source, (source + count) % (2 * count) ^ mask) for source in range(2 * count)]
    return lax.ppermute(part, ("section", "mp"), pairs)


def gather_doubling(part, jobs, hops):
    held = part[None]
    for step, mask in enumerate(reversed(chip_masks())):
        job_token = held
        if hops and step == 0:
            got = hop(held, mask)
            held = hop(held, 0)
        else:
            got = swap(held, mask)
        held = join(held, got, run_job(jobs, job_token))
    return held, swap(held, 1)


def inverse_rms(x_refs):
    half, rows, chunk = x_refs[0].shape
    total = jnp.zeros((rows, chunk), jnp.float32)
    for x_ref in x_refs:

        def add(group, total):
            for step in range(UNROLL):
                wide = x_ref[group * UNROLL + step].astype(jnp.float32)
                total = total + wide * wide
            return total

        total = lax.fori_loop(0, half // UNROLL, add, total)
    return lax.rsqrt(jnp.sum(total, axis=-1, keepdims=True) / (2 * half * chunk) + epsilon)


def span_of(ids_ref, k, chunk):
    return pl.ds(pl.multiple_of(ids_ref[k] * chunk, chunk), chunk)


def normed_chunk(x_ref, gain_ref, scale, k, span):
    wide = x_ref[k].astype(jnp.float32)
    return (wide * scale * gain_ref[:, span]).astype(jnp.bfloat16)


def project_kernel(ids_ref, own_ref, other_ref, gain_ref, wq_ref, wk_ref, wv_ref, out_ref,
                   mine_ref, q_sum, kv_sum, wide):
    queries = wq_ref.shape[1]
    count, rows_dev, _ = out_ref.shape
    half = count // 2
    by_rows = own_ref.shape[1] == rows_dev
    chunk = wq_ref.shape[0] // count
    if by_rows:
        for first, x_ref in ((0, own_ref), (half, other_ref)):
            for place in range(half):
                at = (first + place) * rows_dev
                wide[at : at + rows_dev, :] = x_ref[place].astype(jnp.float32)
        total = 0.0
        for k in range(count):
            part = wide[:, k * chunk : (k + 1) * chunk]
            total += part * part
        mean = jnp.sum(total, axis=-1, keepdims=True) / (count * chunk)
        scale = lax.rsqrt(mean + epsilon)
    else:
        scale = inverse_rms((own_ref, other_ref))
    q_sum[...] = jnp.zeros_like(q_sum)
    kv_sum[...] = jnp.zeros_like(kv_sum)
    for first, x_ref in ((0, own_ref), (half, other_ref)):

        @pl.loop(0, half // UNROLL)
        def _(group):
            q_part = 0.0
            kv_part = 0.0
            for step in range(UNROLL):
                k = group * UNROLL + step
                if by_rows:
                    span = pl.ds(pl.multiple_of((first + k) * chunk, chunk), chunk)
                    normed = (wide[:, span] * scale * gain_ref[:, span]).astype(jnp.bfloat16)
                else:
                    span = span_of(ids_ref, first + k, chunk)
                    normed = normed_chunk(x_ref, gain_ref, scale, k, span)
                q_part += jnp.dot(normed, wq_ref[span, :], preferred_element_type=jnp.float32)
                kv_part += lax.dot_general(
                    normed,
                    jnp.concatenate([wk_ref[:, span], wv_ref[:, span]], axis=0),
                    (((1,), (1,)), ((), ())),
                    preferred_element_type=jnp.float32,
                )
            q_sum[...] += q_part
            kv_sum[...] += kv_part

    for place in range(count):
        owner = ids_ref[place] if by_rows else place
        lines = slice(place * rows_dev, (place + 1) * rows_dev)
        out_ref[owner, :, :queries] = q_sum[lines, :].astype(jnp.bfloat16)
        out_ref[owner, :, queries:] = kv_sum[lines, :].astype(jnp.bfloat16)
        if by_rows:
            span = span_of(ids_ref, 0, chunk)
            mine_ref[owner] = wide[lines, span].astype(jnp.bfloat16)


def project(ids, own, other, gain, wq, wk, wv):
    count = ids.shape[0]
    width, queries = wq.shape
    keys = wk.shape[0]
    size = queries + 2 * keys
    rows_dev = 2 * own.size // (count * width)
    rows = count * rows_dev
    by_rows = own.shape[1] == rows_dev
    return pl.pallas_call(
        project_kernel,
        out_shape=[
            pltpu.VMEM((count, rows_dev, size), jnp.bfloat16),
            pltpu.VMEM((count, rows_dev, width // count), jnp.bfloat16),
        ],
        in_specs=[smem()] + [vmem()] * 6,
        out_specs=[vmem(), vmem()],
        scratch_shapes=[
            pltpu.VMEM((rows, queries), jnp.float32),
            pltpu.VMEM((rows, 2 * keys), jnp.float32),
            pltpu.VMEM((rows, width if by_rows else 128), jnp.float32),
        ],
        compiler_params=pltpu.CompilerParams(vmem_limit_bytes=(3 << 20) + 4 * rows * width),
        cost_estimate=pl.CostEstimate(
            flops=2 * rows * width * size, bytes_accessed=2 * width * size, transcendentals=0
        ),
    )(ids, own, other, gain, *[placed_in(w, pltpu.VMEM) for w in (wq, wk, wv)])


def attend_kernel(where_ref, length_ref, in_ref, cos_ref, sin_ref, key_buf, value_buf, out_ref,
                  lined, wide_q):
    rows, devices, queries = out_ref.shape
    width = key_buf.shape[2]
    keys = (in_ref.shape[2] - queries) // 2
    size = cos_ref.shape[1]
    groups = width // size
    pieces = size // keys
    slots = queries // size
    heads = devices * slots
    places = key_buf.shape[1]
    batch = where_ref[0]

    for device in range(devices):
        wide = in_ref[device].astype(jnp.float32)
        for row in range(rows):
            lined[row, device : device + 1, :] = wide[row : row + 1]
    line = lax.broadcasted_iota(jnp.int32, (devices, 1), 0)
    group_of = line * groups // devices
    for row in range(rows):
        cosine = cos_ref[pl.ds(row, 1), :]
        sine = sin_ref[pl.ds(row, 1), :]

        def turned(wide):
            other = jnp.concatenate([wide[:, size // 2 :], wide[:, : size // 2]], axis=1)
            return (wide * cosine + other * sine).astype(jnp.bfloat16).astype(jnp.float32)

        key_lines = jnp.zeros((devices, size), jnp.float32)
        value_lines = jnp.zeros((devices, size), jnp.float32)
        for group in range(groups):
            own_key, own_value = (
                jnp.concatenate(
                    [
                        lined[row, device : device + 1, at : at + keys]
                        for device in range(group * pieces, (group + 1) * pieces)
                    ],
                    axis=1,
                )
                for at in (queries, queries + keys)
            )
            here = group_of == group
            key_lines = jnp.where(here, turned(own_key), key_lines)
            value_lines = jnp.where(here, own_value, value_lines)
        own_parts = []
        for slot in range(slots):
            part = turned(lined[row, :, slot * size : (slot + 1) * size])
            own_parts.append(jnp.sum(part * key_lines, axis=1, keepdims=True))
            for group in range(groups):
                wide_q[
                    slot * devices : (slot + 1) * devices, group * size : (group + 1) * size
                ] = jnp.where(group_of == group, part, 0.0).astype(jnp.bfloat16)
        own_score = jnp.concatenate(own_parts, axis=0) * (size ** -0.5)
        scores = lax.dot_general(
            wide_q[...], key_buf[row], (((1,), (1,)), ((), ())), preferred_element_type=jnp.float32
        ) * (size ** -0.5)
        spot = lax.broadcasted_iota(jnp.int32, (heads, places), 1)
        scores = jnp.where(spot < length_ref[batch, row], scores, -1e30)
        highest = jnp.maximum(jnp.max(scores, axis=1, keepdims=True), own_score)
        raised = jnp.exp(scores - highest)
        own_raised = jnp.exp(own_score - highest)
        denominator = jnp.sum(raised, axis=1, keepdims=True) + own_raised
        weights = (raised / denominator).astype(jnp.bfloat16)
        own_weight = (own_raised / denominator).astype(jnp.bfloat16).astype(jnp.float32)
        mixed = jnp.dot(weights, value_buf[row], preferred_element_type=jnp.float32)
        for slot in range(slots):
            lines = slice(slot * devices, (slot + 1) * devices)
            picked = own_weight[lines] * value_lines
            for group in range(groups):
                picked = picked + jnp.where(
                    group_of == group, mixed[lines, group * size : (group + 1) * size], 0.0
                )
            out_ref[row, :, slot * size : (slot + 1) * size] = picked.astype(jnp.bfloat16)


def attend(where, lengths, spread, cosine, sine, keys, values, queries):
    devices, rows, length = spread.shape
    places, width = keys.shape[1:]
    heads = devices * queries // HEAD_SIZE
    return pl.pallas_call(
        attend_kernel,
        out_shape=pltpu.VMEM((rows, devices, queries), jnp.bfloat16),
        in_specs=[smem(), smem()] + [vmem()] * 5,
        out_specs=vmem(),
        scratch_shapes=[
            pltpu.VMEM((rows, devices, length), jnp.float32),
            pltpu.VMEM((heads, width), jnp.bfloat16),
        ],
        compiler_params=pltpu.CompilerParams(vmem_limit_bytes=4 << 20),
        cost_estimate=pl.CostEstimate(
            flops=4 * rows * heads * places * width,
            bytes_accessed=4 * rows * places * width,
            transcendentals=rows * heads * places,
        ),
    )(
        where,
        lengths,
        spread,
        cosine,
        sine,
        placed_in(keys, pltpu.VMEM),
        placed_in(values, pltpu.VMEM),
    )


def spread_kernel(ids_ref, x_ref, w_ref, out_ref, values):
    parts, rows, chunk = out_ref.shape
    count, rows_dev, _ = x_ref.shape
    for owner in range(count):
        values[owner * rows_dev : (owner + 1) * rows_dev, :] = x_ref[owner].astype(jnp.float32)
    ready = values[...].astype(jnp.bfloat16)

    @pl.loop(0, parts // UNROLL)
    def _(group):
        for step in range(UNROLL):
            k = group * UNROLL + step
            span = span_of(ids_ref, k, chunk)
            out_ref[k] = jnp.dot(
                ready, w_ref[:, span], preferred_element_type=jnp.float32
            ).astype(jnp.bfloat16)


def spread_project(ids, values, weights):
    count, rows_dev, depth = values.shape
    rows = count * rows_dev
    chunk = weights.shape[1] // count
    parts = ids.shape[0]
    return pl.pallas_call(
        spread_kernel,
        out_shape=pltpu.VMEM((parts, rows, chunk), jnp.bfloat16),
        in_specs=[smem(), vmem(), vmem()],
        out_specs=vmem(),
        scratch_shapes=[pltpu.VMEM((rows, depth), jnp.float32)],
        compiler_params=pltpu.CompilerParams(vmem_limit_bytes=4 << 20),
        cost_estimate=pl.CostEstimate(
            flops=2 * rows * depth * parts * chunk,
            bytes_accessed=2 * depth * parts * chunk,
            transcendentals=0,
        ),
    )(ids, values, placed_in(weights, pltpu.VMEM))


def mlp_kernel(by_rows, me_ref, ids_ref, own_ref, other_ref, gain_ref, down_hbm, *refs):
    pairs, (keep_ref, send_ref, middle_ref), (stacked, wide_x, total, act, down_ref, sems) = (
        refs[:-9],
        refs[-9:-6],
        refs[-6:],
    )
    half, rows, chunk = own_ref.shape
    blocks = pairs
    per_chunk = chunk // 128

    def down_copy(k):
        return pltpu.make_async_copy(
            down_hbm.at[:, span_of(ids_ref, k, chunk)], down_ref.at[lax.rem(k, half)], sems.at[k]
        )

    @pl.loop(0, half)
    def _(k):
        down_copy(k).start()

    scale = inverse_rms((own_ref, other_ref))
    for first, x_ref in ((0, own_ref), (half, other_ref)):

        @pl.loop(0, half)
        def _(place):
            k = first + place
            normed = normed_chunk(x_ref, gain_ref, scale, place, span_of(ids_ref, k, chunk))
            for b in range(per_chunk):
                stacked[k * per_chunk + b] = normed[:, b * 128 : (b + 1) * 128]

    if by_rows:
        rows_dev = middle_ref.shape[0]
        line = lax.broadcasted_iota(jnp.int32, (rows, 1), 0)
        for first, x_ref in ((0, own_ref), (half, other_ref)):

            @pl.loop(0, half)
            def _(place):
                wide = x_ref[place].astype(jnp.float32)
                span = span_of(ids_ref, first + place, chunk)
                for row in range(rows_dev):
                    here = line == me_ref[0] * rows_dev + row
                    middle_ref[row : row + 1, span] = jnp.sum(
                        jnp.where(here, wide, 0.0), axis=0, keepdims=True
                    )

    line = lax.broadcasted_iota(jnp.int32, (128, 512), 0)
    column = lax.broadcasted_iota(jnp.int32, (128, 512), 1)
    aim = jnp.where(column < 256, 2 * line, 2 * line + 257)
    widen = jnp.where(column == aim, 1.0, 0.0).astype(jnp.bfloat16)

    @pl.loop(0, 2 * half * per_chunk // 8)
    def _(group):
        span = pl.ds(group * 8, 8)
        wide = jnp.dot(
            stacked[span].reshape(8 * rows, 128), widen, preferred_element_type=jnp.float32
        ).astype(jnp.bfloat16)
        for b in range(8):
            lines = slice(b * rows, (b + 1) * rows)
            wide_x[group, :rows, b * 256 : (b + 1) * 256] = wide[lines, :256]
            wide_x[group, rows:, b * 256 : (b + 1) * 256] = wide[lines, 256:]

    total[...] = jnp.zeros_like(total)
    per_group = 8 // per_chunk

    @pl.loop(0, wide_x.shape[0])
    def _(group):
        for j in range(0, len(blocks), 2):
            part = 0.0
            for step in range(per_group):
                at = ids_ref[group * per_group + step] * (2 * chunk)
                span = pl.ds(pl.multiple_of(at, 2 * chunk), 2 * chunk)
                pair = jnp.concatenate([blocks[j][span, :], blocks[j + 1][span, :]], axis=1)
                part += jnp.dot(
                    wide_x[group, :, step * 2 * chunk : (step + 1) * 2 * chunk],
                    pair,
                    preferred_element_type=jnp.float32,
                )
            total[:, j * 128 : (j + 2) * 128] += part

    gate = total[:rows, :]
    act[...] = (gate / (1.0 + jnp.exp(-gate)) * total[rows:, :]).astype(jnp.bfloat16)

    def down(first, k):
        down_copy(first + k).wait()
        return jnp.dot(act[...], down_ref[k], preferred_element_type=jnp.float32)

    for first, target in ((0, keep_ref), (half, send_ref)):

        @pl.loop(0, half // UNROLL)
        def _(group):
            for step in range(UNROLL):
                k = group * UNROLL + step
                part = down(first, k)
                if not by_rows:
                    target[k] = part.astype(jnp.bfloat16)
                    continue
                span = span_of(ids_ref, first + k, chunk)
                first_core = ids_ref[0] == 0
                for chip in range(half):
                    at = 2 * chip * rows_dev
                    low = part[at : at + rows_dev]
                    high = part[at + rows_dev : at + 2 * rows_dev]
                    keep_ref[chip, :, span] = jnp.where(first_core, low, high).astype(jnp.bfloat16)
                    send_ref[chip, :, span] = jnp.where(first_core, high, low).astype(jnp.bfloat16)
            if first == 0:
                for step in range(UNROLL):
                    down_copy(half + group * UNROLL + step).start()


def mlp(me, ids, own, other, gain, pairs, down, by_rows):
    half, rows, chunk = own.shape
    units, width = down.shape
    part = (half, rows // (2 * half), width) if by_rows else own.shape
    shape = pltpu.VMEM(part, jnp.bfloat16)
    return pl.pallas_call(
        functools.partial(mlp_kernel, by_rows),
        out_shape=(shape, shape, pltpu.VMEM((rows // (2 * half), width), jnp.float32)),
        in_specs=[smem(), smem()] + [vmem()] * 3 + [hbm()] + [vmem()] * len(pairs),
        out_specs=(vmem(), vmem(), vmem()),
        scratch_shapes=[
            pltpu.VMEM((width // 128, rows, 128), jnp.bfloat16),
            pltpu.VMEM((width // 1024, 2 * rows, 2048), jnp.bfloat16),
            pltpu.VMEM((2 * rows, units), jnp.float32),
            pltpu.VMEM((rows, units), jnp.bfloat16),
            pltpu.VMEM((half, units, chunk), jnp.bfloat16),
            pltpu.SemaphoreType.DMA((2 * half,)),
        ],
        compiler_params=pltpu.CompilerParams(
            vmem_limit_bytes=(3 << 19) + 10 * rows * width + (10 * rows + width) * units
        ),
        cost_estimate=pl.CostEstimate(
            flops=6 * rows * units * width, bytes_accessed=6 * units * width, transcendentals=0
        ),
    )(
        me,
        ids,
        own,
        other,
        gain,
        placed_in(down, pltpu.HBM),
        *[placed_in(pair.reshape(2 * width, 128), pltpu.VMEM) for pair in pairs],
    )


def turning(positions):
    half_dim = HEAD_SIZE // 2
    frequency = 500000.0 ** (-2.0 * jnp.arange(half_dim, dtype=jnp.float32) / HEAD_SIZE)
    angles = positions.astype(jnp.float32)[:, None] * frequency[None, :]
    cosine = jnp.cos(angles)
    sine = jnp.sin(angles)
    return jnp.concatenate([cosine, cosine], axis=1), jnp.concatenate([-sine, sine], axis=1)


def body(
    hidden,
    attn_gain,
    w_query,
    w_key,
    w_value,
    w_out,
    mlp_gain,
    w_gate_up,
    w_down,
    key_cache,
    value_cache,
    lengths,
):
    rows_dev = hidden.shape[1]
    count = lax.axis_size("mp")
    half = count // 2
    section_index = lax.axis_index("section")
    model_index = lax.axis_index("mp")
    core = model_index % 2
    width = hidden.shape[2]
    chips = 2 * jnp.arange(half, dtype=jnp.int32)
    ids = jnp.concatenate([chips + core, chips + 1 - core])
    near = jnp.asarray(relative_ids())
    near_places, far_places = near ^ model_index, near ^ model_index ^ 1
    places = jnp.concatenate([near_places, far_places])
    wk = w_key[0].T
    wv = w_value[0].T
    blocks = w_gate_up.shape[3] // 128
    windows = len(chip_masks())
    bounds = [-(-blocks * step // windows) for step in range(windows + 1)]
    batches = [
        jnp.remainder(section_index + turn_index, 2).astype(jnp.int32).reshape(1)
        for turn_index in range(2)
    ]

    tables = [
        turning(lax.dynamic_index_in_dim(lengths, batch[0], 0, keepdims=False))
        for batch in batches
    ]
    me = model_index.astype(jnp.int32).reshape(1)
    early = (ids, places, near_places, far_places, me, *batches, *tables[0], *tables[1])

    def attention_jobs(turn_index):
        got = {}

        def projections(token):
            got["qkv"] = fetch((token, *early), w_query[0], wk, wv)
            return got["qkv"]

        def out_projection(token):
            got["out"] = fetch((token,), w_out[0])
            return got["out"]

        def caches(token):
            got["caches"] = fetch_caches(token, batches[turn_index], key_cache[0], value_cache[0])
            return got["caches"]

        return got, [projections, out_projection, caches]

    got, jobs = attention_jobs(0)
    own, other = gather_doubling(hidden[0], jobs, False)
    mine = None
    for turn_index in range(2):
        last = turn_index == 1
        batch = batches[turn_index]
        joined, by_owner = project(places, own, other, attn_gain, *got["qkv"])
        spread = lax.all_to_all(joined, "mp", split_axis=0, concat_axis=0)
        mixed = attend(
            batch, lengths, spread, *tables[turn_index], *got["caches"], w_query.shape[2]
        )
        heads_out = lax.all_to_all(mixed.transpose(1, 0, 2), "mp", split_axis=0, concat_axis=0)
        got_core = swap(spread_project(far_places, heads_out, *got["out"]), 1)
        keep = spread_project(near_places, heads_out, *got["out"])
        pairs = []

        def pair_job(first, size):
            def job(token):
                new = fetch_pairs(token, w_gate_up[0], first, size) if size else ()
                pairs.extend(new)
                return new

            return job

        jobs = [pair_job(low, high - low) for low, high in zip(bounds, bounds[1:])]
        middle = scatter_halving(keep, got_core, by_owner if mine is None else mine, jobs)
        own, other = gather(middle)
        keep, send, own_rows = mlp(me, ids, own, other, mlp_gain, pairs, w_down[0], last)
        mlp_part = scatter(send, keep)
        if last:
            middle = own_rows
        mine = (middle.astype(jnp.float32) + mlp_part).astype(jnp.bfloat16)
        if not last:
            got, jobs = attention_jobs(1)
            own, other = gather_doubling(mine, jobs, True)
            mine = own[0]
    return mine[None]


def solution(mesh):
    placed = (
        P("section", "mp", None),
        P("section", None),
        P("section", None, "mp"),
        P("section", None, "mp"),
        P("section", None, "mp"),
        P("section", "mp", None),
        P("section", None),
        P("section", None, None, "mp"),
        P("section", "mp", None),
        P("section", None, "mp", None, None),
        P("section", None, "mp", None, None),
        P(None, "mp"),
    )
    return jax.shard_map(
        body, mesh=mesh, in_specs=placed, out_specs=P("section", "mp", None), check_vma=False
    )
```

```python
import functools

import jax
import jax.numpy as jnp
import numpy as np
from jax import lax
from jax.experimental import pallas as pl
from jax.experimental.pallas import tpu as pltpu
from jax.sharding import PartitionSpec as P

QUERY_HEADS = 64
KEY_VALUE_HEADS = 8
HEAD_SIZE = 128

epsilon = 1e-05

UNROLL = 4


def swap(value, mask, axis="mp"):
    count = lax.axis_size(axis)
    return lax.ppermute(value, axis, [(source, source ^ mask) for source in range(count)])


def exchange(parts):
    count = lax.axis_size("mp")
    groups = [list(range(core, count, 2)) for core in range(2)]
    return lax.all_to_all(
        parts, "mp", split_axis=0, concat_axis=0, axis_index_groups=groups, tiled=True
    )


def chip_masks():
    return [1 << bit for bit in range(1, (lax.axis_size("mp") - 1).bit_length())]


def relative_ids():
    ids = np.zeros((1,), np.int32)
    for mask in reversed(chip_masks()):
        ids = np.concatenate([ids, ids ^ mask])
    return ids


def vmem():
    return pl.BlockSpec(memory_space=pltpu.VMEM)


def smem():
    return pl.BlockSpec(memory_space=pltpu.SMEM)


def placed_in(values, space):
    return pltpu.with_memory_space_constraint(values, space)


def hbm():
    return pl.BlockSpec(memory_space=pl.ANY)


def run_copies(copies):
    for at, copy in enumerate(copies):
        copy.start(priority=at % 2)
    for copy in copies:
        copy.wait()


def fetch_kernel(pieces, tokens, *refs):
    arrays = len(pieces)
    refs, sems = refs[tokens:-1], refs[-1]
    copies = []
    for array, (count, source, target) in enumerate(zip(pieces, refs, refs[arrays:])):
        size = source.shape[0] // count
        for piece in range(count):
            span = pl.ds(piece * size, size)
            copies.append(
                pltpu.make_async_copy(source.at[span], target.at[span], sems.at[array, piece])
            )
    run_copies(copies)


def fetch(tokens, *arrays):
    pieces = [8 if array.shape[0] % 128 == 0 else 1 for array in arrays]
    return pl.pallas_call(
        functools.partial(fetch_kernel, pieces, len(tokens)),
        out_shape=[pltpu.VMEM(array.shape, array.dtype) for array in arrays],
        in_specs=[hbm()] * (len(tokens) + len(arrays)),
        out_specs=[vmem()] * len(arrays),
        scratch_shapes=[pltpu.SemaphoreType.DMA((len(arrays), 8))],
        compiler_params=pltpu.CompilerParams(vmem_limit_bytes=1 << 20),
        cost_estimate=pl.CostEstimate(
            flops=0, bytes_accessed=sum(2 * array.size for array in arrays), transcendentals=0
        ),
    )(*tokens, *[placed_in(array, pltpu.HBM) for array in arrays])


def fetch_caches_kernel(where_ref, keys_ref, values_ref, *refs):
    key_ref, value_ref, sems = refs[-3:]
    rows, places, _ = key_ref.shape
    batch = where_ref[0]
    copies = []
    for array, (source, target) in enumerate(((keys_ref, key_ref), (values_ref, value_ref))):
        for row in range(rows):
            for piece in range(2):
                span = pl.ds(piece * (places // 2), places // 2)
                copies.append(
                    pltpu.make_async_copy(
                        source.at[batch, row, span],
                        target.at[row, span],
                        sems.at[array, row, piece],
                    )
                )
    run_copies(copies)


def fetch_caches(tokens, where, keys, values):
    shape = pltpu.VMEM(keys.shape[1:], keys.dtype)
    return pl.pallas_call(
        fetch_caches_kernel,
        out_shape=[shape, shape],
        in_specs=[smem(), hbm(), hbm()] + [hbm()] * len(tokens),
        out_specs=[vmem(), vmem()],
        scratch_shapes=[pltpu.SemaphoreType.DMA((2, keys.shape[1], 2))],
        compiler_params=pltpu.CompilerParams(vmem_limit_bytes=1 << 20),
        cost_estimate=pl.CostEstimate(
            flops=0, bytes_accessed=2 * keys.size, transcendentals=0
        ),
    )(where, placed_in(keys, pltpu.HBM), placed_in(values, pltpu.HBM), *tokens)


def fetch_chunks_kernel(ids_ref, token_ref, source, target, sems):
    count, _, chunk = target.shape
    run_copies(
        [
            pltpu.make_async_copy(
                source.at[:, span_of(ids_ref, k, chunk)], target.at[k], sems.at[k]
            )
            for k in range(count)
        ]
    )


def fetch_chunks(token, ids, weights, chunk):
    count, depth = ids.shape[0], weights.shape[0]
    return pl.pallas_call(
        fetch_chunks_kernel,
        out_shape=[pltpu.VMEM((count, depth, chunk), weights.dtype)],
        in_specs=[smem(), hbm(), hbm()],
        out_specs=[vmem()],
        scratch_shapes=[pltpu.SemaphoreType.DMA((count,))],
        compiler_params=pltpu.CompilerParams(vmem_limit_bytes=1 << 20),
        cost_estimate=pl.CostEstimate(
            flops=0, bytes_accessed=2 * count * depth * chunk, transcendentals=0
        ),
    )(ids, token, placed_in(weights, pltpu.HBM))


def fetch_pairs_kernel(items, ids_ref, token_ref, source, *refs):
    targets, sems = refs[:-1], refs[-1]
    half = sems.shape[1]
    chunk = targets[0].shape[0] // half
    copies = []
    for at, ((side, block), target) in enumerate(zip(items, targets)):
        for k in range(half):
            copies.append(
                pltpu.make_async_copy(
                    source.at[
                        span_of(ids_ref, side * half + k, chunk), :, pl.ds(block * 128, 128)
                    ],
                    target.at[pl.ds(k * chunk, chunk)],
                    sems.at[at, k],
                )
            )
    run_copies(copies)


def fetch_pairs(token, ids, weights, items):
    half = ids.shape[0] // 2
    size = weights.shape[0] // 2
    return pl.pallas_call(
        functools.partial(fetch_pairs_kernel, items),
        out_shape=[pltpu.VMEM((size, 2, 128), weights.dtype)] * len(items),
        in_specs=[smem(), hbm(), hbm()],
        out_specs=[vmem()] * len(items),
        scratch_shapes=[pltpu.SemaphoreType.DMA((len(items), half))],
        compiler_params=pltpu.CompilerParams(vmem_limit_bytes=1 << 20),
        cost_estimate=pl.CostEstimate(
            flops=0, bytes_accessed=4 * len(items) * size * 128, transcendentals=0
        ),
    )(ids, token, placed_in(weights, pltpu.HBM))


def step_call(kernel, shapes, operands, held_back):
    return pl.pallas_call(
        kernel,
        out_shape=[pltpu.VMEM(shape, jnp.bfloat16) for shape in shapes],
        in_specs=[vmem()] * len(operands) + [hbm()] * len(held_back),
        out_specs=[vmem()] * len(shapes),
        compiler_params=pltpu.CompilerParams(vmem_limit_bytes=4 << 20),
        cost_estimate=pl.CostEstimate(
            flops=2 * operands[0].size, bytes_accessed=6 * operands[0].size, transcendentals=0
        ),
    )(*operands, *[placed_in(array, pltpu.VMEM) for array in held_back])


def add_kernel(outs, operands, *refs):
    targets = refs[-outs:]
    share = targets[0].shape[0]
    for which, target in enumerate(targets):
        for place in range(share):
            total = 0.0
            for ref in refs[:operands]:
                total += ref[which * share + place].astype(jnp.float32)
            target[place] = total.astype(jnp.bfloat16)


def add_parts(operands, outs, held_back=()):
    lead = operands[0].shape[0]
    shape = (lead // outs,) + operands[0].shape[1:]
    return step_call(
        functools.partial(add_kernel, outs, len(operands)), [shape] * outs, operands, held_back
    )


def own_kernel(own_ref, keep_ref, got_ref, *refs):
    out_ref = refs[-1]
    if len(own_ref.shape) == 2:
        own = own_ref[...].astype(jnp.float32)
    else:
        parts = [own_ref[owner].astype(jnp.float32) for owner in range(own_ref.shape[0])]
        own = jnp.concatenate(parts, axis=0)
    for place in range(keep_ref.shape[0]):
        total = keep_ref[place].astype(jnp.float32) + got_ref[place].astype(jnp.float32)
        out_ref[place] = (total + own if place == 0 else total).astype(jnp.bfloat16)


def cross_kernel(here_ref, there_ref, *refs):
    out_ref = refs[-1]
    for place in range(2):
        out_ref[place] = (
            here_ref[place].astype(jnp.float32) + there_ref[1 - place].astype(jnp.float32)
        ).astype(jnp.bfloat16)


def join_kernel(low_ref, high_ref, *refs):
    half = low_ref.shape[0]
    out_ref = refs[-1]
    for place in range(half):
        out_ref[place] = low_ref[place]
        out_ref[half + place] = high_ref[place]


def join(low, high, held_back=()):
    shape = (2 * low.shape[0],) + low.shape[1:]
    return step_call(join_kernel, [shape], (low, high), held_back)[0]


def run_job(jobs, token):
    return jobs.pop(0)(token) if jobs else ()


def scatter(send, keep):
    (held,) = add_parts((keep, swap(send, 1)), 1)
    return jnp.sum(exchange(held).astype(jnp.float32), axis=0)


def halve(keep, got, jobs):
    held_back = ()
    for mask in chip_masks()[:-1]:
        keep, send = add_parts((keep, got), 2, held_back)
        got = swap(send, mask)
        held_back = run_job(jobs, send)
    return keep, got, held_back


def spread_pair(pair, jobs):
    held = pair
    for mask in reversed(chip_masks()[:-1]):
        got = swap(held, mask)
        held = join(held, got, run_job(jobs, held))
    return held, swap(held, 1)


def reduce_to_all(keep, got, own, jobs, hops):
    keep, got, held_back = halve(keep, got, jobs)
    (held,) = step_call(own_kernel, [keep.shape], (own, keep, got), held_back)
    far = chip_masks()[-1]
    here = hop(held, 0) if hops else held
    there = hop(held, far) if hops else swap(held, far)
    (pair,) = step_call(cross_kernel, [held.shape], (here, there), run_job(jobs, held))
    return (pair[0], *spread_pair(pair, jobs))


def hop(part, mask):
    count = lax.axis_size("mp")
    pairs = [(source, ((source + count) % (2 * count)) ^ mask) for source in range(2 * count)]
    return lax.ppermute(part, ("section", "mp"), pairs)


def gather_doubling(part, jobs):
    held = part[None]
    got = swap(held, chip_masks()[-1])
    return spread_pair(join(held, got, run_job(jobs, held)), jobs)


def inverse_rms(x_refs):
    half, rows, chunk = x_refs[0].shape
    total = jnp.zeros((rows, chunk), jnp.float32)
    for x_ref in x_refs:

        def add(group, total):
            for step in range(UNROLL):
                wide = x_ref[group * UNROLL + step].astype(jnp.float32)
                total = total + wide * wide
            return total

        total = lax.fori_loop(0, half // UNROLL, add, total)
    return lax.rsqrt(jnp.sum(total, axis=-1, keepdims=True) / (2 * half * chunk) + epsilon)


def span_of(ids_ref, k, chunk):
    return pl.ds(pl.multiple_of(ids_ref[k] * chunk, chunk), chunk)


def normed_chunk(x_ref, gain_ref, scale, k, span):
    wide = x_ref[k].astype(jnp.float32)
    return (wide * scale * gain_ref[:, span]).astype(jnp.bfloat16)


def project_kernel(ids_ref, own_ref, other_ref, gain_ref, wq_ref, wk_ref, wv_ref, out_ref,
                   mine_ref, q_sum, kv_sum, wide):
    queries = wq_ref.shape[1]
    count, rows_dev, _ = out_ref.shape
    half = count // 2
    by_rows = own_ref.shape[1] == rows_dev
    chunk = wq_ref.shape[0] // count
    if by_rows:
        for first, x_ref in ((0, own_ref), (half, other_ref)):
            for place in range(half):
                at = (first + place) * rows_dev
                wide[at : at + rows_dev, :] = x_ref[place].astype(jnp.float32)
        total = 0.0
        for k in range(count):
            part = wide[:, k * chunk : (k + 1) * chunk]
            total += part * part
        mean = jnp.sum(total, axis=-1, keepdims=True) / (count * chunk)
        scale = lax.rsqrt(mean + epsilon)
    else:
        scale = inverse_rms((own_ref, other_ref))
    q_sum[...] = jnp.zeros_like(q_sum)
    kv_sum[...] = jnp.zeros_like(kv_sum)
    for first, x_ref in ((0, own_ref), (half, other_ref)):

        @pl.loop(0, half // UNROLL)
        def _(group):
            q_part = 0.0
            kv_part = 0.0
            for step in range(UNROLL):
                k = group * UNROLL + step
                if by_rows:
                    span = pl.ds(pl.multiple_of((first + k) * chunk, chunk), chunk)
                    normed = (wide[:, span] * scale * gain_ref[:, span]).astype(jnp.bfloat16)
                else:
                    span = span_of(ids_ref, first + k, chunk)
                    normed = normed_chunk(x_ref, gain_ref, scale, k, span)
                q_part += jnp.dot(normed, wq_ref[span, :], preferred_element_type=jnp.float32)
                kv_part += lax.dot_general(
                    normed,
                    jnp.concatenate([wk_ref[:, span], wv_ref[:, span]], axis=0),
                    (((1,), (1,)), ((), ())),
                    preferred_element_type=jnp.float32,
                )
            q_sum[...] += q_part
            kv_sum[...] += kv_part

    for place in range(count):
        owner = ids_ref[place] if by_rows else place
        lines = slice(place * rows_dev, (place + 1) * rows_dev)
        out_ref[owner, :, :queries] = q_sum[lines, :].astype(jnp.bfloat16)
        out_ref[owner, :, queries:] = kv_sum[lines, :].astype(jnp.bfloat16)
        if by_rows:
            span = span_of(ids_ref, 0, chunk)
            mine_ref[owner] = wide[lines, span].astype(jnp.bfloat16)


def project(ids, own, other, gain, wq, wk, wv):
    count = ids.shape[0]
    width, queries = wq.shape
    keys = wk.shape[0]
    size = queries + 2 * keys
    rows_dev = 2 * own.size // (count * width)
    rows = count * rows_dev
    by_rows = own.shape[1] == rows_dev
    return pl.pallas_call(
        project_kernel,
        out_shape=[
            pltpu.VMEM((count, rows_dev, size), jnp.bfloat16),
            pltpu.VMEM((count, rows_dev, width // count), jnp.bfloat16),
        ],
        in_specs=[smem()] + [vmem()] * 6,
        out_specs=[vmem(), vmem()],
        scratch_shapes=[
            pltpu.VMEM((rows, queries), jnp.float32),
            pltpu.VMEM((rows, 2 * keys), jnp.float32),
            pltpu.VMEM((rows, width if by_rows else 128), jnp.float32),
        ],
        compiler_params=pltpu.CompilerParams(vmem_limit_bytes=(3 << 20) + 4 * rows * width),
        cost_estimate=pl.CostEstimate(
            flops=2 * rows * width * size, bytes_accessed=2 * width * size, transcendentals=0
        ),
    )(ids, own, other, gain, *[placed_in(w, pltpu.VMEM) for w in (wq, wk, wv)])


def attend_kernel(where_ref, length_ref, in_ref, cos_ref, sin_ref, key_buf, value_buf, out_ref,
                  lined, wide_q):
    rows, devices, queries = out_ref.shape
    width = key_buf.shape[2]
    keys = (in_ref.shape[2] - queries) // 2
    size = cos_ref.shape[1]
    groups = width // size
    pieces = size // keys
    slots = queries // size
    heads = devices * slots
    places = key_buf.shape[1]
    batch = where_ref[0]

    for device in range(devices):
        wide = in_ref[device].astype(jnp.float32)
        for row in range(rows):
            lined[row, device : device + 1, :] = wide[row : row + 1]
    line = lax.broadcasted_iota(jnp.int32, (devices, 1), 0)
    group_of = line * groups // devices
    for row in range(rows):
        cosine = cos_ref[pl.ds(row, 1), :]
        sine = sin_ref[pl.ds(row, 1), :]

        def turned(wide):
            other = jnp.concatenate([wide[:, size // 2 :], wide[:, : size // 2]], axis=1)
            return (wide * cosine + other * sine).astype(jnp.bfloat16).astype(jnp.float32)

        key_lines = jnp.zeros((devices, size), jnp.float32)
        value_lines = jnp.zeros((devices, size), jnp.float32)
        for group in range(groups):
            own_key, own_value = (
                jnp.concatenate(
                    [
                        lined[row, device : device + 1, at : at + keys]
                        for device in range(group * pieces, (group + 1) * pieces)
                    ],
                    axis=1,
                )
                for at in (queries, queries + keys)
            )
            here = group_of == group
            key_lines = jnp.where(here, turned(own_key), key_lines)
            value_lines = jnp.where(here, own_value, value_lines)
        own_parts = []
        for slot in range(slots):
            part = turned(lined[row, :, slot * size : (slot + 1) * size])
            own_parts.append(jnp.sum(part * key_lines, axis=1, keepdims=True))
            for group in range(groups):
                wide_q[
                    slot * devices : (slot + 1) * devices, group * size : (group + 1) * size
                ] = jnp.where(group_of == group, part, 0.0).astype(jnp.bfloat16)
        own_score = jnp.concatenate(own_parts, axis=0) * (size ** -0.5)
        scores = lax.dot_general(
            wide_q[...], key_buf[row], (((1,), (1,)), ((), ())), preferred_element_type=jnp.float32
        ) * (size ** -0.5)
        spot = lax.broadcasted_iota(jnp.int32, (heads, places), 1)
        scores = jnp.where(spot < length_ref[batch, row], scores, -1e30)
        highest = jnp.maximum(jnp.max(scores, axis=1, keepdims=True), own_score)
        raised = jnp.exp(scores - highest)
        own_raised = jnp.exp(own_score - highest)
        denominator = jnp.sum(raised, axis=1, keepdims=True) + own_raised
        weights = (raised / denominator).astype(jnp.bfloat16)
        own_weight = (own_raised / denominator).astype(jnp.bfloat16).astype(jnp.float32)
        mixed = jnp.dot(weights, value_buf[row], preferred_element_type=jnp.float32)
        for slot in range(slots):
            lines = slice(slot * devices, (slot + 1) * devices)
            picked = own_weight[lines] * value_lines
            for group in range(groups):
                picked = picked + jnp.where(
                    group_of == group, mixed[lines, group * size : (group + 1) * size], 0.0
                )
            out_ref[row, :, slot * size : (slot + 1) * size] = picked.astype(jnp.bfloat16)


def attend(where, lengths, spread, cosine, sine, keys, values, queries):
    devices, rows, length = spread.shape
    places, width = keys.shape[1:]
    heads = devices * queries // HEAD_SIZE
    return pl.pallas_call(
        attend_kernel,
        out_shape=pltpu.VMEM((rows, devices, queries), jnp.bfloat16),
        in_specs=[smem(), smem()] + [vmem()] * 5,
        out_specs=vmem(),
        scratch_shapes=[
            pltpu.VMEM((rows, devices, length), jnp.float32),
            pltpu.VMEM((heads, width), jnp.bfloat16),
        ],
        compiler_params=pltpu.CompilerParams(vmem_limit_bytes=4 << 20),
        cost_estimate=pl.CostEstimate(
            flops=4 * rows * heads * places * width,
            bytes_accessed=4 * rows * places * width,
            transcendentals=rows * heads * places,
        ),
    )(
        where,
        lengths,
        spread,
        cosine,
        sine,
        placed_in(keys, pltpu.VMEM),
        placed_in(values, pltpu.VMEM),
    )


def spread_kernel(ids_ref, x_ref, w_ref, out_ref, values):
    parts, rows, chunk = out_ref.shape
    count, rows_dev, _ = x_ref.shape
    for owner in range(count):
        values[owner * rows_dev : (owner + 1) * rows_dev, :] = x_ref[owner].astype(jnp.float32)
    ready = values[...].astype(jnp.bfloat16)

    @pl.loop(0, parts // UNROLL)
    def _(group):
        for step in range(UNROLL):
            k = group * UNROLL + step
            span = span_of(ids_ref, k, chunk)
            out_ref[k] = jnp.dot(
                ready, w_ref[:, span], preferred_element_type=jnp.float32
            ).astype(jnp.bfloat16)


def spread_project(ids, values, weights):
    count, rows_dev, depth = values.shape
    rows = count * rows_dev
    chunk = weights.shape[1] // count
    parts = ids.shape[0]
    return pl.pallas_call(
        spread_kernel,
        out_shape=pltpu.VMEM((parts, rows, chunk), jnp.bfloat16),
        in_specs=[smem(), vmem(), vmem()],
        out_specs=vmem(),
        scratch_shapes=[pltpu.VMEM((rows, depth), jnp.float32)],
        compiler_params=pltpu.CompilerParams(vmem_limit_bytes=4 << 20),
        cost_estimate=pl.CostEstimate(
            flops=2 * rows * depth * parts * chunk,
            bytes_accessed=2 * depth * parts * chunk,
            transcendentals=0,
        ),
    )(ids, values, placed_in(weights, pltpu.VMEM))


def gate_up(ids_ref, first, x_ref, gain_ref, blocks, stacked, wide_x, total_ref):
    half, rows, chunk = x_ref.shape
    per_chunk = chunk // 128

    @pl.loop(0, half // UNROLL)
    def _(group):
        for step in range(UNROLL):
            place = group * UNROLL + step
            span = span_of(ids_ref, first + place, chunk)
            scaled = (x_ref[place].astype(jnp.float32) * gain_ref[:, span]).astype(jnp.bfloat16)
            for b in range(per_chunk):
                stacked[place * per_chunk + b] = scaled[:, b * 128 : (b + 1) * 128]

    line = lax.broadcasted_iota(jnp.int32, (128, 512), 0)
    column = lax.broadcasted_iota(jnp.int32, (128, 512), 1)
    aim = jnp.where(column < 256, 2 * line, 2 * line + 257)
    widen = jnp.where(column == aim, 1.0, 0.0).astype(jnp.bfloat16)

    @pl.loop(0, wide_x.shape[0])
    def _(group):
        wide = jnp.dot(
            stacked[pl.ds(group * 8, 8)].reshape(8 * rows, 128),
            widen,
            preferred_element_type=jnp.float32,
        ).astype(jnp.bfloat16)
        for b in range(8):
            lines = slice(b * rows, (b + 1) * rows)
            wide_x[group, :rows, b * 256 : (b + 1) * 256] = wide[lines, :256]
            wide_x[group, rows:, b * 256 : (b + 1) * 256] = wide[lines, 256:]

    per_group = 8 // per_chunk

    @pl.loop(0, wide_x.shape[0])
    def _(group):
        for j in range(0, len(blocks), 2):
            part = 0.0
            for step in range(per_group):
                at = (group * per_group + step) * (2 * chunk)
                span = pl.ds(pl.multiple_of(at, 2 * chunk), 2 * chunk)
                pair = jnp.concatenate([blocks[j][span, :], blocks[j + 1][span, :]], axis=1)
                part += jnp.dot(
                    wide_x[group, :, step * 2 * chunk : (step + 1) * 2 * chunk],
                    pair,
                    preferred_element_type=jnp.float32,
                )
            total_ref[:, j * 128 : (j + 2) * 128] += part


def own_half_kernel(ids_ref, own_ref, gain_ref, *refs):
    blocks, (total_ref, stacked, wide_x) = refs[:-3], refs[-3:]
    total_ref[...] = jnp.zeros_like(total_ref)
    gate_up(ids_ref, 0, own_ref, gain_ref, blocks, stacked, wide_x, total_ref)


def own_half(ids, own, gain, pairs):
    half, rows, chunk = own.shape
    units = 128 * len(pairs)
    width = 2 * half * chunk
    return pl.pallas_call(
        own_half_kernel,
        out_shape=pltpu.VMEM((2 * rows, units), jnp.float32),
        in_specs=[smem(), vmem(), vmem()] + [vmem()] * len(pairs),
        out_specs=vmem(),
        scratch_shapes=[
            pltpu.VMEM((width // 256, rows, 128), jnp.bfloat16),
            pltpu.VMEM((width // 2048, 2 * rows, 2048), jnp.bfloat16),
        ],
        compiler_params=pltpu.CompilerParams(vmem_limit_bytes=(2 << 20) + 5 * rows * width),
        cost_estimate=pl.CostEstimate(
            flops=2 * rows * units * width, bytes_accessed=2 * units * width, transcendentals=0
        ),
    )(ids, own, gain, *pairs)


def other_half_kernel(last, me_ref, ids_ref, own_ref, other_ref, gain_ref, own_total, near_ref,
                      down_hbm, *refs):
    blocks, outs, (stacked, wide_x, total, act, far_ref, sems) = refs[:-9], refs[-9:-6], refs[-6:]
    half, rows, chunk = own_ref.shape

    def far_copy(k):
        return pltpu.make_async_copy(
            down_hbm.at[:, span_of(ids_ref, half + k, chunk)], far_ref.at[k], sems.at[k]
        )

    @pl.loop(0, half)
    def _(k):
        far_copy(k).start()

    total[...] = own_total[...]
    gate_up(ids_ref, half, other_ref, gain_ref, blocks, stacked, wide_x, total)
    scale = inverse_rms((own_ref, other_ref))
    gate = total[:rows, :] * scale
    act[...] = (gate / (1.0 + jnp.exp(-gate)) * (total[rows:, :] * scale)).astype(jnp.bfloat16)

    def down(weights):
        return jnp.dot(act[...], weights, preferred_element_type=jnp.float32)

    if not last:
        send_ref, act_ref, _ = outs
        act_ref[...] = act[...]

        @pl.loop(0, half // UNROLL)
        def _(group):
            for step in range(UNROLL):
                k = group * UNROLL + step
                far_copy(k).wait()
                send_ref[k] = down(far_ref[k]).astype(jnp.bfloat16)

        return

    send_ref, keep_ref, middle_ref = outs
    rows_dev = middle_ref.shape[0]
    line = lax.broadcasted_iota(jnp.int32, (rows, 1), 0)
    first_core = lax.rem(me_ref[0], 2) == 0
    for first, x_ref in ((0, own_ref), (half, other_ref)):

        @pl.loop(0, half // UNROLL)
        def _(group):
            for step in range(UNROLL):
                k = group * UNROLL + step
                span = span_of(ids_ref, first + k, chunk)
                wide = x_ref[k].astype(jnp.float32)
                for row in range(rows_dev):
                    here = line == me_ref[0] * rows_dev + row
                    middle_ref[row : row + 1, span] = jnp.sum(
                        jnp.where(here, wide, 0.0), axis=0, keepdims=True
                    )
                if first:
                    far_copy(k).wait()
                part = down(far_ref[k] if first else near_ref[k])
                for chip in range(half):
                    at = 2 * chip * rows_dev
                    low = part[at : at + rows_dev]
                    high = part[at + rows_dev : at + 2 * rows_dev]
                    keep_ref[chip, :, span] = jnp.where(first_core, low, high).astype(jnp.bfloat16)
                    send_ref[chip, :, span] = jnp.where(first_core, high, low).astype(jnp.bfloat16)


def other_half(last, me, ids, own, other, gain, own_total, near, down, pairs):
    half, rows, chunk = own.shape
    units, width = down.shape
    rows_dev = rows // (2 * half)
    if last:
        shapes = [((half, rows_dev, width), jnp.bfloat16)] * 2 + [((rows_dev, width), jnp.float32)]
    else:
        shapes = [(own.shape, jnp.bfloat16), ((rows, units), jnp.bfloat16), ((8, 128), jnp.float32)]
    return pl.pallas_call(
        functools.partial(other_half_kernel, last),
        out_shape=[pltpu.VMEM(shape, kind) for shape, kind in shapes],
        in_specs=[smem(), smem()] + [vmem()] * 5 + [hbm()] + [vmem()] * len(pairs),
        out_specs=[vmem()] * 3,
        scratch_shapes=[
            pltpu.VMEM((width // 256, rows, 128), jnp.bfloat16),
            pltpu.VMEM((width // 2048, 2 * rows, 2048), jnp.bfloat16),
            pltpu.VMEM((2 * rows, units), jnp.float32),
            pltpu.VMEM((rows, units), jnp.bfloat16),
            pltpu.VMEM((half, units, chunk), jnp.bfloat16),
            pltpu.SemaphoreType.DMA((half,)),
        ],
        compiler_params=pltpu.CompilerParams(
            vmem_limit_bytes=(2 << 20) + 5 * rows * width + (10 * rows + width) * units
        ),
        cost_estimate=pl.CostEstimate(
            flops=4 * rows * units * width, bytes_accessed=3 * units * width, transcendentals=0
        ),
    )(me, ids, own, other, gain, own_total, near, placed_in(down, pltpu.HBM), *pairs)


def keep_kernel(act_ref, near_ref, out_ref):
    @pl.loop(0, out_ref.shape[0] // UNROLL)
    def _(group):
        for step in range(UNROLL):
            k = group * UNROLL + step
            out_ref[k] = jnp.dot(
                act_ref[...], near_ref[k], preferred_element_type=jnp.float32
            ).astype(jnp.bfloat16)


def keep_half(act, near):
    rows = act.shape[0]
    half, _, chunk = near.shape
    return pl.pallas_call(
        keep_kernel,
        out_shape=pltpu.VMEM((half, rows, chunk), jnp.bfloat16),
        in_specs=[vmem(), vmem()],
        out_specs=vmem(),
        compiler_params=pltpu.CompilerParams(vmem_limit_bytes=4 << 20),
        cost_estimate=pl.CostEstimate(
            flops=2 * rows * near.size, bytes_accessed=2 * near.size, transcendentals=0
        ),
    )(act, near)


def turning(positions):
    half_dim = HEAD_SIZE // 2
    frequency = 500000.0 ** (-2.0 * jnp.arange(half_dim, dtype=jnp.float32) / HEAD_SIZE)
    angles = positions.astype(jnp.float32)[:, None] * frequency[None, :]
    cosine = jnp.cos(angles)
    sine = jnp.sin(angles)
    return jnp.concatenate([cosine, cosine], axis=1), jnp.concatenate([-sine, sine], axis=1)


def body(
    hidden,
    attn_gain,
    w_query,
    w_key,
    w_value,
    w_out,
    mlp_gain,
    w_gate_up,
    w_down,
    key_cache,
    value_cache,
    lengths,
):
    rows_dev = hidden.shape[1]
    count = lax.axis_size("mp")
    section_index = lax.axis_index("section")
    model_index = lax.axis_index("mp")
    width = hidden.shape[2]
    near = jnp.asarray(relative_ids())
    near_places, far_places = near ^ model_index, near ^ model_index ^ 1
    places = jnp.concatenate([near_places, far_places])
    wk = w_key[0].T
    wv = w_value[0].T
    blocks = w_gate_up.shape[3] // 128
    windows = len(chip_masks())
    bounds = [(4 * blocks * step + windows) // (2 * windows) for step in range(windows + 1)]
    batches = [
        jnp.remainder(section_index + turn_index, 2).astype(jnp.int32).reshape(1)
        for turn_index in range(2)
    ]

    tables = [
        turning(lax.dynamic_index_in_dim(lengths, batch[0], 0, keepdims=False))
        for batch in batches
    ]
    me = model_index.astype(jnp.int32).reshape(1)
    early = (places, near_places, far_places, me, *batches, *tables[0], *tables[1])

    def attention_jobs(turn_index):
        got = {}

        def projections(token):
            got["qkv"] = fetch((token,), w_query[0], wk, wv)
            return got["qkv"]

        def out_projection(token):
            got["out"] = fetch((token,), w_out[0])
            return got["out"]

        def caches(token):
            tokens = (token,) if turn_index else (token, *early)
            got["caches"] = fetch_caches(tokens, batches[turn_index], key_cache[0], value_cache[0])
            return got["caches"]

        return got, [caches, projections, out_projection]

    got, jobs = attention_jobs(0)
    own, other = gather_doubling(hidden[0], jobs)
    for turn_index in range(2):
        last = turn_index == 1
        batch = batches[turn_index]
        joined, by_owner = project(places, own, other, attn_gain, *got["qkv"])
        spread = lax.all_to_all(joined, "mp", split_axis=0, concat_axis=0)
        mixed = attend(
            batch, lengths, spread, *tables[turn_index], *got["caches"], w_query.shape[2]
        )
        heads_out = lax.all_to_all(mixed.transpose(1, 0, 2), "mp", split_axis=0, concat_axis=0)
        got_core = swap(spread_project(far_places, heads_out, *got["out"]), 1)
        keep = spread_project(near_places, heads_out, *got["out"])
        pairs = {}

        def pair_job(new):
            def job(token):
                if not new:
                    return ()
                arrays = fetch_pairs(token, places, w_gate_up[0], new)
                pairs.update(zip(new, arrays))
                return arrays

            return job

        items = [(side, block) for side in range(2) for block in range(blocks)]
        jobs = [pair_job(items[low:high]) for low, high in zip(bounds, bounds[1:])]
        near_down = []

        def down_job(token):
            near_down.extend(fetch_chunks(token, near_places, w_down[0], width // count))
            return near_down

        jobs.append(down_job)
        addend = by_owner if turn_index == 0 else mine
        middle, own, other = reduce_to_all(keep, got_core, addend, jobs, False)
        near_pairs, far_pairs = (
            [
                placed_in(pairs[side, block].reshape(width, 128), pltpu.VMEM)
                for block in range(blocks)
            ]
            for side in range(2)
        )
        own_total = own_half(places, own, mlp_gain, near_pairs)
        send, act, own_rows = other_half(
            last, me, places, own, other, mlp_gain, own_total, near_down[0], w_down[0], far_pairs
        )
        if last:
            mine = (own_rows + scatter(send, act)).astype(jnp.bfloat16)
        else:
            got, jobs = attention_jobs(1)
            got_core = swap(send, 1)
            keep = keep_half(act, near_down[0])
            mine, own, other = reduce_to_all(keep, got_core, middle, jobs, True)
    return mine[None]


def solution(mesh):
    placed = (
        P("section", "mp", None),
        P("section", None),
        P("section", None, "mp"),
        P("section", None, "mp"),
        P("section", None, "mp"),
        P("section", "mp", None),
        P("section", None),
        P("section", None, None, "mp"),
        P("section", "mp", None),
        P("section", None, "mp", None, None),
        P("section", None, "mp", None, None),
        P(None, "mp"),
    )
    return jax.shard_map(
        body, mesh=mesh, in_specs=placed, out_specs=P("section", "mp", None), check_vma=False
    )
```

```python
import functools

import jax
import jax.numpy as jnp
import numpy as np
from jax import lax
from jax.experimental import pallas as pl
from jax.experimental.pallas import tpu as pltpu
from jax.sharding import PartitionSpec as P

QUERY_HEADS = 64
KEY_VALUE_HEADS = 8
HEAD_SIZE = 128

epsilon = 1e-05

UNROLL = 4


def swap(value, mask, axis="mp"):
    count = lax.axis_size(axis)
    return lax.ppermute(value, axis, [(source, source ^ mask) for source in range(count)])


def exchange(parts):
    count = lax.axis_size("mp")
    groups = [list(range(core, count, 2)) for core in range(2)]
    return lax.all_to_all(
        parts, "mp", split_axis=0, concat_axis=0, axis_index_groups=groups, tiled=True
    )


def chip_masks():
    return [1 << bit for bit in range(1, (lax.axis_size("mp") - 1).bit_length())]


def relative_ids():
    ids = np.zeros((1,), np.int32)
    for mask in reversed(chip_masks()):
        ids = np.concatenate([ids, ids ^ mask])
    return ids


def vmem():
    return pl.BlockSpec(memory_space=pltpu.VMEM)


def smem():
    return pl.BlockSpec(memory_space=pltpu.SMEM)


def placed_in(values, space):
    return pltpu.with_memory_space_constraint(values, space)


def hbm():
    return pl.BlockSpec(memory_space=pl.ANY)


def run_copies(copies):
    for at, copy in enumerate(copies):
        copy.start(priority=at % 2)
    for copy in copies:
        copy.wait()


def fetch_kernel(pieces, tokens, *refs):
    arrays = len(pieces)
    refs, sems = refs[tokens:-1], refs[-1]
    copies = []
    for array, (count, source, target) in enumerate(zip(pieces, refs, refs[arrays:])):
        size = source.shape[0] // count
        for piece in range(count):
            span = pl.ds(piece * size, size)
            copies.append(
                pltpu.make_async_copy(source.at[span], target.at[span], sems.at[array, piece])
            )
    run_copies(copies)


def fetch(tokens, *arrays):
    pieces = [8 if array.shape[0] % 128 == 0 else 1 for array in arrays]
    return pl.pallas_call(
        functools.partial(fetch_kernel, pieces, len(tokens)),
        out_shape=[pltpu.VMEM(array.shape, array.dtype) for array in arrays],
        in_specs=[hbm()] * (len(tokens) + len(arrays)),
        out_specs=[vmem()] * len(arrays),
        scratch_shapes=[pltpu.SemaphoreType.DMA((len(arrays), 8))],
        compiler_params=pltpu.CompilerParams(vmem_limit_bytes=1 << 20),
        cost_estimate=pl.CostEstimate(
            flops=0, bytes_accessed=sum(2 * array.size for array in arrays), transcendentals=0
        ),
    )(*tokens, *[placed_in(array, pltpu.HBM) for array in arrays])


def fetch_caches_kernel(where_ref, keys_ref, values_ref, *refs):
    key_ref, value_ref, sems = refs[-3:]
    rows, places, _ = key_ref.shape
    batch = where_ref[0]
    copies = []
    for array, (source, target) in enumerate(((keys_ref, key_ref), (values_ref, value_ref))):
        for row in range(rows):
            for piece in range(2):
                span = pl.ds(piece * (places // 2), places // 2)
                copies.append(
                    pltpu.make_async_copy(
                        source.at[batch, row, span],
                        target.at[row, span],
                        sems.at[array, row, piece],
                    )
                )
    run_copies(copies)


def fetch_caches(tokens, where, keys, values):
    shape = pltpu.VMEM(keys.shape[1:], keys.dtype)
    return pl.pallas_call(
        fetch_caches_kernel,
        out_shape=[shape, shape],
        in_specs=[smem(), hbm(), hbm()] + [hbm()] * len(tokens),
        out_specs=[vmem(), vmem()],
        scratch_shapes=[pltpu.SemaphoreType.DMA((2, keys.shape[1], 2))],
        compiler_params=pltpu.CompilerParams(vmem_limit_bytes=1 << 20),
        cost_estimate=pl.CostEstimate(
            flops=0, bytes_accessed=2 * keys.size, transcendentals=0
        ),
    )(where, placed_in(keys, pltpu.HBM), placed_in(values, pltpu.HBM), *tokens)


def fetch_pairs_kernel(items, ids_ref, token_ref, source, *refs):
    targets, sems = refs[:-1], refs[-1]
    half = sems.shape[1]
    chunk = targets[0].shape[0] // half
    copies = []
    for at, ((side, block), target) in enumerate(zip(items, targets)):
        for k in range(half):
            copies.append(
                pltpu.make_async_copy(
                    source.at[
                        span_of(ids_ref, side * half + k, chunk), :, pl.ds(block * 128, 128)
                    ],
                    target.at[pl.ds(k * chunk, chunk)],
                    sems.at[at, k],
                )
            )
    run_copies(copies)


def fetch_pairs(token, ids, weights, items):
    half = ids.shape[0] // 2
    size = weights.shape[0] // 2
    return pl.pallas_call(
        functools.partial(fetch_pairs_kernel, items),
        out_shape=[pltpu.VMEM((size, 2, 128), weights.dtype)] * len(items),
        in_specs=[smem(), hbm(), hbm()],
        out_specs=[vmem()] * len(items),
        scratch_shapes=[pltpu.SemaphoreType.DMA((len(items), half))],
        compiler_params=pltpu.CompilerParams(vmem_limit_bytes=1 << 20),
        cost_estimate=pl.CostEstimate(
            flops=0, bytes_accessed=4 * len(items) * size * 128, transcendentals=0
        ),
    )(ids, token, placed_in(weights, pltpu.HBM))


def in_vmem(arrays):
    return [placed_in(x, pltpu.VMEM) if x.size > 1 << 14 else x for x in arrays]


def step_call(kernel, shapes, operands, held_back):
    return pl.pallas_call(
        kernel,
        out_shape=[pltpu.VMEM(shape, jnp.bfloat16) for shape in shapes],
        in_specs=[vmem()] * len(operands) + [hbm()] * len(held_back),
        out_specs=[vmem()] * len(shapes),
        compiler_params=pltpu.CompilerParams(vmem_limit_bytes=4 << 20),
        cost_estimate=pl.CostEstimate(
            flops=2 * operands[-1].size, bytes_accessed=6 * operands[-1].size, transcendentals=0
        ),
    )(*operands, *in_vmem(held_back))


def add_kernel(outs, operands, *refs):
    targets = refs[-outs:]
    share = targets[0].shape[0]
    for which, target in enumerate(targets):
        for place in range(share):
            total = 0.0
            for ref in refs[:operands]:
                total += ref[which * share + place].astype(jnp.float32)
            target[place] = total.astype(jnp.bfloat16)


def add_parts(operands, outs, held_back=()):
    lead = operands[0].shape[0]
    shape = (lead // outs,) + operands[0].shape[1:]
    return step_call(
        functools.partial(add_kernel, outs, len(operands)), [shape] * outs, operands, held_back
    )


def cross_kernel(addend_ref, here_ref, there_ref, *refs):
    out_ref = refs[-1]
    for place in range(2):
        if len(addend_ref.shape) == 3:
            addend = addend_ref[place].astype(jnp.float32)
        else:
            owners = range(addend_ref.shape[1])
            parts = [addend_ref[place, owner].astype(jnp.float32) for owner in owners]
            addend = jnp.concatenate(parts, axis=0)
        out_ref[place] = (
            addend
            + here_ref[place].astype(jnp.float32)
            + there_ref[1 - place].astype(jnp.float32)
        ).astype(jnp.bfloat16)


def join_kernel(low_ref, high_ref, *refs):
    half = low_ref.shape[0]
    out_ref = refs[-1]
    for place in range(half):
        out_ref[place] = low_ref[place]
        out_ref[half + place] = high_ref[place]


def join(low, high, held_back=()):
    shape = (2 * low.shape[0],) + low.shape[1:]
    return step_call(join_kernel, [shape], (low, high), held_back)[0]


def run_job(jobs, token):
    return jobs.pop(0)(token) if jobs else ()


def scatter(send, keep):
    (held,) = add_parts((keep, swap(send, 1)), 1)
    return jnp.sum(exchange(held).astype(jnp.float32), axis=0)


def halve(keep, got, jobs):
    held_back = ()
    for mask in chip_masks()[:-1]:
        keep, send = add_parts((keep, got), 2, held_back)
        got = swap(send, mask)
        held_back = run_job(jobs, send)
    return keep, got, held_back


def hop(part, mask):
    count = lax.axis_size("mp")
    pairs = [(source, ((source + count) % (2 * count)) ^ mask) for source in range(2 * count)]
    return lax.ppermute(part, ("section", "mp"), pairs)


def reduce_to_pair(keep, got, addend, jobs, hops):
    keep, got, held_back = halve(keep, got, jobs)
    (held,) = add_parts((keep, got), 1, held_back)
    far = chip_masks()[-1]
    here = hop(held, 0) if hops else held
    there = hop(held, far) if hops else swap(held, far)
    if hops:
        addend = hop(addend, 0)
    return step_call(cross_kernel, [held.shape], (addend, here, there), run_job(jobs, held))[0]


def spread_pair(pair, jobs):
    held = pair
    for mask in reversed(chip_masks()[1:-1]):
        got = swap(held, mask)
        held = join(held, got, run_job(jobs, held))
    got = swap(held, chip_masks()[0])
    return held, swap(held, 1), got


def all_quarters(quarters):
    return *quarters, swap(quarters[2], 1)


def pass_kernel(in_ref, *refs):
    refs[-1][...] = in_ref[...]


def gather_doubling(part, jobs):
    held = part[None]
    got = swap(held, chip_masks()[-1])
    return spread_pair(join(held, got, run_job(jobs, held)), jobs)


def quarter_starts(count):
    return 0, count // 2, count // 4, count // 2 + count // 4


def inverse_rms(x_refs):
    parts, rows, chunk = x_refs[0].shape
    total = jnp.zeros((rows, chunk), jnp.float32)
    for x_ref in x_refs:

        def add(group, total):
            for step in range(UNROLL):
                wide = x_ref[group * UNROLL + step].astype(jnp.float32)
                total = total + wide * wide
            return total

        total = lax.fori_loop(0, parts // UNROLL, add, total)
    mean = jnp.sum(total, axis=-1, keepdims=True) / (4 * parts * chunk)
    return lax.rsqrt(mean + epsilon)


def span_of(ids_ref, k, chunk):
    return pl.ds(pl.multiple_of(ids_ref[k] * chunk, chunk), chunk)


def normed_chunk(x_ref, gain_ref, scale, k, span):
    wide = x_ref[k].astype(jnp.float32)
    return (wide * scale * gain_ref[:, span]).astype(jnp.bfloat16)


def project_kernel(ids_ref, *refs):
    x_refs, (gain_ref, wq_ref, wk_ref, wv_ref) = refs[:4], refs[4:8]
    out_ref, mine_ref, q_sum, kv_sum, wide = refs[-5:]
    queries = wq_ref.shape[1]
    count, rows_dev, _ = out_ref.shape
    quarter = count // 4
    by_rows = x_refs[0].shape[1] == rows_dev
    chunk = wq_ref.shape[0] // count
    starts = quarter_starts(count)
    if by_rows:
        for first, x_ref in zip(starts, x_refs):
            for place in range(quarter):
                at = (first + place) * rows_dev
                wide[at : at + rows_dev, :] = x_ref[place].astype(jnp.float32)
        total = 0.0
        for k in range(count):
            part = wide[:, k * chunk : (k + 1) * chunk]
            total += part * part
        mean = jnp.sum(total, axis=-1, keepdims=True) / (count * chunk)
        scale = lax.rsqrt(mean + epsilon)
    else:
        scale = inverse_rms(x_refs)
    q_sum[...] = jnp.zeros_like(q_sum)
    kv_sum[...] = jnp.zeros_like(kv_sum)
    for first, x_ref in zip(starts, x_refs):

        @pl.loop(0, quarter // UNROLL)
        def _(group):
            q_part = 0.0
            kv_part = 0.0
            for step in range(UNROLL):
                k = group * UNROLL + step
                if by_rows:
                    span = pl.ds(pl.multiple_of((first + k) * chunk, chunk), chunk)
                    normed = (wide[:, span] * scale * gain_ref[:, span]).astype(jnp.bfloat16)
                else:
                    span = span_of(ids_ref, first + k, chunk)
                    normed = normed_chunk(x_ref, gain_ref, scale, k, span)
                q_part += jnp.dot(normed, wq_ref[span, :], preferred_element_type=jnp.float32)
                kv_part += lax.dot_general(
                    normed,
                    jnp.concatenate([wk_ref[:, span], wv_ref[:, span]], axis=0),
                    (((1,), (1,)), ((), ())),
                    preferred_element_type=jnp.float32,
                )
            q_sum[...] += q_part
            kv_sum[...] += kv_part

    for place in range(count):
        owner = ids_ref[place] if by_rows else place
        lines = slice(place * rows_dev, (place + 1) * rows_dev)
        out_ref[owner, :, :queries] = q_sum[lines, :].astype(jnp.bfloat16)
        out_ref[owner, :, queries:] = kv_sum[lines, :].astype(jnp.bfloat16)
        if by_rows:
            for which in range(2):
                span = span_of(ids_ref, which, chunk)
                mine_ref[which, owner] = wide[lines, span].astype(jnp.bfloat16)


def project(ids, quarters, gain, wq, wk, wv, held_back):
    count = ids.shape[0]
    width, queries = wq.shape
    keys = wk.shape[0]
    size = queries + 2 * keys
    rows_dev = 4 * quarters[0].size // (count * width)
    rows = count * rows_dev
    by_rows = quarters[0].shape[1] == rows_dev
    return pl.pallas_call(
        project_kernel,
        out_shape=[
            pltpu.VMEM((count, rows_dev, size), jnp.bfloat16),
            pltpu.VMEM((2, count, rows_dev, width // count), jnp.bfloat16),
        ],
        in_specs=[smem()] + [vmem()] * 8 + [hbm()] * len(held_back),
        out_specs=[vmem(), vmem()],
        scratch_shapes=[
            pltpu.VMEM((rows, queries), jnp.float32),
            pltpu.VMEM((rows, 2 * keys), jnp.float32),
            pltpu.VMEM((rows, width if by_rows else 128), jnp.float32),
        ],
        compiler_params=pltpu.CompilerParams(vmem_limit_bytes=(3 << 20) + 4 * rows * width),
        cost_estimate=pl.CostEstimate(
            flops=2 * rows * width * size, bytes_accessed=2 * width * size, transcendentals=0
        ),
    )(ids, *quarters, gain, *in_vmem((wq, wk, wv, *held_back)))


def attend_kernel(where_ref, length_ref, in_ref, cos_ref, sin_ref, key_buf, value_buf, out_ref,
                  lined, wide_q):
    rows, devices, queries = out_ref.shape
    width = key_buf.shape[2]
    keys = (in_ref.shape[2] - queries) // 2
    size = cos_ref.shape[1]
    groups = width // size
    pieces = size // keys
    slots = queries // size
    heads = devices * slots
    places = key_buf.shape[1]
    batch = where_ref[0]

    for device in range(devices):
        wide = in_ref[device].astype(jnp.float32)
        for row in range(rows):
            lined[row, device : device + 1, :] = wide[row : row + 1]
    line = lax.broadcasted_iota(jnp.int32, (devices, 1), 0)
    group_of = line * groups // devices
    for row in range(rows):
        cosine = cos_ref[pl.ds(row, 1), :]
        sine = sin_ref[pl.ds(row, 1), :]

        def turned(wide):
            other = jnp.concatenate([wide[:, size // 2 :], wide[:, : size // 2]], axis=1)
            return (wide * cosine + other * sine).astype(jnp.bfloat16).astype(jnp.float32)

        key_lines = jnp.zeros((devices, size), jnp.float32)
        value_lines = jnp.zeros((devices, size), jnp.float32)
        for group in range(groups):
            own_key, own_value = (
                jnp.concatenate(
                    [
                        lined[row, device : device + 1, at : at + keys]
                        for device in range(group * pieces, (group + 1) * pieces)
                    ],
                    axis=1,
                )
                for at in (queries, queries + keys)
            )
            here = group_of == group
            key_lines = jnp.where(here, turned(own_key), key_lines)
            value_lines = jnp.where(here, own_value, value_lines)
        own_parts = []
        for slot in range(slots):
            part = turned(lined[row, :, slot * size : (slot + 1) * size])
            own_parts.append(jnp.sum(part * key_lines, axis=1, keepdims=True))
            for group in range(groups):
                wide_q[
                    slot * devices : (slot + 1) * devices, group * size : (group + 1) * size
                ] = jnp.where(group_of == group, part, 0.0).astype(jnp.bfloat16)
        own_score = jnp.concatenate(own_parts, axis=0) * (size ** -0.5)
        scores = lax.dot_general(
            wide_q[...], key_buf[row], (((1,), (1,)), ((), ())), preferred_element_type=jnp.float32
        ) * (size ** -0.5)
        spot = lax.broadcasted_iota(jnp.int32, (heads, places), 1)
        scores = jnp.where(spot < length_ref[batch, row], scores, -1e30)
        highest = jnp.maximum(jnp.max(scores, axis=1, keepdims=True), own_score)
        raised = jnp.exp(scores - highest)
        own_raised = jnp.exp(own_score - highest)
        denominator = jnp.sum(raised, axis=1, keepdims=True) + own_raised
        weights = (raised / denominator).astype(jnp.bfloat16)
        own_weight = (own_raised / denominator).astype(jnp.bfloat16).astype(jnp.float32)
        mixed = jnp.dot(weights, value_buf[row], preferred_element_type=jnp.float32)
        for slot in range(slots):
            lines = slice(slot * devices, (slot + 1) * devices)
            picked = own_weight[lines] * value_lines
            for group in range(groups):
                picked = picked + jnp.where(
                    group_of == group, mixed[lines, group * size : (group + 1) * size], 0.0
                )
            out_ref[row, :, slot * size : (slot + 1) * size] = picked.astype(jnp.bfloat16)


def attend(where, lengths, spread, cosine, sine, keys, values, queries):
    devices, rows, length = spread.shape
    places, width = keys.shape[1:]
    heads = devices * queries // HEAD_SIZE
    return pl.pallas_call(
        attend_kernel,
        out_shape=pltpu.VMEM((rows, devices, queries), jnp.bfloat16),
        in_specs=[smem(), smem()] + [vmem()] * 5,
        out_specs=vmem(),
        scratch_shapes=[
            pltpu.VMEM((rows, devices, length), jnp.float32),
            pltpu.VMEM((heads, width), jnp.bfloat16),
        ],
        compiler_params=pltpu.CompilerParams(vmem_limit_bytes=4 << 20),
        cost_estimate=pl.CostEstimate(
            flops=4 * rows * heads * places * width,
            bytes_accessed=4 * rows * places * width,
            transcendentals=rows * heads * places,
        ),
    )(
        where,
        lengths,
        spread,
        cosine,
        sine,
        placed_in(keys, pltpu.VMEM),
        placed_in(values, pltpu.VMEM),
    )


def spread_kernel(ids_ref, x_ref, w_ref, out_ref, values):
    parts, rows, chunk = out_ref.shape
    count, rows_dev, _ = x_ref.shape
    for owner in range(count):
        values[owner * rows_dev : (owner + 1) * rows_dev, :] = x_ref[owner].astype(jnp.float32)
    ready = values[...].astype(jnp.bfloat16)

    @pl.loop(0, parts // UNROLL)
    def _(group):
        for step in range(UNROLL):
            k = group * UNROLL + step
            span = span_of(ids_ref, k, chunk)
            out_ref[k] = jnp.dot(
                ready, w_ref[:, span], preferred_element_type=jnp.float32
            ).astype(jnp.bfloat16)


def spread_project(ids, values, weights):
    count, rows_dev, depth = values.shape
    rows = count * rows_dev
    chunk = weights.shape[1] // count
    parts = ids.shape[0]
    return pl.pallas_call(
        spread_kernel,
        out_shape=pltpu.VMEM((parts, rows, chunk), jnp.bfloat16),
        in_specs=[smem(), vmem(), vmem()],
        out_specs=vmem(),
        scratch_shapes=[pltpu.VMEM((rows, depth), jnp.float32)],
        compiler_params=pltpu.CompilerParams(vmem_limit_bytes=4 << 20),
        cost_estimate=pl.CostEstimate(
            flops=2 * rows * depth * parts * chunk,
            bytes_accessed=2 * depth * parts * chunk,
            transcendentals=0,
        ),
    )(ids, values, placed_in(weights, pltpu.VMEM))


def gate_up(ids_ref, first, x_ref, gain_ref, blocks, stacked, wide_x, total_ref):
    parts, rows, chunk = x_ref.shape
    per_chunk = chunk // 128
    base = first % (2 * parts)

    @pl.loop(0, parts // UNROLL)
    def _(group):
        for step in range(UNROLL):
            place = group * UNROLL + step
            span = span_of(ids_ref, first + place, chunk)
            scaled = (x_ref[place].astype(jnp.float32) * gain_ref[:, span]).astype(jnp.bfloat16)
            for b in range(per_chunk):
                stacked[place * per_chunk + b] = scaled[:, b * 128 : (b + 1) * 128]

    line = lax.broadcasted_iota(jnp.int32, (128, 512), 0)
    column = lax.broadcasted_iota(jnp.int32, (128, 512), 1)
    aim = jnp.where(column < 256, 2 * line, 2 * line + 257)
    widen = jnp.where(column == aim, 1.0, 0.0).astype(jnp.bfloat16)
    groups = parts * per_chunk // 8
    for group in range(groups):
        wide = jnp.dot(
            stacked[group * 8 : (group + 1) * 8].reshape(8 * rows, 128),
            widen,
            preferred_element_type=jnp.float32,
        ).astype(jnp.bfloat16)
        for b in range(8):
            lines = slice(b * rows, (b + 1) * rows)
            wide_x[group, :rows, b * 256 : (b + 1) * 256] = wide[lines, :256]
            wide_x[group, rows:, b * 256 : (b + 1) * 256] = wide[lines, 256:]

    per_group = 8 // per_chunk

    @pl.loop(0, groups)
    def _(group):
        for j in range(0, len(blocks), 2):
            part = 0.0
            for step in range(per_group):
                at = (base + group * per_group + step) * (2 * chunk)
                span = pl.ds(pl.multiple_of(at, 2 * chunk), 2 * chunk)
                pair = jnp.concatenate([blocks[j][span, :], blocks[j + 1][span, :]], axis=1)
                part += jnp.dot(
                    wide_x[group, :, step * 2 * chunk : (step + 1) * 2 * chunk],
                    pair,
                    preferred_element_type=jnp.float32,
                )
            total_ref[:, j * 128 : (j + 2) * 128] += part


def down_copies(ids_ref, first, source, target, sems):
    count, _, chunk = target.shape

    def copy(k):
        return pltpu.make_async_copy(
            source.at[:, span_of(ids_ref, first + k, chunk)], target.at[k], sems.at[k]
        )

    return [copy(k) for k in range(count)]


def quarter_kernel(first, fetch_first, ids_ref, x_ref, gain_ref, before_ref, down_hbm, *refs):
    blocks, (total_ref, down_ref, stacked, wide_x, sems) = refs[:-5], refs[-5:]
    copies = []
    if fetch_first is not None:
        copies = down_copies(ids_ref, fetch_first, down_hbm, down_ref, sems)
    for copy in copies:
        copy.start()
    if first:
        total_ref[...] = before_ref[...]
    else:
        total_ref[...] = jnp.zeros_like(total_ref)
    gate_up(ids_ref, first, x_ref, gain_ref, blocks, stacked, wide_x, total_ref)
    for copy in copies:
        copy.wait()


def quarter(first, fetch_first, ids, x, gain, before, down, pairs):
    parts, rows, chunk = x.shape
    units, width = down.shape
    got = (parts, units, chunk) if fetch_first is not None else (1, 8, 128)
    return pl.pallas_call(
        functools.partial(quarter_kernel, first, fetch_first),
        out_shape=[
            pltpu.VMEM((2 * rows, units), jnp.float32),
            pltpu.VMEM(got, jnp.bfloat16),
        ],
        in_specs=[smem()] + [vmem()] * 3 + [hbm()] + [vmem()] * len(pairs),
        out_specs=[vmem(), vmem()],
        scratch_shapes=[
            pltpu.VMEM((width // 512, rows, 128), jnp.bfloat16),
            pltpu.VMEM((width // 4096, 2 * rows, 2048), jnp.bfloat16),
            pltpu.SemaphoreType.DMA((parts,)),
        ],
        compiler_params=pltpu.CompilerParams(vmem_limit_bytes=(2 << 20) + 5 * rows * width // 2),
        cost_estimate=pl.CostEstimate(
            flops=rows * units * width, bytes_accessed=units * width, transcendentals=0
        ),
    )(ids, x, gain, before, placed_in(down, pltpu.HBM), *pairs)


def finish_kernel(last, me_ref, ids_ref, *refs):
    x_refs, (gain_ref, before_ref, low_ref, high_ref, down_hbm) = refs[:4], refs[4:9]
    blocks, outs, (stacked, wide_x, total, act, far_ref, sems) = refs[9:-9], refs[-9:-6], refs[-6:]
    parts, rows, chunk = x_refs[0].shape
    half = 2 * parts
    copies = down_copies(ids_ref, half, down_hbm, far_ref, sems)
    for copy in copies:
        copy.start()
    total[...] = before_ref[...]
    starts = quarter_starts(2 * half)
    gate_up(ids_ref, starts[3], x_refs[3], gain_ref, blocks, stacked, wide_x, total)
    scale = inverse_rms(x_refs)
    gate = total[:rows, :] * scale
    act[...] = (gate / (1.0 + jnp.exp(-gate)) * (total[rows:, :] * scale)).astype(jnp.bfloat16)

    def down(weights):
        return jnp.dot(act[...], weights, preferred_element_type=jnp.float32)

    for copy in copies:
        copy.wait()
    if not last:
        send_ref, act_ref, _ = outs
        act_ref[...] = act[...]

        @pl.loop(0, half // UNROLL)
        def _(group):
            for step in range(UNROLL):
                k = group * UNROLL + step
                send_ref[k] = down(far_ref[k]).astype(jnp.bfloat16)

        return

    send_ref, keep_ref, middle_ref = outs
    rows_dev = middle_ref.shape[0]
    line = lax.broadcasted_iota(jnp.int32, (rows, 1), 0)
    first_core = lax.rem(me_ref[0], 2) == 0
    for which, (first, x_ref) in enumerate(zip(starts, x_refs)):

        @pl.loop(0, parts // UNROLL)
        def _(group):
            for step in range(UNROLL):
                k = group * UNROLL + step
                span = span_of(ids_ref, first + k, chunk)
                wide = x_ref[k].astype(jnp.float32)
                for row in range(rows_dev):
                    here = line == me_ref[0] * rows_dev + row
                    middle_ref[row : row + 1, span] = jnp.sum(
                        jnp.where(here, wide, 0.0), axis=0, keepdims=True
                    )
                if which % 2:
                    part = down(far_ref[first - half + k])
                else:
                    part = down((high_ref if which else low_ref)[k])
                for chip in range(half):
                    at = 2 * chip * rows_dev
                    low = part[at : at + rows_dev]
                    high = part[at + rows_dev : at + 2 * rows_dev]
                    keep_ref[chip, :, span] = jnp.where(first_core, low, high).astype(jnp.bfloat16)
                    send_ref[chip, :, span] = jnp.where(first_core, high, low).astype(jnp.bfloat16)


def finish(last, me, ids, quarters, gain, before, low, high, down, pairs):
    parts, rows, chunk = quarters[0].shape
    half = 2 * parts
    units, width = down.shape
    rows_dev = rows // (2 * half)
    if last:
        shapes = [((half, rows_dev, width), jnp.bfloat16)] * 2 + [((rows_dev, width), jnp.float32)]
    else:
        shapes = [
            ((half, rows, chunk), jnp.bfloat16),
            ((rows, units), jnp.bfloat16),
            ((8, 128), jnp.float32),
        ]
    return pl.pallas_call(
        functools.partial(finish_kernel, last),
        out_shape=[pltpu.VMEM(shape, kind) for shape, kind in shapes],
        in_specs=[smem(), smem()] + [vmem()] * 8 + [hbm()] + [vmem()] * len(pairs),
        out_specs=[vmem()] * 3,
        scratch_shapes=[
            pltpu.VMEM((width // 512, rows, 128), jnp.bfloat16),
            pltpu.VMEM((width // 4096, 2 * rows, 2048), jnp.bfloat16),
            pltpu.VMEM((2 * rows, units), jnp.float32),
            pltpu.VMEM((rows, units), jnp.bfloat16),
            pltpu.VMEM((half, units, chunk), jnp.bfloat16),
            pltpu.SemaphoreType.DMA((half,)),
        ],
        compiler_params=pltpu.CompilerParams(
            vmem_limit_bytes=(2 << 20) + 5 * rows * width // 2 + (10 * rows + width) * units
        ),
        cost_estimate=pl.CostEstimate(
            flops=3 * rows * units * width, bytes_accessed=2 * units * width, transcendentals=0
        ),
    )(
        me,
        ids,
        *quarters,
        gain,
        before,
        *in_vmem((low, high)),
        placed_in(down, pltpu.HBM),
        *pairs,
    )


def keep_kernel(act_ref, low_ref, high_ref, out_ref):
    parts = low_ref.shape[0]
    for first, near_ref in ((0, low_ref), (parts, high_ref)):

        @pl.loop(0, parts // UNROLL)
        def _(group):
            for step in range(UNROLL):
                k = group * UNROLL + step
                out_ref[first + k] = jnp.dot(
                    act_ref[...], near_ref[k], preferred_element_type=jnp.float32
                ).astype(jnp.bfloat16)


def keep_half(act, low, high):
    rows = act.shape[0]
    parts, _, chunk = low.shape
    return pl.pallas_call(
        keep_kernel,
        out_shape=pltpu.VMEM((2 * parts, rows, chunk), jnp.bfloat16),
        in_specs=[vmem(), vmem(), vmem()],
        out_specs=vmem(),
        compiler_params=pltpu.CompilerParams(vmem_limit_bytes=4 << 20),
        cost_estimate=pl.CostEstimate(
            flops=4 * rows * low.size, bytes_accessed=4 * low.size, transcendentals=0
        ),
    )(act, *in_vmem((low, high)))


def turning(positions):
    half_dim = HEAD_SIZE // 2
    frequency = 500000.0 ** (-2.0 * jnp.arange(half_dim, dtype=jnp.float32) / HEAD_SIZE)
    angles = positions.astype(jnp.float32)[:, None] * frequency[None, :]
    cosine = jnp.cos(angles)
    sine = jnp.sin(angles)
    return jnp.concatenate([cosine, cosine], axis=1), jnp.concatenate([-sine, sine], axis=1)


def body(
    hidden,
    attn_gain,
    w_query,
    w_key,
    w_value,
    w_out,
    mlp_gain,
    w_gate_up,
    w_down,
    key_cache,
    value_cache,
    lengths,
):
    rows_dev = hidden.shape[1]
    count = lax.axis_size("mp")
    section_index = lax.axis_index("section")
    model_index = lax.axis_index("mp")
    width = hidden.shape[2]
    near = jnp.asarray(relative_ids())
    near_places, far_places = near ^ model_index, near ^ model_index ^ 1
    places = jnp.concatenate([near_places, far_places])
    wk = w_key[0].T
    wv = w_value[0].T
    blocks = w_gate_up.shape[3] // 128
    windows = 2 * len(chip_masks()) - 2
    bounds = [(4 * blocks * step + windows) // (2 * windows) for step in range(windows + 1)]
    batches = [
        jnp.remainder(section_index + turn_index, 2).astype(jnp.int32).reshape(1)
        for turn_index in range(2)
    ]

    tables = [
        turning(lax.dynamic_index_in_dim(lengths, batch[0], 0, keepdims=False))
        for batch in batches
    ]
    me = model_index.astype(jnp.int32).reshape(1)
    early = (places, near_places, far_places, me, *batches, *tables[0], *tables[1])

    def attention_jobs(turn_index):
        got = {}

        def projections(token):
            got["qkv"] = fetch((token,), w_query[0], wk, wv)
            return got["qkv"]

        def out_projection(token):
            got["out"] = fetch((token,), w_out[0])
            return got["out"]

        def caches(token):
            got["caches"] = fetch_caches((token,), batches[turn_index], key_cache[0], value_cache[0])
            return got["caches"]

        if turn_index == 0:
            return got, [lambda token: early, projections], [out_projection, caches]
        return got, [projections, caches, out_projection], []

    got, jobs, rest = attention_jobs(0)
    quarters = gather_doubling(hidden[0], jobs)
    for job in rest:
        job(quarters[0])
    for turn_index in range(2):
        last = turn_index == 1
        batch = batches[turn_index]
        held_back = (*got["out"], *got["caches"])
        joined, by_owner = project(places, all_quarters(quarters), attn_gain, *got["qkv"], held_back)
        if turn_index == 0:
            addend = by_owner
        spread = lax.all_to_all(joined, "mp", split_axis=0, concat_axis=0)
        mixed = attend(
            batch, lengths, spread, *tables[turn_index], *got["caches"], w_query.shape[2]
        )
        heads_out = lax.all_to_all(mixed.transpose(1, 0, 2), "mp", split_axis=0, concat_axis=0)
        got_core = swap(spread_project(far_places, heads_out, *got["out"]), 1)
        keep = spread_project(near_places, heads_out, *got["out"])
        pairs = {}

        def pair_job(new):
            def job(token):
                if not new:
                    return ()
                arrays = fetch_pairs(token, places, w_gate_up[0], new)
                pairs.update(zip(new, arrays))
                return arrays

            return job

        items = [(side, block) for side in range(2) for block in range(blocks)]
        jobs = [pair_job(items[low:high]) for low, high in zip(bounds, bounds[1:])]
        middle = reduce_to_pair(keep, got_core, addend, jobs, False)
        quarters = spread_pair(middle, jobs)
        sides = [
            [
                placed_in(pairs[side, block].reshape(width, 128), pltpu.VMEM)
                for block in range(blocks)
            ]
            for side in range(2)
        ]
        total = jnp.zeros((8, 128), jnp.float32)
        down = []
        for which, first in enumerate(quarter_starts(count)[:3]):
            if which == 2:
                far_parts = quarters[2]
                (far_parts,) = step_call(pass_kernel, [far_parts.shape], (far_parts,), (total,))
                quarters = all_quarters((*quarters[:2], far_parts))
            fetch_first = (0, count // 4, None)[which]
            total, got_down = quarter(
                first, fetch_first, places, quarters[which], mlp_gain, total, w_down[0],
                sides[which % 2],
            )
            down.append(got_down)
        send, act, own_rows = finish(
            last, me, places, quarters, mlp_gain, total, *down[:2], w_down[0], sides[1]
        )
        if last:
            mine = (own_rows + scatter(send, act)).astype(jnp.bfloat16)
        else:
            got, jobs, _ = attention_jobs(1)
            got_core = swap(send, 1)
            keep = keep_half(act, *down[:2])
            addend = reduce_to_pair(keep, got_core, middle, jobs, True)
            quarters = spread_pair(addend, jobs)
    return mine[None]


def solution(mesh):
    placed = (
        P("section", "mp", None),
        P("section", None),
        P("section", None, "mp"),
        P("section", None, "mp"),
        P("section", None, "mp"),
        P("section", "mp", None),
        P("section", None),
        P("section", None, None, "mp"),
        P("section", "mp", None),
        P("section", None, "mp", None, None),
        P("section", None, "mp", None, None),
        P(None, "mp"),
    )
    return jax.shard_map(
        body, mesh=mesh, in_specs=placed, out_specs=P("section", "mp", None), check_vma=False
    )
```

```python
import functools

import jax
import jax.numpy as jnp
import numpy as np
from jax import lax
from jax.experimental import pallas as pl
from jax.experimental.pallas import tpu as pltpu
from jax.sharding import PartitionSpec as P

QUERY_HEADS = 64
KEY_VALUE_HEADS = 8
HEAD_SIZE = 128

epsilon = 1e-05

UNROLL = 4


def swap(value, mask, axis="mp"):
    count = lax.axis_size(axis)
    return lax.ppermute(value, axis, [(source, source ^ mask) for source in range(count)])


def exchange(parts):
    count = lax.axis_size("mp")
    groups = [list(range(core, count, 2)) for core in range(2)]
    return lax.all_to_all(
        parts, "mp", split_axis=0, concat_axis=0, axis_index_groups=groups, tiled=True
    )


def chip_masks():
    return [1 << bit for bit in range(1, (lax.axis_size("mp") - 1).bit_length())]


def relative_ids():
    ids = np.zeros((1,), np.int32)
    for mask in reversed(chip_masks()):
        ids = np.concatenate([ids, ids ^ mask])
    return ids


def vmem():
    return pl.BlockSpec(memory_space=pltpu.VMEM)


def smem():
    return pl.BlockSpec(memory_space=pltpu.SMEM)


def placed_in(values, space):
    return pltpu.with_memory_space_constraint(values, space)


def hbm():
    return pl.BlockSpec(memory_space=pl.ANY)


def run_copies(copies):
    for at, copy in enumerate(copies):
        copy.start(priority=at % 2)
    for copy in copies:
        copy.wait()


def fetch_kernel(pieces, tokens, *refs):
    arrays = len(pieces)
    refs, sems = refs[tokens:-1], refs[-1]
    copies = []
    for array, (count, source, target) in enumerate(zip(pieces, refs, refs[arrays:])):
        size = source.shape[0] // count
        for piece in range(count):
            span = pl.ds(piece * size, size)
            copies.append(
                pltpu.make_async_copy(source.at[span], target.at[span], sems.at[array, piece])
            )
    run_copies(copies)


def fetch(tokens, *arrays):
    pieces = [8 if array.shape[0] % 128 == 0 else 1 for array in arrays]
    return pl.pallas_call(
        functools.partial(fetch_kernel, pieces, len(tokens)),
        out_shape=[pltpu.VMEM(array.shape, array.dtype) for array in arrays],
        in_specs=[hbm()] * (len(tokens) + len(arrays)),
        out_specs=[vmem()] * len(arrays),
        scratch_shapes=[pltpu.SemaphoreType.DMA((len(arrays), 8))],
        compiler_params=pltpu.CompilerParams(vmem_limit_bytes=1 << 20),
        cost_estimate=pl.CostEstimate(
            flops=0, bytes_accessed=sum(2 * array.size for array in arrays), transcendentals=0
        ),
    )(*tokens, *[placed_in(array, pltpu.HBM) for array in arrays])


def fetch_caches_kernel(where_ref, keys_ref, values_ref, *refs):
    key_ref, value_ref, sems = refs[-3:]
    rows, places, _ = key_ref.shape
    batch = where_ref[0]
    copies = []
    for array, (source, target) in enumerate(((keys_ref, key_ref), (values_ref, value_ref))):
        for row in range(rows):
            for piece in range(2):
                span = pl.ds(piece * (places // 2), places // 2)
                copies.append(
                    pltpu.make_async_copy(
                        source.at[batch, row, span],
                        target.at[row, span],
                        sems.at[array, row, piece],
                    )
                )
    run_copies(copies)


def fetch_caches(tokens, where, keys, values):
    shape = pltpu.VMEM(keys.shape[1:], keys.dtype)
    return pl.pallas_call(
        fetch_caches_kernel,
        out_shape=[shape, shape],
        in_specs=[smem(), hbm(), hbm()] + [hbm()] * len(tokens),
        out_specs=[vmem(), vmem()],
        scratch_shapes=[pltpu.SemaphoreType.DMA((2, keys.shape[1], 2))],
        compiler_params=pltpu.CompilerParams(vmem_limit_bytes=1 << 20),
        cost_estimate=pl.CostEstimate(
            flops=0, bytes_accessed=2 * keys.size, transcendentals=0
        ),
    )(where, placed_in(keys, pltpu.HBM), placed_in(values, pltpu.HBM), *tokens)


def fetch_pairs_kernel(items, ids_ref, token_ref, source, *refs):
    targets, sems = refs[:-1], refs[-1]
    half = sems.shape[1]
    chunk = targets[0].shape[0] // half
    copies = []
    for at, ((side, block), target) in enumerate(zip(items, targets)):
        for k in range(half):
            copies.append(
                pltpu.make_async_copy(
                    source.at[
                        span_of(ids_ref, side * half + k, chunk), :, pl.ds(block * 128, 128)
                    ],
                    target.at[pl.ds(k * chunk, chunk)],
                    sems.at[at, k],
                )
            )
    run_copies(copies)


def fetch_pairs(token, ids, weights, items):
    half = ids.shape[0] // 2
    size = weights.shape[0] // 2
    return pl.pallas_call(
        functools.partial(fetch_pairs_kernel, items),
        out_shape=[pltpu.VMEM((size, 2, 128), weights.dtype)] * len(items),
        in_specs=[smem(), hbm(), hbm()],
        out_specs=[vmem()] * len(items),
        scratch_shapes=[pltpu.SemaphoreType.DMA((len(items), half))],
        compiler_params=pltpu.CompilerParams(vmem_limit_bytes=1 << 20),
        cost_estimate=pl.CostEstimate(
            flops=0, bytes_accessed=4 * len(items) * size * 128, transcendentals=0
        ),
    )(ids, token, placed_in(weights, pltpu.HBM))


def in_vmem(arrays):
    return [placed_in(x, pltpu.VMEM) if x.size > 1 << 14 else x for x in arrays]


def step_call(kernel, shapes, operands, held_back):
    return pl.pallas_call(
        kernel,
        out_shape=[pltpu.VMEM(shape, jnp.bfloat16) for shape in shapes],
        in_specs=[vmem()] * len(operands) + [hbm()] * len(held_back),
        out_specs=[vmem()] * len(shapes),
        compiler_params=pltpu.CompilerParams(vmem_limit_bytes=4 << 20),
        cost_estimate=pl.CostEstimate(
            flops=2 * operands[-1].size, bytes_accessed=6 * operands[-1].size, transcendentals=0
        ),
    )(*operands, *in_vmem(held_back))


def add_kernel(outs, operands, *refs):
    targets = refs[-outs:]
    share = targets[0].shape[0]
    for which, target in enumerate(targets):
        for place in range(share):
            total = 0.0
            for ref in refs[:operands]:
                total += ref[which * share + place].astype(jnp.float32)
            target[place] = total.astype(jnp.bfloat16)


def add_parts(operands, outs, held_back=()):
    lead = operands[0].shape[0]
    shape = (lead // outs,) + operands[0].shape[1:]
    return step_call(
        functools.partial(add_kernel, outs, len(operands)), [shape] * outs, operands, held_back
    )


def cross_kernel(addend_ref, here_ref, there_ref, *refs):
    out_ref = refs[-1]
    for place in range(2):
        if len(addend_ref.shape) == 3:
            addend = addend_ref[addend_ref.shape[0] - 2 + place].astype(jnp.float32)
        else:
            owners = range(addend_ref.shape[1])
            parts = [addend_ref[place, owner].astype(jnp.float32) for owner in owners]
            addend = jnp.concatenate(parts, axis=0)
        out_ref[place] = (
            addend
            + here_ref[place].astype(jnp.float32)
            + there_ref[1 - place].astype(jnp.float32)
        ).astype(jnp.bfloat16)


def join_kernel(low_ref, high_ref, *refs):
    half = low_ref.shape[0]
    out_ref = refs[-1]
    for place in range(half):
        out_ref[place] = low_ref[place]
        out_ref[half + place] = high_ref[place]


def join(low, high, held_back=()):
    shape = (2 * low.shape[0],) + low.shape[1:]
    return step_call(join_kernel, [shape], (low, high), held_back)[0]


def run_job(jobs, token):
    return jobs.pop(0)(token) if jobs else ()


def scatter(send, keep):
    (held,) = add_parts((keep, swap(send, 1)), 1)
    return jnp.sum(exchange(held).astype(jnp.float32), axis=0)


def halve(keep, got, jobs):
    held_back = ()
    for mask in chip_masks()[:-1]:
        keep, send = add_parts((keep, got), 2, held_back)
        got = swap(send, mask)
        held_back = run_job(jobs, send)
    return keep, got, held_back


def hop(part, mask):
    count = lax.axis_size("mp")
    pairs = [(source, ((source + count) % (2 * count)) ^ mask) for source in range(2 * count)]
    return lax.ppermute(part, ("section", "mp"), pairs)


def reduce_to_pair(keep, got, addend, jobs, hops):
    keep, got, held_back = halve(keep, got, jobs)
    (held,) = add_parts((keep, got), 1, held_back)
    far = chip_masks()[-1]
    if hops:
        here = hop(join(held, addend), 0)
        return step_call(
            cross_kernel, [held.shape], (here, here, hop(held, far)), run_job(jobs, held)
        )[0]
    here, there = held, swap(held, far)
    return step_call(cross_kernel, [held.shape], (addend, here, there), run_job(jobs, held))[0]


def spread_pair(pair, jobs):
    held = pair
    for mask in reversed(chip_masks()[1:-1]):
        got = swap(held, mask)
        held = join(held, got, run_job(jobs, held))
    got = swap(held, chip_masks()[0])
    return held, swap(held, 1), got


def pass_kernel(in_ref, *refs):
    refs[-1][...] = in_ref[...]


def gather_doubling(part, jobs):
    held = part[None]
    got = swap(held, chip_masks()[-1])
    (near,) = step_call(pass_kernel, [held.shape], (held,), run_job(jobs, held))
    return spread_pair(join(near, got), jobs)


def quarter_starts(count):
    return 0, count // 2, count // 4, count // 2 + count // 4


def inverse_rms(x_refs):
    parts, rows, chunk = x_refs[0].shape
    total = jnp.zeros((rows, chunk), jnp.float32)
    for x_ref in x_refs:

        def add(group, total):
            for step in range(UNROLL):
                wide = x_ref[group * UNROLL + step].astype(jnp.float32)
                total = total + wide * wide
            return total

        total = lax.fori_loop(0, parts // UNROLL, add, total)
    mean = jnp.sum(total, axis=-1, keepdims=True) / (4 * parts * chunk)
    return lax.rsqrt(mean + epsilon)


def span_of(ids_ref, k, chunk):
    return pl.ds(pl.multiple_of(ids_ref[k] * chunk, chunk), chunk)


def project_into(read, spans, groups, gain_ref, wq_ref, wk_ref, wv_ref, q_sum, kv_sum):
    @pl.loop(0, groups)
    def _(group):
        q_part = 0.0
        kv_part = 0.0
        for step in range(UNROLL):
            k = group * UNROLL + step
            span = spans(k)
            scaled = (read(k) * gain_ref[:, span]).astype(jnp.bfloat16)
            q_part += jnp.dot(scaled, wq_ref[span, :], preferred_element_type=jnp.float32)
            kv_part += lax.dot_general(
                scaled,
                jnp.concatenate([wk_ref[:, span], wv_ref[:, span]], axis=0),
                (((1,), (1,)), ((), ())),
                preferred_element_type=jnp.float32,
            )
        q_sum[...] += q_part
        kv_sum[...] += kv_part


def project_quarters(ids_ref, starts, x_refs, *rest):
    parts, _, chunk = x_refs[0].shape
    for first, x_ref in zip(starts, x_refs):
        project_into(
            lambda k: x_ref[k].astype(jnp.float32),
            lambda k: span_of(ids_ref, first + k, chunk),
            parts // UNROLL,
            *rest,
        )


def project_near_kernel(ids_ref, near_ref, other_ref, gain_ref, wq_ref, wk_ref, wv_ref, q_sum,
                        kv_sum):
    q_sum[...] = jnp.zeros_like(q_sum)
    kv_sum[...] = jnp.zeros_like(kv_sum)
    starts = quarter_starts(4 * near_ref.shape[0])[:2]
    project_quarters(
        ids_ref, starts, (near_ref, other_ref), gain_ref, wq_ref, wk_ref, wv_ref, q_sum, kv_sum
    )


def project_cost(rows, width, size):
    return pl.CostEstimate(
        flops=2 * rows * width * size, bytes_accessed=2 * width * size, transcendentals=0
    )


def project_near(ids, near, other, gain, wq, wk, wv):
    rows = near.shape[1]
    width, queries = wq.shape
    keys = wk.shape[0]
    return pl.pallas_call(
        project_near_kernel,
        out_shape=[
            pltpu.VMEM((rows, queries), jnp.float32),
            pltpu.VMEM((rows, 2 * keys), jnp.float32),
        ],
        in_specs=[smem()] + [vmem()] * 6,
        out_specs=[vmem(), vmem()],
        compiler_params=pltpu.CompilerParams(vmem_limit_bytes=3 << 20),
        cost_estimate=project_cost(rows, width // 2, queries + 2 * keys),
    )(ids, near, other, gain, *in_vmem((wq, wk, wv)))


def project_kernel(ids_ref, *refs):
    x_refs, (gain_ref, wq_ref, wk_ref, wv_ref, q_before, kv_before) = refs[:4], refs[4:10]
    out_ref, mine_ref, q_sum, kv_sum, wide = refs[-5:]
    weights = (wq_ref, wk_ref, wv_ref)
    queries = wq_ref.shape[1]
    count, rows_dev, _ = out_ref.shape
    quarter = count // 4
    by_rows = x_refs[0].shape[1] == rows_dev
    chunk = wq_ref.shape[0] // count
    starts = quarter_starts(count)
    if by_rows:
        q_sum[...] = jnp.zeros_like(q_sum)
        kv_sum[...] = jnp.zeros_like(kv_sum)
        for first, x_ref in zip(starts, x_refs):
            for place in range(quarter):
                at = (first + place) * rows_dev
                wide[at : at + rows_dev, :] = x_ref[place].astype(jnp.float32)
        total = 0.0
        for k in range(count):
            part = wide[:, k * chunk : (k + 1) * chunk]
            total += part * part
        mean = jnp.sum(total, axis=-1, keepdims=True) / (count * chunk)
        scale = lax.rsqrt(mean + epsilon)

        def straight(k):
            return pl.ds(pl.multiple_of(k * chunk, chunk), chunk)

        project_into(
            lambda k: wide[:, straight(k)],
            straight,
            count // UNROLL,
            gain_ref,
            *weights,
            q_sum,
            kv_sum,
        )
    else:
        q_sum[...] = q_before[...]
        kv_sum[...] = kv_before[...]
        scale = inverse_rms(x_refs)
        project_quarters(ids_ref, starts[2:], x_refs[2:], gain_ref, *weights, q_sum, kv_sum)

    q_sum[...] *= scale
    kv_sum[...] *= scale
    for place in range(count):
        owner = ids_ref[place] if by_rows else place
        lines = slice(place * rows_dev, (place + 1) * rows_dev)
        out_ref[owner, :, :queries] = q_sum[lines, :].astype(jnp.bfloat16)
        out_ref[owner, :, queries:] = kv_sum[lines, :].astype(jnp.bfloat16)
        if by_rows:
            for which in range(2):
                span = span_of(ids_ref, which, chunk)
                mine_ref[which, owner] = wide[lines, span].astype(jnp.bfloat16)


def project(ids, quarters, gain, wq, wk, wv, before, held_back):
    count = ids.shape[0]
    width, queries = wq.shape
    keys = wk.shape[0]
    size = queries + 2 * keys
    rows_dev = 4 * quarters[0].size // (count * width)
    rows = count * rows_dev
    by_rows = quarters[0].shape[1] == rows_dev
    return pl.pallas_call(
        project_kernel,
        out_shape=[
            pltpu.VMEM((count, rows_dev, size), jnp.bfloat16),
            pltpu.VMEM((2, count, rows_dev, width // count), jnp.bfloat16),
        ],
        in_specs=[smem()] + [vmem()] * 10 + [hbm()] * len(held_back),
        out_specs=[vmem(), vmem()],
        scratch_shapes=[
            pltpu.VMEM((rows, queries), jnp.float32),
            pltpu.VMEM((rows, 2 * keys), jnp.float32),
            pltpu.VMEM((rows, width if by_rows else 128), jnp.float32),
        ],
        compiler_params=pltpu.CompilerParams(vmem_limit_bytes=(3 << 20) + 4 * rows * width),
        cost_estimate=project_cost(rows, width, size),
    )(ids, *quarters, gain, *in_vmem((wq, wk, wv)), *before, *in_vmem(held_back))


def attend_kernel(where_ref, length_ref, in_ref, cos_ref, sin_ref, key_buf, value_buf, out_ref,
                  lined, wide_q):
    rows, devices, queries = out_ref.shape
    width = key_buf.shape[2]
    keys = (in_ref.shape[2] - queries) // 2
    size = cos_ref.shape[1]
    groups = width // size
    pieces = size // keys
    slots = queries // size
    heads = devices * slots
    places = key_buf.shape[1]
    batch = where_ref[0]

    for device in range(devices):
        wide = in_ref[device].astype(jnp.float32)
        for row in range(rows):
            lined[row, device : device + 1, :] = wide[row : row + 1]
    line = lax.broadcasted_iota(jnp.int32, (devices, 1), 0)
    group_of = line * groups // devices
    for row in range(rows):
        cosine = cos_ref[pl.ds(row, 1), :]
        sine = sin_ref[pl.ds(row, 1), :]

        def turned(wide):
            other = jnp.concatenate([wide[:, size // 2 :], wide[:, : size // 2]], axis=1)
            return (wide * cosine + other * sine).astype(jnp.bfloat16).astype(jnp.float32)

        key_lines = jnp.zeros((devices, size), jnp.float32)
        value_lines = jnp.zeros((devices, size), jnp.float32)
        for group in range(groups):
            own_key, own_value = (
                jnp.concatenate(
                    [
                        lined[row, device : device + 1, at : at + keys]
                        for device in range(group * pieces, (group + 1) * pieces)
                    ],
                    axis=1,
                )
                for at in (queries, queries + keys)
            )
            here = group_of == group
            key_lines = jnp.where(here, turned(own_key), key_lines)
            value_lines = jnp.where(here, own_value, value_lines)
        own_parts = []
        for slot in range(slots):
            part = turned(lined[row, :, slot * size : (slot + 1) * size])
            own_parts.append(jnp.sum(part * key_lines, axis=1, keepdims=True))
            for group in range(groups):
                wide_q[
                    slot * devices : (slot + 1) * devices, group * size : (group + 1) * size
                ] = jnp.where(group_of == group, part, 0.0).astype(jnp.bfloat16)
        own_score = jnp.concatenate(own_parts, axis=0) * (size ** -0.5)
        scores = lax.dot_general(
            wide_q[...], key_buf[row], (((1,), (1,)), ((), ())), preferred_element_type=jnp.float32
        ) * (size ** -0.5)
        spot = lax.broadcasted_iota(jnp.int32, (heads, places), 1)
        scores = jnp.where(spot < length_ref[batch, row], scores, -1e30)
        highest = jnp.maximum(jnp.max(scores, axis=1, keepdims=True), own_score)
        raised = jnp.exp(scores - highest)
        own_raised = jnp.exp(own_score - highest)
        denominator = jnp.sum(raised, axis=1, keepdims=True) + own_raised
        weights = (raised / denominator).astype(jnp.bfloat16)
        own_weight = (own_raised / denominator).astype(jnp.bfloat16).astype(jnp.float32)
        mixed = jnp.dot(weights, value_buf[row], preferred_element_type=jnp.float32)
        for slot in range(slots):
            lines = slice(slot * devices, (slot + 1) * devices)
            picked = own_weight[lines] * value_lines
            for group in range(groups):
                picked = picked + jnp.where(
                    group_of == group, mixed[lines, group * size : (group + 1) * size], 0.0
                )
            out_ref[row, :, slot * size : (slot + 1) * size] = picked.astype(jnp.bfloat16)


def attend(where, lengths, spread, cosine, sine, keys, values, queries):
    devices, rows, length = spread.shape
    places, width = keys.shape[1:]
    heads = devices * queries // HEAD_SIZE
    return pl.pallas_call(
        attend_kernel,
        out_shape=pltpu.VMEM((rows, devices, queries), jnp.bfloat16),
        in_specs=[smem(), smem()] + [vmem()] * 5,
        out_specs=vmem(),
        scratch_shapes=[
            pltpu.VMEM((rows, devices, length), jnp.float32),
            pltpu.VMEM((heads, width), jnp.bfloat16),
        ],
        compiler_params=pltpu.CompilerParams(vmem_limit_bytes=4 << 20),
        cost_estimate=pl.CostEstimate(
            flops=4 * rows * heads * places * width,
            bytes_accessed=4 * rows * places * width,
            transcendentals=rows * heads * places,
        ),
    )(
        where,
        lengths,
        spread,
        cosine,
        sine,
        placed_in(keys, pltpu.VMEM),
        placed_in(values, pltpu.VMEM),
    )


def spread_kernel(ids_ref, x_ref, w_ref, out_ref, values):
    parts, rows, chunk = out_ref.shape
    count, rows_dev, _ = x_ref.shape
    for owner in range(count):
        values[owner * rows_dev : (owner + 1) * rows_dev, :] = x_ref[owner].astype(jnp.float32)
    ready = values[...].astype(jnp.bfloat16)

    @pl.loop(0, parts // UNROLL)
    def _(group):
        for step in range(UNROLL):
            k = group * UNROLL + step
            span = span_of(ids_ref, k, chunk)
            out_ref[k] = jnp.dot(
                ready, w_ref[:, span], preferred_element_type=jnp.float32
            ).astype(jnp.bfloat16)


def spread_project(ids, values, weights):
    count, rows_dev, depth = values.shape
    rows = count * rows_dev
    chunk = weights.shape[1] // count
    parts = ids.shape[0]
    return pl.pallas_call(
        spread_kernel,
        out_shape=pltpu.VMEM((parts, rows, chunk), jnp.bfloat16),
        in_specs=[smem(), vmem(), vmem()],
        out_specs=vmem(),
        scratch_shapes=[pltpu.VMEM((rows, depth), jnp.float32)],
        compiler_params=pltpu.CompilerParams(vmem_limit_bytes=4 << 20),
        cost_estimate=pl.CostEstimate(
            flops=2 * rows * depth * parts * chunk,
            bytes_accessed=2 * depth * parts * chunk,
            transcendentals=0,
        ),
    )(ids, values, placed_in(weights, pltpu.VMEM))


def gate_up(ids_ref, first, x_ref, gain_ref, blocks, stacked, wide_x, total_ref):
    parts, rows, chunk = x_ref.shape
    per_chunk = chunk // 128
    base = first % (2 * parts)

    @pl.loop(0, parts // UNROLL)
    def _(group):
        for step in range(UNROLL):
            place = group * UNROLL + step
            span = span_of(ids_ref, first + place, chunk)
            scaled = (x_ref[place].astype(jnp.float32) * gain_ref[:, span]).astype(jnp.bfloat16)
            for b in range(per_chunk):
                stacked[place * per_chunk + b] = scaled[:, b * 128 : (b + 1) * 128]

    line = lax.broadcasted_iota(jnp.int32, (128, 512), 0)
    column = lax.broadcasted_iota(jnp.int32, (128, 512), 1)
    aim = jnp.where(column < 256, 2 * line, 2 * line + 257)
    widen = jnp.where(column == aim, 1.0, 0.0).astype(jnp.bfloat16)
    groups = parts * per_chunk // 8
    for group in range(groups):
        wide = jnp.dot(
            stacked[group * 8 : (group + 1) * 8].reshape(8 * rows, 128),
            widen,
            preferred_element_type=jnp.float32,
        ).astype(jnp.bfloat16)
        for b in range(8):
            lines = slice(b * rows, (b + 1) * rows)
            wide_x[group, :rows, b * 256 : (b + 1) * 256] = wide[lines, :256]
            wide_x[group, rows:, b * 256 : (b + 1) * 256] = wide[lines, 256:]

    per_group = 8 // per_chunk

    @pl.loop(0, groups)
    def _(group):
        for j in range(0, len(blocks), 2):
            part = 0.0
            for step in range(per_group):
                at = (base + group * per_group + step) * (2 * chunk)
                span = pl.ds(pl.multiple_of(at, 2 * chunk), 2 * chunk)
                pair = jnp.concatenate([blocks[j][span, :], blocks[j + 1][span, :]], axis=1)
                part += jnp.dot(
                    wide_x[group, :, step * 2 * chunk : (step + 1) * 2 * chunk],
                    pair,
                    preferred_element_type=jnp.float32,
                )
            total_ref[:, j * 128 : (j + 2) * 128] += part


def down_copies(ids_ref, first, source, target, sems):
    count, _, chunk = target.shape

    def copy(k):
        return pltpu.make_async_copy(
            source.at[:, span_of(ids_ref, first + k, chunk)], target.at[k], sems.at[k]
        )

    return [copy(k) for k in range(count)]


def quarter_kernel(first, fetch_first, ids_ref, x_ref, gain_ref, before_ref, down_hbm, *refs):
    blocks, (total_ref, down_ref, stacked, wide_x, sems) = refs[:-5], refs[-5:]
    copies = []
    if fetch_first is not None:
        copies = down_copies(ids_ref, fetch_first, down_hbm, down_ref, sems)
    for copy in copies:
        copy.start()
    if first:
        total_ref[...] = before_ref[...]
    else:
        total_ref[...] = jnp.zeros_like(total_ref)
    gate_up(ids_ref, first, x_ref, gain_ref, blocks, stacked, wide_x, total_ref)
    for copy in copies:
        copy.wait()


def quarter(first, fetch_first, ids, x, gain, before, down, pairs):
    parts, rows, chunk = x.shape
    units, width = down.shape
    got = (parts, units, chunk) if fetch_first is not None else (1, 8, 128)
    return pl.pallas_call(
        functools.partial(quarter_kernel, first, fetch_first),
        out_shape=[
            pltpu.VMEM((2 * rows, units), jnp.float32),
            pltpu.VMEM(got, jnp.bfloat16),
        ],
        in_specs=[smem()] + [vmem()] * 3 + [hbm()] + [vmem()] * len(pairs),
        out_specs=[vmem(), vmem()],
        scratch_shapes=[
            pltpu.VMEM((width // 512, rows, 128), jnp.bfloat16),
            pltpu.VMEM((width // 4096, 2 * rows, 2048), jnp.bfloat16),
            pltpu.SemaphoreType.DMA((parts,)),
        ],
        compiler_params=pltpu.CompilerParams(vmem_limit_bytes=(2 << 20) + 5 * rows * width // 2),
        cost_estimate=pl.CostEstimate(
            flops=rows * units * width, bytes_accessed=units * width, transcendentals=0
        ),
    )(ids, x, gain, before, placed_in(down, pltpu.HBM), *pairs)


def finish_kernel(last, me_ref, ids_ref, *refs):
    x_refs, (gain_ref, before_ref, low_ref, high_ref, down_hbm) = refs[:4], refs[4:9]
    blocks, outs, (stacked, wide_x, total, act, far_ref, sems) = refs[9:-9], refs[-9:-6], refs[-6:]
    parts, rows, chunk = x_refs[0].shape
    half = 2 * parts
    copies = down_copies(ids_ref, half, down_hbm, far_ref, sems)
    for copy in copies:
        copy.start()
    total[...] = before_ref[...]
    starts = quarter_starts(2 * half)
    gate_up(ids_ref, starts[3], x_refs[3], gain_ref, blocks, stacked, wide_x, total)
    scale = inverse_rms(x_refs)
    gate = total[:rows, :] * scale
    act[...] = (gate / (1.0 + jnp.exp(-gate)) * (total[rows:, :] * scale)).astype(jnp.bfloat16)

    def down(weights):
        return jnp.dot(act[...], weights, preferred_element_type=jnp.float32)

    for copy in copies:
        copy.wait()
    if not last:
        send_ref, act_ref, _ = outs
        act_ref[...] = act[...]

        @pl.loop(0, half // UNROLL)
        def _(group):
            for step in range(UNROLL):
                k = group * UNROLL + step
                send_ref[k] = down(far_ref[k]).astype(jnp.bfloat16)

        return

    send_ref, keep_ref, middle_ref = outs
    rows_dev = middle_ref.shape[0]
    line = lax.broadcasted_iota(jnp.int32, (rows, 1), 0)
    first_core = lax.rem(me_ref[0], 2) == 0
    for which, (first, x_ref) in enumerate(zip(starts, x_refs)):

        @pl.loop(0, parts // UNROLL)
        def _(group):
            for step in range(UNROLL):
                k = group * UNROLL + step
                span = span_of(ids_ref, first + k, chunk)
                wide = x_ref[k].astype(jnp.float32)
                for row in range(rows_dev):
                    here = line == me_ref[0] * rows_dev + row
                    middle_ref[row : row + 1, span] = jnp.sum(
                        jnp.where(here, wide, 0.0), axis=0, keepdims=True
                    )
                if which % 2:
                    part = down(far_ref[first - half + k])
                else:
                    part = down((high_ref if which else low_ref)[k])
                for chip in range(half):
                    at = 2 * chip * rows_dev
                    low = part[at : at + rows_dev]
                    high = part[at + rows_dev : at + 2 * rows_dev]
                    keep_ref[chip, :, span] = jnp.where(first_core, low, high).astype(jnp.bfloat16)
                    send_ref[chip, :, span] = jnp.where(first_core, high, low).astype(jnp.bfloat16)


def finish(last, me, ids, quarters, gain, before, low, high, down, pairs):
    parts, rows, chunk = quarters[0].shape
    half = 2 * parts
    units, width = down.shape
    rows_dev = rows // (2 * half)
    if last:
        shapes = [((half, rows_dev, width), jnp.bfloat16)] * 2 + [((rows_dev, width), jnp.float32)]
    else:
        shapes = [
            ((half, rows, chunk), jnp.bfloat16),
            ((rows, units), jnp.bfloat16),
            ((8, 128), jnp.float32),
        ]
    return pl.pallas_call(
        functools.partial(finish_kernel, last),
        out_shape=[pltpu.VMEM(shape, kind) for shape, kind in shapes],
        in_specs=[smem(), smem()] + [vmem()] * 8 + [hbm()] + [vmem()] * len(pairs),
        out_specs=[vmem()] * 3,
        scratch_shapes=[
            pltpu.VMEM((width // 512, rows, 128), jnp.bfloat16),
            pltpu.VMEM((width // 4096, 2 * rows, 2048), jnp.bfloat16),
            pltpu.VMEM((2 * rows, units), jnp.float32),
            pltpu.VMEM((rows, units), jnp.bfloat16),
            pltpu.VMEM((half, units, chunk), jnp.bfloat16),
            pltpu.SemaphoreType.DMA((half,)),
        ],
        compiler_params=pltpu.CompilerParams(
            vmem_limit_bytes=(2 << 20) + 5 * rows * width // 2 + (10 * rows + width) * units
        ),
        cost_estimate=pl.CostEstimate(
            flops=3 * rows * units * width, bytes_accessed=2 * units * width, transcendentals=0
        ),
    )(
        me,
        ids,
        *quarters,
        gain,
        before,
        *in_vmem((low, high)),
        placed_in(down, pltpu.HBM),
        *pairs,
    )


def keep_kernel(act_ref, low_ref, high_ref, out_ref):
    parts = low_ref.shape[0]
    for first, near_ref in ((0, low_ref), (parts, high_ref)):

        @pl.loop(0, parts // UNROLL)
        def _(group):
            for step in range(UNROLL):
                k = group * UNROLL + step
                out_ref[first + k] = jnp.dot(
                    act_ref[...], near_ref[k], preferred_element_type=jnp.float32
                ).astype(jnp.bfloat16)


def keep_half(act, low, high):
    rows = act.shape[0]
    parts, _, chunk = low.shape
    return pl.pallas_call(
        keep_kernel,
        out_shape=pltpu.VMEM((2 * parts, rows, chunk), jnp.bfloat16),
        in_specs=[vmem(), vmem(), vmem()],
        out_specs=vmem(),
        compiler_params=pltpu.CompilerParams(vmem_limit_bytes=4 << 20),
        cost_estimate=pl.CostEstimate(
            flops=4 * rows * low.size, bytes_accessed=4 * low.size, transcendentals=0
        ),
    )(act, *in_vmem((low, high)))


def turning(positions):
    half_dim = HEAD_SIZE // 2
    frequency = 500000.0 ** (-2.0 * jnp.arange(half_dim, dtype=jnp.float32) / HEAD_SIZE)
    angles = positions.astype(jnp.float32)[:, None] * frequency[None, :]
    cosine = jnp.cos(angles)
    sine = jnp.sin(angles)
    return jnp.concatenate([cosine, cosine], axis=1), jnp.concatenate([-sine, sine], axis=1)


def body(
    hidden,
    attn_gain,
    w_query,
    w_key,
    w_value,
    w_out,
    mlp_gain,
    w_gate_up,
    w_down,
    key_cache,
    value_cache,
    lengths,
):
    rows_dev = hidden.shape[1]
    count = lax.axis_size("mp")
    section_index = lax.axis_index("section")
    model_index = lax.axis_index("mp")
    width = hidden.shape[2]
    near = jnp.asarray(relative_ids())
    near_places, far_places = near ^ model_index, near ^ model_index ^ 1
    places = jnp.concatenate([near_places, far_places])
    wk = w_key[0].T
    wv = w_value[0].T
    blocks = w_gate_up.shape[3] // 128
    levels = len(chip_masks())
    loads = np.array([5] + [3] * (levels - 2) + [5] + [3] * (levels - 2))
    bounds = [0, *np.rint(2 * blocks * np.cumsum(loads) / np.sum(loads)).astype(int).tolist()]
    batches = [
        jnp.remainder(section_index + turn_index, 2).astype(jnp.int32).reshape(1)
        for turn_index in range(2)
    ]

    tables = [
        turning(lax.dynamic_index_in_dim(lengths, batch[0], 0, keepdims=False))
        for batch in batches
    ]
    me = model_index.astype(jnp.int32).reshape(1)
    early = (places, near_places, far_places, me, *batches, *tables[0], *tables[1])

    def attention_jobs(turn_index):
        got = {}

        def projections(token):
            got["qkv"] = fetch((token,), w_query[0], wk, wv)
            return got["qkv"]

        def out_projection(token):
            got["out"] = fetch((token,), w_out[0])
            return got["out"]

        def caches(token):
            got["caches"] = fetch_caches((token,), batches[turn_index], key_cache[0], value_cache[0])
            return got["caches"]

        if turn_index == 0:
            return got, [lambda token: early, projections], [out_projection, caches]
        return got, [projections, caches, out_projection], []

    def passed(quarters, held_back):
        far_parts = quarters[2]
        (far_parts,) = step_call(pass_kernel, [far_parts.shape], (far_parts,), held_back)
        return *quarters[:2], far_parts, swap(far_parts, 1)

    got, jobs, rest = attention_jobs(0)
    quarters = gather_doubling(hidden[0], jobs)
    waited = [array for job in rest for array in job(quarters[0])]
    before = [jnp.zeros((8, 128), jnp.float32)] * 2
    for turn_index in range(2):
        last = turn_index == 1
        batch = batches[turn_index]
        held_back = (*got["out"], *got["caches"])
        if last:
            before = waited = project_near(places, *quarters[:2], attn_gain, *got["qkv"])
        quarters = passed(quarters, waited)
        joined, by_owner = project(
            places, quarters, attn_gain, *got["qkv"], before, held_back
        )
        if turn_index == 0:
            addend = by_owner
        spread = lax.all_to_all(joined, "mp", split_axis=0, concat_axis=0)
        mixed = attend(
            batch, lengths, spread, *tables[turn_index], *got["caches"], w_query.shape[2]
        )
        heads_out = lax.all_to_all(mixed.transpose(1, 0, 2), "mp", split_axis=0, concat_axis=0)
        got_core = swap(spread_project(far_places, heads_out, *got["out"]), 1)
        keep = spread_project(near_places, heads_out, *got["out"])
        pairs = {}

        def pair_job(new):
            def job(token):
                if not new:
                    return ()
                arrays = fetch_pairs(token, places, w_gate_up[0], new)
                pairs.update(zip(new, arrays))
                return arrays

            return job

        items = [(side, block) for side in range(2) for block in range(blocks)]
        jobs = [pair_job(items[low:high]) for low, high in zip(bounds, bounds[1:])]
        middle = reduce_to_pair(keep, got_core, addend, jobs, False)
        quarters = spread_pair(middle, jobs)
        sides = [
            [
                placed_in(pairs[side, block].reshape(width, 128), pltpu.VMEM)
                for block in range(blocks)
            ]
            for side in range(2)
        ]
        total = jnp.zeros((8, 128), jnp.float32)
        down = []
        for which, first in enumerate(quarter_starts(count)[:3]):
            if which == 2:
                quarters = passed(quarters, (total,))
            fetch_first = (0, count // 4, None)[which]
            total, got_down = quarter(
                first, fetch_first, places, quarters[which], mlp_gain, total, w_down[0],
                sides[which % 2],
            )
            down.append(got_down)
        send, act, own_rows = finish(
            last, me, places, quarters, mlp_gain, total, *down[:2], w_down[0], sides[1]
        )
        if last:
            mine = (own_rows + scatter(send, act)).astype(jnp.bfloat16)
        else:
            got, jobs, _ = attention_jobs(1)
            got_core = swap(send, 1)
            keep = keep_half(act, *down[:2])
            addend = reduce_to_pair(keep, got_core, middle, jobs, True)
            quarters = spread_pair(addend, jobs)
    return mine[None]


def solution(mesh):
    placed = (
        P("section", "mp", None),
        P("section", None),
        P("section", None, "mp"),
        P("section", None, "mp"),
        P("section", None, "mp"),
        P("section", "mp", None),
        P("section", None),
        P("section", None, None, "mp"),
        P("section", "mp", None),
        P("section", None, "mp", None, None),
        P("section", None, "mp", None, None),
        P(None, "mp"),
    )
    return jax.shard_map(
        body, mesh=mesh, in_specs=placed, out_specs=P("section", "mp", None), check_vma=False
    )
```
